512 devices in a mesh: dp: 32 (over x, y), mp: 16 (over z, core).
Axes of the slice: x: 4, y: 8, z: 8, core: 2. Of those that a mesh axis runs over, the one named last changes fastest.
Arguments:
- tokens: bfloat16 [8192, 2432], P('dp', 'mp'), may hold values from -6 to 6
- route: int32 [8192, 1], P('dp'), may hold values from 0 to 31; in each aligned block of 256 rows (0 to 255, 256 to 511, ...) at most 16 rows name the same one
- tsteps: int32 [32], replicated, may hold values from 0 to 27
- mod_table: bfloat16 [28, 3, 2432], replicated, may hold values from -10 to 10
- w_qkv: bfloat16 [2432, 3, 2048], P(None, None, 'mp'), may hold values from -0.125 to 0.125
- qk_gain: float32 [2, 64], replicated, may hold values from 0.1 to 1.9
- context: bfloat16 [32, 2, 333, 2048], P('dp', None, None, 'mp'), may hold values from -43 to 43
- w_out: bfloat16 [2048, 2432], P('mp'), may hold values from -0.125 to 0.125
Outputs:
- mixed: bfloat16 [8192, 2432], P('dp', 'mp')
The draws below stay inside these ranges and needn't reach their ends.
Inputs may be any that keep to these rules, and one draw needn't show every extreme that they name: `route`: one index of dp holds at most 16 rows of one request; some request reaches 16; every request has rows.
All inputs are finite; a program needn't handle non-finite values.
Results may differ from the reference program's by a relative error of at most 0.024.
Values may be sent and summed in bfloat16 or wider, within the bound.
No kernel may reach another device: no remote copies, remote signals or barrier semaphores. Data moves between devices by JAX's collectives and lax.ppermute only.
A program may use at most 64 MiB of HBM per device.

```python
import math
import jax
import jax.numpy as jnp
import numpy as np
from jax import lax

D = 2432
HEADS = 32
HD = 64
TXT = 333
TSTEPS = 28
ROW_DEV = 256
REQ_DEV = 1
CAP = 16
REQS = 32
TOKENS = 8192
INNER = 2048
N_DP = 32
N_MP = 16


def draw_context(key, part):
    key = jax.random.fold_in(key, 7)
    first = jax.random.fold_in(key, 0)
    values = jnp.clip(jax.random.normal(first, (REQS, 2, TXT, INNER), jnp.float32), -6.0, 6.0)
    return values.astype(jnp.bfloat16)


def touch_ends(values, stream_key, smallest, top_value):
    spot = [jax.random.randint(jax.random.fold_in(stream_key, axis), (), 0, length) for axis, length in enumerate(values.shape)]
    main_axis = values.shape.index(max(values.shape))
    beside = spot[:main_axis] + [(spot[main_axis] + 1) % values.shape[main_axis]] + spot[main_axis + 1:]
    return values.at[tuple(spot)].set(smallest).at[tuple(beside)].set(top_value)


def levels(stream_key, extent, pieces, least, top_value):
    loudness = 1.0
    for dim, parts in pieces:
        heights = jax.random.uniform(jax.random.fold_in(jax.random.fold_in(stream_key, 6), dim), (parts,), jnp.float32, least / len(pieces), top_value / len(pieces))
        loudness = loudness * jnp.repeat(jnp.exp(heights), extent[dim] // parts).reshape((-1,) + (1,) * (len(extent) - 1 - dim))
    return loudness


def deal_out(own_key, own, number, rows, count, top, reach, slope):
    order = jax.random.permutation(own_key, count)
    crowded, ordinary = load_shares(count, rows * top, reach, slope, True), load_shares(count, rows * top, reach, slope, False)
    places = jnp.arange(count)

    def named(lengths, rotation):
        used = int((lengths > 0).sum())
        fixed = max(1, used // 4)
        passed = fixed + (places - fixed + rotation * (used - fixed)) % max(1, count - fixed)
        return jnp.zeros((count,), jnp.int32).at[order[jnp.where(places < fixed, places, passed)]].set(jnp.asarray(lengths, jnp.int32))

    lengths = jnp.where(number % 4 == 0, named(crowded, number // 4), named(ordinary, number - number // 4 - 1))
    mixed = jax.random.permutation(jax.random.fold_in(own, 3), count)
    giver, taker = mixed[0:count // 2 * 2:2], mixed[1:count // 2 * 2:2]
    margin = jnp.minimum(lengths[giver] - 1, reach - lengths[taker]) // 2
    margin = jnp.where((giver == order[0]) | (taker == order[0]) | (lengths[taker] == 0), 0, jnp.maximum(margin, 0))
    passed = jax.random.randint(jax.random.fold_in(own, 4), (count // 2,), 0, 1 << 20) % (margin + 1)
    lengths = lengths.at[giver].add(-passed).at[taker].add(passed)
    labels = jnp.searchsorted(jnp.cumsum(lengths), jnp.arange(rows * top), side="right").astype(jnp.int32)
    grid = labels.reshape(top, rows).T
    grid = grid[jax.random.permutation(jax.random.fold_in(own, 1), rows)]
    rotation = jax.random.randint(jax.random.fold_in(own, 2), (rows, 1), 0, top)
    return jnp.take_along_axis(grid, (jnp.arange(top)[None, :] + rotation) % top, axis=1)


def load_shares(amount, total, most, lean, full):
    loads = [(1 << 20) // math.isqrt(rank ** lean) + 1 for rank in range(1, amount + 1)]
    largest = most if full else min(most, max(-(-total // amount), total * loads[0] // sum(loads)))
    least = 1 if total - largest >= amount - 1 else 0
    holding, surplus = [largest] + [least] * (amount - 1), total - largest - least * (amount - 1)
    while surplus > 0:
        candidates = [i for i in range(1, amount) if holding[i] < largest] or [i for i in range(1, amount) if holding[i] < most]
        whole, left = sum([loads[i] for i in candidates]), surplus
        for i in candidates:
            more = min(most - holding[i], max(1, left * loads[i] // whole), surplus)
            holding[i] = holding[i] + more
            surplus = surplus - more
    return np.array(holding)


def gaussian(key, shape, deviation, reach, shards=(), held_as=jnp.bfloat16):
    entries = jax.random.normal(key, shape, jnp.float32) * deviation
    if len(shards) > 0:
        entries = levels(key, shape, shards, -0.22, 0.18) * entries
    return jnp.clip(entries, min=-reach, max=reach).astype(held_as)


def setup_inputs(seed: int = 0) -> dict:
    splits = jax.random.split(jax.random.key(seed), 9)
    tokens = gaussian(splits[0], (TOKENS, D), 1.0, 6.0, ((0, 32), (1, 16)))
    route_keys = jax.random.split(jax.random.fold_in(splits[1], 1), TOKENS // ROW_DEV)
    route_turns = jax.random.permutation(jax.random.fold_in(splits[1], 3), TOKENS // ROW_DEV)
    route = jax.vmap(lambda own, number: deal_out(jax.random.fold_in(splits[1], 2), own, number, ROW_DEV, N_DP * REQ_DEV, 1, CAP, 2))(route_keys, route_turns).reshape((TOKENS, 1))
    tsteps = touch_ends(jax.random.randint(splits[2], (REQS,), 0, TSTEPS), jax.random.fold_in(splits[2], 1), 0, TSTEPS - 1).astype(jnp.int32)
    mod_table = gaussian(splits[3], (TSTEPS, 3, D), 2.0, 10.0)
    w_qkv = gaussian(splits[4], (D, 3, INNER), D ** -0.5, 0.125, ((2, 16),))
    qk_gain = jnp.clip(1.0 + 0.18 * jax.random.normal(splits[5], (2, HD), jnp.float32), 0.1, 1.9)
    context = draw_context(jax.random.fold_in(splits[8], 71), 0)
    w_out = gaussian(splits[7], (INNER, D), INNER ** -0.5, 0.125, ((0, 16),))
    return {"tokens": tokens, "route": route, "tsteps": tsteps, "mod_table": mod_table, "w_qkv": w_qkv, "qk_gain": qk_gain, "context": context, "w_out": w_out}


EPS = 1e-06

def modulate(values, shift_rows, scale_rows):
    widened = values.astype(jnp.float32)
    center = lax.optimization_barrier(jnp.mean(widened, axis=-1, keepdims=True))
    spread = lax.optimization_barrier(jnp.mean(jnp.square(widened - center), axis=-1, keepdims=True))
    normed = (widened - center) * lax.rsqrt(spread + EPS)
    return (normed * (1.0 + scale_rows) + shift_rows).astype(jnp.bfloat16)

def rms_scaled(values, gain_row):
    return values * lax.rsqrt(lax.optimization_barrier(jnp.mean(jnp.square(values), axis=-1, keepdims=True)) + EPS) * gain_row

def project_heads(hidden, w_qkv, qk_gain, head_count):
    count = hidden.shape[0]
    mixed = jnp.dot(hidden, w_qkv.reshape(w_qkv.shape[0], -1), preferred_element_type=jnp.float32)
    mixed = mixed.reshape(count, 3, head_count, HD)
    queries = rms_scaled(mixed[:, 0], qk_gain[0])
    keys_img = rms_scaled(mixed[:, 1], qk_gain[1])
    return jnp.stack([queries, keys_img, mixed[:, 2]], axis=1).astype(jnp.bfloat16)

def one_request(packed, live, ctx):
    span = packed.shape[0]
    ctx_heads = ctx.reshape(2, TXT, HEADS, HD).astype(jnp.float32)
    queries = packed[:, 0].astype(jnp.float32)
    keys_img = packed[:, 1].astype(jnp.float32)
    values_img = packed[:, 2].astype(jnp.float32)
    factor = HD ** (-0.5)
    own = jnp.einsum('shd,thd->hst', queries, keys_img) * factor
    own = jnp.where(live[None, None, :] > 0, own, -1e+30)
    far = jnp.einsum('shd,thd->hst', queries, ctx_heads[0]) * factor
    scores = jnp.concatenate([own, far], axis=-1)
    top = lax.optimization_barrier(jnp.max(scores, axis=-1, keepdims=True))
    weights = jnp.exp(scores - top)
    total = lax.optimization_barrier(jnp.sum(weights, axis=-1, keepdims=True))
    probs = lax.optimization_barrier((weights / total).astype(jnp.bfloat16)).astype(jnp.float32)
    values_all = jnp.concatenate([values_img, ctx_heads[1]], axis=0)
    result = jnp.einsum('hst,thd->shd', probs, values_all)
    return result.astype(jnp.bfloat16).reshape(span, HEADS * HD)

def reference(tokens, route, tsteps, mod_table, w_qkv, qk_gain, context, w_out):
    reqs = N_DP * REQ_DEV
    cap = max(2, 2 * ROW_DEV // (REQ_DEV * N_DP))
    span = N_DP * cap
    inner = HEADS * HD
    request = route[:, 0]
    step_rows = tsteps[request]
    table = mod_table.astype(jnp.float32)
    shift_rows = table[:, 0, :][step_rows]
    scale_rows = table[:, 1, :][step_rows]
    hidden = modulate(tokens, shift_rows, scale_rows)
    packed = project_heads(hidden, w_qkv, qk_gain, HEADS)
    blocks = request.reshape(N_DP, ROW_DEV)
    onehot = (blocks[:, :, None] == jnp.arange(reqs, dtype=jnp.int32)[None, None, :]).astype(jnp.int32)
    rank = lax.optimization_barrier(jnp.sum(jnp.cumsum(onehot, axis=1) * onehot, axis=-1)) - 1
    source = jnp.arange(N_DP * ROW_DEV, dtype=jnp.int32) // ROW_DEV
    index = (request * span + source * cap + rank.reshape(-1)).astype(jnp.int32)
    slot_buf = jnp.zeros((reqs * span, 3, HEADS, HD), jnp.bfloat16).at[index].set(packed)
    live = jnp.zeros((reqs * span,), jnp.int32).at[index].set(1)
    outputs = lax.map(lambda items: one_request(items[0], items[1], items[2]), (slot_buf.reshape(reqs, span, 3, HEADS, HD), live.reshape(reqs, span), context))
    attn_rows = outputs.reshape(reqs * span, inner)[index]
    width = inner // N_MP
    out_sum = jnp.zeros((attn_rows.shape[0], D), jnp.float32)
    for group in range(N_MP):
        partial_term = jnp.dot(attn_rows[:, group * width:(group + 1) * width], w_out[group * width:(group + 1) * width], preferred_element_type=jnp.float32)
        out_sum = out_sum + lax.optimization_barrier(partial_term.astype(jnp.bfloat16)).astype(jnp.float32)
    gate_rows = table[:, 2, :][step_rows]
    return (tokens.astype(jnp.float32) + gate_rows * out_sum).astype(jnp.bfloat16)
```

```python
import jax
import jax.numpy as jnp
from jax import lax
from jax.sharding import PartitionSpec as P

HD = 64
TXT = 333
TSTEPS = 28
EPS = 1e-06
DEAD = 1e30


def rms_scaled(values, gain_row):
    return values * lax.rsqrt(jnp.mean(jnp.square(values), axis=-1, keepdims=True) + EPS) * gain_row


def attend(slots, context, head_count):
    span = slots.shape[0]
    grid = slots.reshape(span, 3, head_count, HD)
    live = slots[:, head_count * HD] < DEAD * 0.5
    ctx_heads = context.reshape(2, TXT, head_count, HD)
    factor = HD ** (-0.5)
    queries, keys_img, values_img = grid[:, 0], grid[:, 1], grid[:, 2]
    own = jnp.einsum("shd,thd->hst", queries, keys_img, preferred_element_type=jnp.float32) * factor
    own = jnp.where(live[None, None, :], own, -1e30)
    far = jnp.einsum("shd,thd->hst", queries, ctx_heads[0], preferred_element_type=jnp.float32) * factor
    top = jnp.maximum(jnp.max(own, axis=-1, keepdims=True), jnp.max(far, axis=-1, keepdims=True))
    own_weights = jnp.exp(own - top)
    far_weights = jnp.exp(far - top)
    total = jnp.sum(own_weights, axis=-1, keepdims=True) + jnp.sum(far_weights, axis=-1, keepdims=True)
    own_probs = (own_weights / total).astype(jnp.bfloat16)
    far_probs = (far_weights / total).astype(jnp.bfloat16)
    result = jnp.einsum("hst,thd->shd", own_probs, values_img, preferred_element_type=jnp.float32)
    result = result + jnp.einsum("hst,thd->shd", far_probs, ctx_heads[1], preferred_element_type=jnp.float32)
    return result.astype(jnp.bfloat16).reshape(span, head_count * HD)


def body(tokens, route, tsteps, mod_table, w_qkv, qk_gain, context, w_out):
    rows, width = tokens.shape
    requests = lax.axis_size("dp")
    parts = lax.axis_size("mp")
    chips = parts // 2
    cap = max(2, 2 * rows // requests)
    slots = requests * cap
    depth = w_qkv.shape[0]
    heads = w_qkv.shape[2] // HD
    inner = heads * HD
    core = lax.axis_index("mp") % 2
    along_z = [[2 * z + c for z in range(chips)] for c in range(2)]
    sibling = [(i, i ^ 1) for i in range(parts)]

    tokens_t = tokens.T
    own_half = lax.all_to_all(
        jnp.broadcast_to(tokens_t, (chips, width, rows)), "mp", 0, 0, axis_index_groups=along_z, tiled=True
    )
    other_half = lax.ppermute(own_half, "mp", sibling)

    request = route[:, 0]
    same = request[:, None] == request[None, :]
    before = jnp.arange(rows)[None, :] < jnp.arange(rows)[:, None]
    rank = jnp.sum((same & before).astype(jnp.int32), axis=1)
    position = request * cap + rank
    hits = position[None, :] == jnp.arange(slots, dtype=jnp.int32)[:, None]
    place = hits.astype(jnp.bfloat16)
    filled = jnp.any(hits, axis=1)
    step_of = jnp.dot(
        (request[:, None] == jnp.arange(requests, dtype=jnp.int32)[None, :]).astype(jnp.float32),
        tsteps.astype(jnp.float32),
    )
    pick = (step_of[:, None] == jnp.arange(TSTEPS, dtype=jnp.float32)[None, :]).astype(jnp.bfloat16)

    first = jnp.where(core == 0, own_half, other_half)
    second = jnp.where(core == 0, other_half, own_half)
    whole = jnp.stack([first, second], axis=1).reshape(depth, rows).astype(jnp.float32)
    shift_t = jnp.einsum("td,rt->dr", mod_table[:, 0], pick, preferred_element_type=jnp.float32)
    scale_t = jnp.einsum("td,rt->dr", mod_table[:, 1], pick, preferred_element_type=jnp.float32)
    center = jnp.mean(whole, axis=0, keepdims=True)
    spread = jnp.mean(jnp.square(whole - center), axis=0, keepdims=True)
    hidden = ((whole - center) * lax.rsqrt(spread + EPS) * (1.0 + scale_t) + shift_t).astype(jnp.bfloat16)
    proj = jnp.einsum("dr,dk->rk", hidden, w_qkv.reshape(depth, 3 * inner), preferred_element_type=jnp.float32)
    proj = proj.reshape(rows, 3, heads, HD)
    packed = jnp.stack(
        [rms_scaled(proj[:, 0], qk_gain[0]), rms_scaled(proj[:, 1], qk_gain[1]), proj[:, 2]], axis=1
    ).astype(jnp.bfloat16).reshape(rows, 3 * inner)
    send = jnp.dot(place, packed, preferred_element_type=jnp.float32).astype(jnp.bfloat16)
    is_key = (jnp.arange(3 * inner) >= inner) & (jnp.arange(3 * inner) < 2 * inner)
    send = jnp.where(is_key[None, :] & ~filled[:, None], jnp.bfloat16(DEAD), send)
    arrived = lax.all_to_all(send.reshape(requests, cap, 3 * inner), "dp", 0, 0, tiled=True)

    attn = attend(arrived.reshape(slots, 3 * inner), context[0], heads)
    returned = lax.all_to_all(attn.reshape(requests, cap, inner), "dp", 0, 0, tiled=True).reshape(slots, inner)
    attn_rows = jnp.einsum("sr,sk->rk", place, returned, preferred_element_type=jnp.float32).astype(jnp.bfloat16)

    partial = jnp.einsum("kd,rk->dr", w_out, attn_rows, preferred_element_type=jnp.float32)
    partial = partial.reshape(chips, 2, width, rows)
    keep = jnp.where(core == 0, partial[:, 0], partial[:, 1])
    give = jnp.where(core == 0, partial[:, 1], partial[:, 0]).astype(jnp.bfloat16)
    paired = (keep + lax.ppermute(give, "mp", sibling).astype(jnp.float32)).astype(jnp.bfloat16)
    spread_out = lax.all_to_all(paired, "mp", 0, 0, axis_index_groups=along_z, tiled=True)
    out_sum = jnp.sum(spread_out.astype(jnp.float32), axis=0)

    gate_table = lax.dynamic_slice_in_dim(mod_table[:, 2, :], lax.axis_index("mp") * width, width, 1)
    gate_t = jnp.einsum("td,rt->dr", gate_table, pick, preferred_element_type=jnp.float32)
    return (tokens_t.astype(jnp.float32) + gate_t * out_sum).astype(jnp.bfloat16).T


def solution(mesh):
    return jax.shard_map(
        body,
        mesh=mesh,
        in_specs=(
            P("dp", "mp"),
            P("dp", None),
            P(),
            P(),
            P(None, None, "mp"),
            P(),
            P("dp", None, None, "mp"),
            P("mp", None),
        ),
        out_specs=P("dp", "mp"),
        check_vma=False,
    )
```

```python
import functools

import jax
import jax.numpy as jnp
from jax import lax
from jax.experimental import pallas as pl
from jax.experimental.pallas import tpu as pltpu
from jax.sharding import PartitionSpec as P

HD = 64
TSTEPS = 28
EPS = 1e-06
DEAD = 1e30
MASKED = -1e30
VMEM_LIMIT = 24 * 1024 * 1024
F32, BF16 = jnp.float32, jnp.bfloat16


def dot_nt(a, b):
    return lax.dot_general(a, b, (((1,), (1,)), ((), ())), preferred_element_type=F32)


def project_kernel(core_ref, own_ref, other_ref, scale_ref, shift_ref, w_ref, gain_ref, pos_ref, send_ref, hid_ref):
    chips, width, rows = own_ref.shape
    depth = 2 * chips * width
    slots = send_ref.shape[0]
    inner = w_ref.shape[0] // 3
    is_first = core_ref[0] == 0

    def columns(ref):
        return [ref[z].astype(F32) for z in range(chips)]

    total = sum(jnp.sum(x, axis=0, keepdims=True) for x in columns(own_ref) + columns(other_ref))
    mean = total * (1.0 / depth)
    square = sum(jnp.sum(jnp.square(x - mean), axis=0, keepdims=True) for x in columns(own_ref) + columns(other_ref))
    inverse = lax.rsqrt(square * (1.0 / depth) + EPS)
    for z in range(chips):
        own, other = own_ref[z].astype(F32), other_ref[z].astype(F32)
        pair = jnp.concatenate([jnp.where(is_first, own, other), jnp.where(is_first, other, own)], axis=0)
        span = pl.ds(z * 2 * width, 2 * width)
        scale, shift = scale_ref[span, :].astype(F32), shift_ref[span, :].astype(F32)
        hid_ref[span, :] = ((pair - mean) * inverse * (1.0 + scale) + shift).astype(BF16)
    proj = jnp.dot(w_ref[...], hid_ref[...], preferred_element_type=F32)
    pieces = []
    for start in range(0, 2 * inner, HD):
        head = proj[start : start + HD]
        power = jnp.mean(jnp.square(head), axis=0, keepdims=True)
        pieces.append(head * lax.rsqrt(power + EPS) * gain_ref[pl.ds(start, HD), :])
    pieces.append(proj[2 * inner :])
    packed = jnp.concatenate(pieces, axis=0).astype(BF16)
    hits = lax.broadcasted_iota(jnp.int32, (slots, rows), 0) == pos_ref[...]
    place = jnp.where(hits, 1.0, 0.0)
    filled = jnp.sum(place, axis=1, keepdims=True)
    send = dot_nt(place.astype(BF16), packed)
    send_ref[:, 0:inner] = send[:, 0:inner].astype(BF16)
    send_ref[:, inner : 2 * inner] = jnp.where(filled > 0.5, send[:, inner : 2 * inner], DEAD).astype(BF16)
    send_ref[:, 2 * inner :] = send[:, 2 * inner :].astype(BF16)


def attend_kernel(text_len, slots_ref, ctx_ref, out_ref):
    slots, inner = out_ref.shape
    block = 128
    text_pad = ctx_ref.shape[1]
    queries = slots_ref[:, 0:inner]
    keys = slots_ref[:, inner : 2 * inner].astype(F32)
    values = slots_ref[:, 2 * inner :]
    text_keys, text_values = ctx_ref[0], ctx_ref[1]
    dead = keys > 0.5 * DEAD
    marks = jnp.where(dead, 1.0, 0.0).astype(BF16)
    keys = jnp.where(dead, 0.0, keys).astype(BF16)
    own_bias = dot_nt(jnp.full((8, inner), MASKED, BF16), marks)[0:1]
    text_lane = lax.broadcasted_iota(jnp.int32, (1, text_pad), 1)
    text_bias = jnp.where(text_lane < text_len, 0.0, MASKED)
    lane = lax.broadcasted_iota(jnp.int32, (1, inner), 1)
    one = jnp.ones((), BF16)
    zero = jnp.zeros((), BF16)
    for row in range(0, slots, block):
        parts = []
        for head in range(inner // HD):
            mine = (lane >= head * HD) & (lane < (head + 1) * HD)
            query = jnp.where(mine, queries[row : row + block], zero)
            own = dot_nt(query, keys) + own_bias
            far = dot_nt(query, text_keys) + text_bias
            top = jnp.maximum(jnp.max(own, axis=1, keepdims=True), jnp.max(far, axis=1, keepdims=True))
            own = jnp.exp(own - top).astype(BF16)
            far = jnp.exp(far - top).astype(BF16)
            mixed = jnp.dot(own, jnp.where(mine, values, one), preferred_element_type=F32)
            mixed = mixed + jnp.dot(far, jnp.where(mine, text_values, one), preferred_element_type=F32)
            parts.append((mine, mixed / pltpu.roll(mixed, HD, 1)))
        out_ref[row : row + block, :] = jnp.where(parts[0][0], parts[0][1], parts[1][1]).astype(BF16)


def give_kernel(core_ref, back_ref, pos_ref, w_ref, give_ref, rows_ref):
    slots = back_ref.shape[0]
    rows = rows_ref.shape[0]
    hits = lax.broadcasted_iota(jnp.int32, (rows, slots), 1) == pos_ref[...]
    place = jnp.where(hits, 1.0, 0.0).astype(BF16)
    attn = jnp.dot(place, back_ref[...], preferred_element_type=F32).astype(BF16)
    rows_ref[...] = attn
    other = 1 - core_ref[0]
    for z in range(give_ref.shape[0]):
        give_ref[z] = dot_nt(w_ref[z, other], attn).astype(BF16)


def keep_kernel(core_ref, rows_ref, w_ref, keep_ref):
    core = core_ref[0]
    for z in range(keep_ref.shape[0]):
        keep_ref[z] = dot_nt(w_ref[z, core], rows_ref[...])


def call(kernel, out_shape, smem, vmem, scratch=(), flops=0):
    whole = pl.BlockSpec(memory_space=pltpu.VMEM)
    outs = jax.tree.map(lambda _: whole, out_shape)
    return pl.pallas_call(
        kernel,
        out_shape=out_shape,
        in_specs=[pl.BlockSpec(memory_space=pltpu.SMEM)] * smem + [whole] * vmem,
        out_specs=outs,
        scratch_shapes=list(scratch),
        compiler_params=pltpu.CompilerParams(vmem_limit_bytes=VMEM_LIMIT),
        cost_estimate=pl.CostEstimate(flops=flops, bytes_accessed=1 << 20, transcendentals=0),
    )


def body(tokens, route, tsteps, mod_table, w_qkv, qk_gain, context, w_out):
    rows, width = tokens.shape
    requests = lax.axis_size("dp")
    parts = lax.axis_size("mp")
    chips = parts // 2
    cap = max(2, 2 * rows // requests)
    slots = requests * cap
    depth = w_qkv.shape[0]
    inner = w_qkv.shape[2]
    text_len = context.shape[2]
    text_pad = -(-text_len // 128) * 128
    along_z = [[2 * z + c for z in range(chips)] for c in range(2)]
    sibling = [(i, i ^ 1) for i in range(parts)]
    core = lax.rem(lax.axis_index("mp"), 2).astype(jnp.int32).reshape(1)

    tokens_t = tokens.T
    own_half = lax.all_to_all(
        jnp.broadcast_to(tokens_t, (chips, width, rows)), "mp", 0, 0, axis_index_groups=along_z, tiled=True
    )

    request = route[:, 0]
    same = request[:, None] == request[None, :]
    before = jnp.arange(rows)[None, :] < jnp.arange(rows)[:, None]
    rank = jnp.sum((same & before).astype(jnp.int32), axis=1)
    position = request * cap + rank
    step_of = jnp.dot(
        (request[:, None] == jnp.arange(requests, dtype=jnp.int32)[None, :]).astype(F32), tsteps.astype(F32)
    )
    pick = (step_of[:, None] == jnp.arange(TSTEPS, dtype=F32)[None, :]).astype(BF16)
    shift_t = jnp.einsum("td,rt->dr", mod_table[:, 0], pick, preferred_element_type=F32).astype(BF16)
    scale_t = jnp.einsum("td,rt->dr", mod_table[:, 1], pick, preferred_element_type=F32).astype(BF16)
    gate_table = lax.dynamic_slice_in_dim(mod_table[:, 2, :], lax.axis_index("mp") * width, width, 1)
    gate_t = jnp.einsum("td,rt->dr", gate_table, pick, preferred_element_type=F32)
    w_t = w_qkv.transpose(1, 2, 0).reshape(3 * inner, depth)
    w_out_t = w_out.T.reshape(chips, 2, width, inner)
    gains = jnp.concatenate(
        [jnp.tile(qk_gain[0] * HD ** (-0.5), inner // HD), jnp.tile(qk_gain[1], inner // HD)]
    ).reshape(2 * inner, 1)
    text = jnp.pad(context[0], ((0, 0), (0, text_pad - text_len), (0, 0)))
    own_half, position, shift_t, scale_t, gate_t, w_t, w_out_t, gains, text = lax.optimization_barrier(
        (own_half, position, shift_t, scale_t, gate_t, w_t, w_out_t, gains, text)
    )
    other_half = lax.ppermute(own_half, "mp", sibling)

    send = call(
        project_kernel,
        jax.ShapeDtypeStruct((slots, 3 * inner), BF16),
        1,
        7,
        [pltpu.VMEM((depth, rows), BF16)],
        flops=2 * depth * rows * 3 * inner,
    )(core, own_half, other_half, scale_t, shift_t, w_t, gains, position.reshape(1, rows))
    arrived = lax.all_to_all(send.reshape(requests, cap, 3 * inner), "dp", 0, 0, tiled=True)

    attn = call(
        functools.partial(attend_kernel, text_len),
        jax.ShapeDtypeStruct((slots, inner), BF16),
        0,
        2,
        flops=8 * slots * (slots + text_pad) * inner,
    )(arrived.reshape(slots, 3 * inner), text)
    returned = lax.all_to_all(attn.reshape(requests, cap, inner), "dp", 0, 0, tiled=True).reshape(slots, inner)

    give, attn_rows = call(
        give_kernel,
        (jax.ShapeDtypeStruct((chips, width, rows), BF16), jax.ShapeDtypeStruct((rows, inner), BF16)),
        1,
        3,
        flops=depth * rows * inner,
    )(core, returned, position.reshape(rows, 1), w_out_t)
    given = lax.ppermute(give, "mp", sibling)
    keep = call(
        keep_kernel, jax.ShapeDtypeStruct((chips, width, rows), F32), 1, 2, flops=depth * rows * inner
    )(core, attn_rows, w_out_t)
    paired = (keep + given.astype(F32)).astype(BF16)
    spread_out = lax.all_to_all(paired, "mp", 0, 0, axis_index_groups=along_z, tiled=True)
    out_sum = jnp.sum(spread_out.astype(F32), axis=0)
    return (tokens_t.astype(F32) + gate_t * out_sum).astype(BF16).T


def solution(mesh):
    return jax.shard_map(
        body,
        mesh=mesh,
        in_specs=(
            P("dp", "mp"),
            P("dp", None),
            P(),
            P(),
            P(None, None, "mp"),
            P(),
            P("dp", None, None, "mp"),
            P("mp", None),
        ),
        out_specs=P("dp", "mp"),
        check_vma=False,
    )
```

```python
import functools

import jax
import jax.numpy as jnp
from jax import lax
from jax.experimental import pallas as pl
from jax.experimental.pallas import tpu as pltpu
from jax.sharding import PartitionSpec as P

HD = 64
EPS = 1e-06
DEAD = 1e30
MASKED = -1e30
VMEM_LIMIT = 24 * 1024 * 1024
F32, BF16, I32 = jnp.float32, jnp.bfloat16, jnp.int32


def dot_nt(a, b):
    return lax.dot_general(a, b, (((1,), (1,)), ((), ())), preferred_element_type=F32)


def dot_tn(a, b):
    return lax.dot_general(a, b, (((0,), (0,)), ((), ())), preferred_element_type=F32)


def iota(shape, axis):
    return lax.broadcasted_iota(I32, shape, axis)


def as_column(row):
    n = row.shape[1]
    return jnp.sum(jnp.where(iota((n, n), 0) == iota((n, n), 1), row, 0.0), axis=1, keepdims=True)


def one_hot(flags):
    return jnp.where(flags, 1.0, 0.0).astype(BF16)


def dealt(rows):
    half = rows // 2
    place = iota((rows, rows), 0)
    return jnp.where(place < half, 2 * place, 2 * (place - half) + 1).astype(F32)


def spread_kernel(tok_ref, req_ref, out_ref, perm_ref, pos_ref):
    width, rows = tok_ref.shape
    half = rows // 2
    req = req_ref[...].astype(F32)
    req_col = as_column(req)
    earlier = (req_col < req) | ((req_col == req) & (iota((rows, rows), 0) < iota((rows, rows), 1)))
    pos = jnp.sum(jnp.where(earlier, 1.0, 0.0), axis=0, keepdims=True)
    pos_ref[...] = pos
    perm = dot_nt(tok_ref[...], one_hot(pos == dealt(rows))).astype(BF16)
    perm_ref[...] = perm
    for m in range(out_ref.shape[0]):
        out_ref[m] = perm[:, (m % 2) * half : (m % 2 + 1) * half]


def prepare_kernel(
    cap, core_ref, req_ref, pos_ref, steps_ref, table_ref, gate_ref,
    scale_ref, shift_ref, gates_ref, place_ref, place_t_ref, mark_ref,
):
    rows = req_ref.shape[1]
    half = rows // 2
    slots = place_ref.shape[0]
    requests = steps_ref.shape[1]
    levels = table_ref.shape[1]
    is_first = core_ref[0] == 0
    req = req_ref[...].astype(F32)
    first = jnp.sum(jnp.where(as_column(req) < req, 1.0, 0.0), axis=0, keepdims=True)
    deal = one_hot(pos_ref[...] == dealt(rows))
    line = iota((8, rows), 0)
    both = jnp.where(line == 0, req, jnp.where(line == 1, first, 0.0)).astype(BF16)
    both = dot_nt(both, deal)
    req_s, first_s = both[0:1], both[1:2]
    index = iota((1, rows), 1)
    odd = jnp.where(index >= half, 1, 0)
    start = jnp.floor((first_s - odd.astype(F32) + 1.0) * 0.5)
    slot = req_s * cap + (index - half * odd).astype(F32) - start
    chosen = one_hot(iota((requests, rows), 0).astype(F32) == req_s)
    steps = jnp.broadcast_to(steps_ref[...].astype(F32), (8, requests)).astype(BF16)
    step = jnp.dot(steps, chosen, preferred_element_type=F32)[0:1]
    pick = one_hot(iota((levels, rows), 0).astype(F32) == step)
    gates_ref[...] = dot_tn(gate_ref[...], pick)
    pick = jnp.where(is_first, pick[:, :half].astype(F32), pick[:, half:].astype(F32)).astype(BF16)
    shift_ref[...] = dot_tn(table_ref[0], pick).astype(BF16)
    scale_ref[...] = dot_tn(table_ref[1], pick).astype(BF16)
    slot = jnp.where(is_first, slot[:, :half], slot[:, half:])
    hits = iota((slots, half), 0).astype(F32) == slot
    place_ref[...] = one_hot(hits)
    filled = jnp.sum(jnp.where(hits, 1.0, 0.0), axis=1, keepdims=True)
    mark_ref[...] = jnp.broadcast_to(jnp.where(filled > 0.5, 0.0, DEAD), mark_ref.shape)
    place_t_ref[...] = one_hot(iota((half, slots), 1).astype(F32) == as_column(slot))


def project_kernel(
    core_ref, tok_ref, scale_ref, shift_ref, own_ref, sib_ref, gain_ref, place_ref, mark_ref, send_ref, hid_ref
):
    parts, width, rows = tok_ref.shape
    depth = parts * width
    inner = own_ref.shape[0] // 3
    total = sum(jnp.sum(tok_ref[m].astype(F32), axis=0, keepdims=True) for m in range(parts))
    mean = total * (1.0 / depth)
    square = sum(jnp.sum(jnp.square(tok_ref[m].astype(F32) - mean), axis=0, keepdims=True) for m in range(parts))
    inverse = lax.rsqrt(square * (1.0 / depth) + EPS)
    for m in range(0, parts, 2):
        pair = jnp.concatenate([tok_ref[m].astype(F32), tok_ref[m + 1].astype(F32)], axis=0)
        span = pl.ds(m * width, 2 * width)
        scale, shift = scale_ref[span, :].astype(F32), shift_ref[span, :].astype(F32)
        hid_ref[span, :] = ((pair - mean) * inverse * (1.0 + scale) + shift).astype(BF16)
    hidden = hid_ref[...]
    for w_ref, target in ((own_ref, core_ref[0]), (sib_ref, 1 - core_ref[0])):
        proj = jnp.dot(w_ref[...], hidden, preferred_element_type=F32)
        pieces = []
        for start in range(0, 2 * inner, HD):
            head = proj[start : start + HD]
            power = jnp.mean(jnp.square(head), axis=0, keepdims=True)
            pieces.append(head * lax.rsqrt(power + EPS) * gain_ref[pl.ds(start, HD), :])
        pieces.append(proj[2 * inner :])
        send = dot_nt(place_ref[...], jnp.concatenate(pieces, axis=0).astype(BF16))
        mark = mark_ref[...]
        send = jnp.concatenate([send[:, :inner], send[:, inner : 2 * inner] + mark, send[:, 2 * inner :]], axis=1)
        send_ref[target] = send.astype(BF16)


def attend_kernel(text_len, slots_ref, ctx_ref, out_ref):
    slots, inner = out_ref.shape
    block = 128
    text_pad = ctx_ref.shape[1]
    queries = slots_ref[:, 0:inner]
    keys = slots_ref[:, inner : 2 * inner].astype(F32)
    values = slots_ref[:, 2 * inner :]
    text_keys, text_values = ctx_ref[0], ctx_ref[1]
    dead = keys > 0.5 * DEAD
    marks = jnp.where(dead, 1.0, 0.0).astype(BF16)
    keys = jnp.where(dead, 0.0, keys).astype(BF16)
    own_bias = dot_nt(jnp.full((8, inner), MASKED, BF16), marks)[0:1]
    text_bias = jnp.where(iota((1, text_pad), 1) < text_len, 0.0, MASKED)
    lane = iota((1, inner), 1)
    one = jnp.ones((), BF16)
    zero = jnp.zeros((), BF16)
    for row in range(0, slots, block):
        parts = []
        for head in range(inner // HD):
            mine = (lane >= head * HD) & (lane < (head + 1) * HD)
            query = jnp.where(mine, queries[row : row + block], zero)
            own = dot_nt(query, keys) + own_bias
            far = dot_nt(query, text_keys) + text_bias
            top = jnp.maximum(jnp.max(own, axis=1, keepdims=True), jnp.max(far, axis=1, keepdims=True))
            own = jnp.exp(own - top).astype(BF16)
            far = jnp.exp(far - top).astype(BF16)
            mixed = jnp.dot(own, jnp.where(mine, values, one), preferred_element_type=F32)
            mixed = mixed + jnp.dot(far, jnp.where(mine, text_values, one), preferred_element_type=F32)
            parts.append((mine, mixed / pltpu.roll(mixed, HD, 1)))
        out_ref[row : row + block, :] = jnp.where(parts[0][0], parts[0][1], parts[1][1]).astype(BF16)


def output_kernel(core_ref, back_ref, place_t_ref, w_ref, part_ref):
    core = core_ref[0]
    place_t = place_t_ref[...]
    own = jnp.dot(place_t, back_ref[core], preferred_element_type=F32).astype(BF16)
    sib = jnp.dot(place_t, back_ref[1 - core], preferred_element_type=F32).astype(BF16)
    attn = jnp.concatenate([own, sib], axis=1)
    for m in range(part_ref.shape[0]):
        part_ref[m] = dot_nt(w_ref[m], attn).astype(BF16)


def finish_kernel(sums_ref, perm_ref, gates_ref, pos_ref, out_ref):
    parts = sums_ref.shape[0]
    halves = [sum(sums_ref[m].astype(F32) for m in range(c, parts, 2)) for c in range(2)]
    total = jnp.concatenate(halves, axis=1)
    mixed = (perm_ref[...].astype(F32) + gates_ref[...] * total).astype(BF16)
    rows = perm_ref.shape[1]
    deal = one_hot(pos_ref[...] == dealt(rows))
    out_ref[...] = jnp.dot(mixed, deal, preferred_element_type=F32).astype(BF16)


def call(kernel, out_shape, smem, vmem, scratch=(), flops=0):
    whole = pl.BlockSpec(memory_space=pltpu.VMEM)
    outs = jax.tree.map(lambda _: whole, out_shape)
    return pl.pallas_call(
        kernel,
        out_shape=out_shape,
        in_specs=[pl.BlockSpec(memory_space=pltpu.SMEM)] * smem + [whole] * vmem,
        out_specs=outs,
        scratch_shapes=list(scratch),
        compiler_params=pltpu.CompilerParams(vmem_limit_bytes=VMEM_LIMIT),
        cost_estimate=pl.CostEstimate(flops=flops, bytes_accessed=1 << 20, transcendentals=0),
    )


def body(tokens, route, tsteps, mod_table, w_qkv, qk_gain, context, w_out):
    rows, width = tokens.shape
    half = rows // 2
    requests = lax.axis_size("dp")
    parts = lax.axis_size("mp")
    chips = parts // 2
    cap = max(2, 2 * rows // requests) // 2
    slots = requests * cap
    depth = w_qkv.shape[0]
    inner = w_qkv.shape[2]
    text_len = context.shape[2]
    text_pad = -(-text_len // 128) * 128
    sibling = [(i, i ^ 1) for i in range(parts)]
    planes = [[dp * parts + 2 * z + c for c in range(2) for dp in range(requests)] for z in range(chips)]
    core = lax.rem(lax.axis_index("mp"), 2).astype(I32).reshape(1)
    shape = jax.ShapeDtypeStruct

    req = route.reshape(1, rows)
    spread, perm, pos = call(
        spread_kernel,
        (shape((parts, width, half), BF16), shape((width, rows), BF16), shape((1, rows), F32)),
        0,
        2,
    )(tokens.T, req)
    whole = lax.all_to_all(spread, "mp", 0, 0, tiled=True)

    w_own = w_qkv.transpose(1, 2, 0).reshape(3 * inner, depth)
    w_sib = lax.ppermute(w_own, "mp", sibling)
    out_own = w_out.T
    out_sib = lax.ppermute(out_own, "mp", sibling)
    w_back = jnp.concatenate([out_own, out_sib], axis=1).reshape(parts, width, 2 * inner)
    gate_table = lax.dynamic_slice_in_dim(mod_table[:, 2, :], lax.axis_index("mp") * width, width, 1)
    scale, shift, gates, place, place_t, mark = call(
        functools.partial(prepare_kernel, cap),
        (
            shape((depth, half), BF16),
            shape((depth, half), BF16),
            shape((width, rows), F32),
            shape((slots, half), BF16),
            shape((half, slots), BF16),
            shape((slots, inner), F32),
        ),
        1,
        5,
    )(core, req, pos, tsteps.reshape(1, requests), mod_table.transpose(1, 0, 2), gate_table)
    gains = jnp.concatenate(
        [jnp.tile(qk_gain[0] * HD ** (-0.5), inner // HD), jnp.tile(qk_gain[1], inner // HD)]
    ).reshape(2 * inner, 1)
    text = jnp.pad(context[0], ((0, 0), (0, text_pad - text_len), (0, 0)))
    whole, w_own, w_sib, w_back, scale, shift, gates, place, place_t, mark, gains, text = lax.optimization_barrier(
        (whole, w_own, w_sib, w_back, scale, shift, gates, place, place_t, mark, gains, text)
    )

    send = call(
        project_kernel,
        shape((2, slots, 3 * inner), BF16),
        1,
        8,
        [pltpu.VMEM((depth, half), BF16)],
        flops=4 * depth * half * 3 * inner,
    )(core, whole, scale, shift, w_own, w_sib, gains, place, mark)
    arrived = lax.all_to_all(
        send.reshape(2 * requests, cap, 3 * inner), ("dp", "mp"), 0, 0, axis_index_groups=planes, tiled=True
    )
    attn = call(
        functools.partial(attend_kernel, text_len),
        shape((2 * slots, inner), BF16),
        0,
        2,
        flops=16 * slots * (2 * slots + text_pad) * inner,
    )(arrived.reshape(2 * slots, 3 * inner), text)
    returned = lax.all_to_all(
        attn.reshape(2 * requests, cap, inner), ("dp", "mp"), 0, 0, axis_index_groups=planes, tiled=True
    )
    partial = call(output_kernel, shape((parts, width, half), BF16), 1, 3, flops=4 * depth * half * inner)(
        core, returned.reshape(2, slots, inner), place_t, w_back
    )
    sums = lax.all_to_all(partial, "mp", 0, 0, tiled=True)
    return call(finish_kernel, shape((width, rows), BF16), 0, 4)(sums, perm, gates, pos).T


def solution(mesh):
    return jax.shard_map(
        body,
        mesh=mesh,
        in_specs=(
            P("dp", "mp"),
            P("dp", None),
            P(),
            P(),
            P(None, None, "mp"),
            P(),
            P("dp", None, None, "mp"),
            P("mp", None),
        ),
        out_specs=P("dp", "mp"),
        check_vma=False,
    )
```

```python
import functools

import jax
import jax.numpy as jnp
from jax import lax
from jax.experimental import pallas as pl
from jax.experimental.pallas import tpu as pltpu
from jax.sharding import PartitionSpec as P

HD = 64
EPS = 1e-06
DEAD = 1e30
MASKED = -1e30
VMEM_LIMIT = 24 * 1024 * 1024
F32, BF16, I32 = jnp.float32, jnp.bfloat16, jnp.int32


PLACES = {
    "s": pl.BlockSpec(memory_space=pltpu.SMEM),
    "v": pl.BlockSpec(memory_space=pltpu.VMEM),
    "a": pl.BlockSpec(memory_space=pl.ANY),
}


def dot_nt(a, b):
    return lax.dot_general(a, b, (((1,), (1,)), ((), ())), preferred_element_type=F32)


def dot_tn(a, b):
    return lax.dot_general(a, b, (((0,), (0,)), ((), ())), preferred_element_type=F32)


def iota(shape, axis):
    return lax.broadcasted_iota(I32, shape, axis)


def as_column(row):
    n = row.shape[1]
    return jnp.sum(jnp.where(iota((n, n), 0) == iota((n, n), 1), row, 0.0), axis=1, keepdims=True)


def one_hot(flags):
    return jnp.where(flags, 1.0, 0.0).astype(BF16)


def dealt(rows):
    half = rows // 2
    place = iota((rows, rows), 0)
    return jnp.where(place < half, 2 * place, 2 * (place - half) + 1).astype(F32)


def spread_kernel(tok_ref, req_ref, out_ref, perm_ref, pos_ref):
    width, rows = tok_ref.shape
    half = rows // 2
    req = req_ref[...].astype(F32)
    req_col = as_column(req)
    earlier = (req_col < req) | ((req_col == req) & (iota((rows, rows), 0) < iota((rows, rows), 1)))
    pos = jnp.sum(jnp.where(earlier, 1.0, 0.0), axis=0, keepdims=True)
    pos_ref[...] = pos
    perm = dot_nt(tok_ref[...], one_hot(pos == dealt(rows))).astype(BF16)
    perm_ref[...] = perm
    for m in range(out_ref.shape[0]):
        out_ref[m] = perm[:, (m % 2) * half : (m % 2 + 1) * half]


def prepare_kernel(
    cap, core_ref, req_ref, pos_ref, steps_ref, table_ref, gate_ref, mod_hbm, gates_ref, slot_ref, mod_ref, sem
):
    rows = req_ref.shape[1]
    half = rows // 2
    requests = steps_ref.shape[1]
    levels = table_ref.shape[1]
    is_first = core_ref[0] == 0
    req = req_ref[...].astype(F32)
    first = jnp.sum(jnp.where(as_column(req) < req, 1.0, 0.0), axis=0, keepdims=True)
    deal = one_hot(pos_ref[...] == dealt(rows))
    line = iota((8, rows), 0)
    both = jnp.where(line == 0, req, jnp.where(line == 1, first, 0.0)).astype(BF16)
    both = dot_nt(both, deal)
    req_s, first_s = both[0:1], both[1:2]
    index = iota((1, rows), 1)
    odd = jnp.where(index >= half, 1, 0)
    start = jnp.floor((first_s - odd.astype(F32) + 1.0) * 0.5)
    slot = req_s * cap + (index - half * odd).astype(F32) - start
    slot_ref[...] = jnp.where(is_first, slot[:, :half], slot[:, half:])
    chosen = one_hot(iota((requests, rows), 0).astype(F32) == req_s)
    steps = jnp.broadcast_to(steps_ref[...].astype(F32), (8, requests)).astype(BF16)
    step = jnp.dot(steps, chosen, preferred_element_type=F32)[0:1]
    pick = one_hot(iota((levels, rows), 0).astype(F32) == step)
    gates_ref[...] = dot_tn(gate_ref[...], pick).astype(BF16)
    pick = jnp.where(is_first, pick[:, :half].astype(F32), pick[:, half:].astype(F32)).astype(BF16)
    mod_ref[0] = dot_tn(table_ref[0], pick).astype(BF16)
    mod_ref[1] = dot_tn(table_ref[1], pick).astype(BF16)
    copy = pltpu.make_async_copy(mod_ref, mod_hbm, sem)
    copy.start()
    copy.wait()


def flip_kernel(own_ref, sib_ref, out_ref):
    inner, depth = own_ref.shape
    for start in range(0, depth, 128):
        for side, ref in enumerate((own_ref, sib_ref)):
            block = ref[:, start : start + 128].astype(F32).T
            out_ref[start : start + 128, side * inner : (side + 1) * inner] = block.astype(BF16)


def project_kernel(
    core_ref, tok_hbm, mod_hbm, own_hbm, sib_hbm, gain_ref, slot_ref, send_ref, tok_ref, mod_ref, w_ref, hid_ref, sems
):
    parts, width, rows = tok_ref.shape
    depth = parts * width
    kinds, _, inner = own_hbm.shape
    span = kinds * inner
    copies = [pltpu.make_async_copy(tok_hbm, tok_ref, sems.at[0]), pltpu.make_async_copy(mod_hbm, mod_ref, sems.at[1])]
    for side, hbm in enumerate((own_hbm, sib_hbm)):
        for kind in range(kinds):
            lanes = pl.ds(side * span + kind * inner, inner)
            copies.append(pltpu.make_async_copy(hbm.at[kind], w_ref.at[:, lanes], sems.at[2 + side * kinds + kind]))
    for copy in copies:
        copy.start()
    hits = iota((send_ref.shape[1], rows), 0).astype(F32) == slot_ref[...]
    filled = jnp.sum(jnp.where(hits, 1.0, 0.0), axis=1, keepdims=True)
    mark = jnp.where(filled > 0.5, 0.0, DEAD)
    place = one_hot(hits)
    copies[0].wait()
    total = sum(jnp.sum(tok_ref[m].astype(F32), axis=0, keepdims=True) for m in range(parts))
    mean = total * (1.0 / depth)
    square = sum(jnp.sum(jnp.square(tok_ref[m].astype(F32) - mean), axis=0, keepdims=True) for m in range(parts))
    inverse = lax.rsqrt(square * (1.0 / depth) + EPS)
    copies[1].wait()
    for m in range(0, parts, 2):
        pair = jnp.concatenate([tok_ref[m].astype(F32), tok_ref[m + 1].astype(F32)], axis=0)
        lines = pl.ds(m * width, 2 * width)
        shift, scale = mod_ref[0, lines, :].astype(F32), mod_ref[1, lines, :].astype(F32)
        hid_ref[lines, :] = ((pair - mean) * inverse * (1.0 + scale) + shift).astype(BF16)
    for copy in copies[2:]:
        copy.wait()
    proj = dot_tn(hid_ref[...], w_ref[...])
    normed = 2 * inner
    heads = one_hot(iota((normed, normed), 0) // HD == iota((normed, normed), 1) // HD)
    for side, target in enumerate((core_ref[0], 1 - core_ref[0])):
        mixed = proj[:, side * span : (side + 1) * span]
        turned = mixed[:, :normed]
        power = jnp.square(turned)
        high = power.astype(BF16)
        low = (power - high.astype(F32)).astype(BF16)
        power = jnp.dot(high, heads, preferred_element_type=F32) + jnp.dot(low, heads, preferred_element_type=F32)
        turned = turned * lax.rsqrt(power * (1.0 / HD) + EPS) * gain_ref[...]
        packed = jnp.concatenate([turned, mixed[:, normed:]], axis=1).astype(BF16)
        send = jnp.dot(place, packed, preferred_element_type=F32)
        send = jnp.concatenate([send[:, :inner], send[:, inner:normed] + mark, send[:, normed:]], axis=1)
        send_ref[target] = send.astype(BF16)


def attend_kernel(text_len, slots_ref, ctx_ref, out_ref):
    slots, inner = out_ref.shape
    block = 128
    text_pad = ctx_ref.shape[1]
    queries = slots_ref[:, 0:inner]
    keys = slots_ref[:, inner : 2 * inner].astype(F32)
    values = slots_ref[:, 2 * inner :]
    text_keys, text_values = ctx_ref[0], ctx_ref[1]
    dead = keys > 0.5 * DEAD
    marks = jnp.where(dead, 1.0, 0.0).astype(BF16)
    keys = jnp.where(dead, 0.0, keys).astype(BF16)
    own_bias = dot_nt(jnp.full((8, inner), MASKED, BF16), marks)[0:1]
    text_bias = jnp.where(iota((1, text_pad), 1) < text_len, 0.0, MASKED)
    lane = iota((1, inner), 1)
    one = jnp.ones((), BF16)
    zero = jnp.zeros((), BF16)
    for row in range(0, slots, block):
        parts = []
        for head in range(inner // HD):
            mine = (lane >= head * HD) & (lane < (head + 1) * HD)
            query = jnp.where(mine, queries[row : row + block], zero)
            own = dot_nt(query, keys) + own_bias
            far = dot_nt(query, text_keys) + text_bias
            top = jnp.maximum(jnp.max(own, axis=1, keepdims=True), jnp.max(far, axis=1, keepdims=True))
            own = jnp.exp(own - top).astype(BF16)
            far = jnp.exp(far - top).astype(BF16)
            mixed = jnp.dot(own, jnp.where(mine, values, one), preferred_element_type=F32)
            mixed = mixed + jnp.dot(far, jnp.where(mine, text_values, one), preferred_element_type=F32)
            parts.append((mine, mixed / pltpu.roll(mixed, HD, 1)))
        out_ref[row : row + block, :] = jnp.where(parts[0][0], parts[0][1], parts[1][1]).astype(BF16)


def output_kernel(core_ref, back_ref, slot_ref, w_ref, part_ref):
    core = core_ref[0]
    slots, rows = back_ref.shape[1], slot_ref.shape[1]
    place_t = one_hot(iota((rows, slots), 1).astype(F32) == as_column(slot_ref[...]))
    own = jnp.dot(place_t, back_ref[core], preferred_element_type=F32).astype(BF16)
    sib = jnp.dot(place_t, back_ref[1 - core], preferred_element_type=F32).astype(BF16)
    attn = jnp.concatenate([own, sib], axis=1)
    for m in range(part_ref.shape[0]):
        part_ref[m] = dot_nt(w_ref[m], attn).astype(BF16)


def finish_kernel(sums_ref, perm_ref, gates_ref, pos_ref, out_ref):
    parts = sums_ref.shape[0]
    halves = [sum(sums_ref[m].astype(F32) for m in range(c, parts, 2)) for c in range(2)]
    total = jnp.concatenate(halves, axis=1)
    mixed = (perm_ref[...].astype(F32) + gates_ref[...].astype(F32) * total).astype(BF16)
    rows = perm_ref.shape[1]
    deal = one_hot(pos_ref[...] == dealt(rows))
    out_ref[...] = jnp.dot(mixed, deal, preferred_element_type=F32).astype(BF16)


def call(kernel, out_shape, specs, out_specs, scratch=(), flops=0):
    return pl.pallas_call(
        kernel,
        out_shape=out_shape,
        in_specs=[PLACES[letter] for letter in specs],
        out_specs=tuple(PLACES[letter] for letter in out_specs) if len(out_specs) > 1 else PLACES[out_specs],
        scratch_shapes=list(scratch),
        compiler_params=pltpu.CompilerParams(vmem_limit_bytes=VMEM_LIMIT),
        cost_estimate=pl.CostEstimate(flops=flops, bytes_accessed=1 << 20, transcendentals=0),
    )


def body(tokens, route, tsteps, mod_table, w_qkv, qk_gain, context, w_out):
    rows, width = tokens.shape
    half = rows // 2
    requests = lax.axis_size("dp")
    parts = lax.axis_size("mp")
    chips = parts // 2
    cap = max(2, 2 * rows // requests) // 2
    slots = requests * cap
    depth, kinds, inner = w_qkv.shape
    text_len = context.shape[2]
    text_pad = -(-text_len // 128) * 128
    sibling = [(i, i ^ 1) for i in range(parts)]
    planes = [[dp * parts + 2 * z + c for c in range(2) for dp in range(requests)] for z in range(chips)]
    core = lax.rem(lax.axis_index("mp"), 2).astype(I32).reshape(1)
    shape = jax.ShapeDtypeStruct

    req = route.reshape(1, rows)
    spread, perm, pos = call(
        spread_kernel,
        (shape((parts, width, half), BF16), shape((width, rows), BF16), shape((1, rows), F32)),
        "vv",
        "vvv",
    )(tokens.T, req)
    spread, w_qkv, w_out = lax.optimization_barrier((spread, w_qkv, w_out))
    whole = lax.all_to_all(spread, "mp", 0, 0, tiled=True)

    w_own = w_qkv.transpose(1, 0, 2)
    w_sib = lax.ppermute(w_own, "mp", sibling)
    out_sib = lax.ppermute(w_out, "mp", sibling)
    gate_table = lax.dynamic_slice_in_dim(mod_table[:, 2, :], lax.axis_index("mp") * width, width, 1)
    mod, gates, slot = call(
        functools.partial(prepare_kernel, cap),
        (shape((2, depth, half), BF16), shape((width, rows), BF16), shape((1, half), F32)),
        "svvvvv",
        "avv",
        [pltpu.VMEM((2, depth, half), BF16), pltpu.SemaphoreType.DMA],
    )(core, req, pos, tsteps.reshape(1, requests), mod_table.transpose(1, 0, 2), gate_table)
    w_back = call(flip_kernel, shape((depth, 2 * inner), BF16), "vv", "v")(w_out, out_sib)
    gains = jnp.concatenate(
        [jnp.tile(qk_gain[0] * HD ** (-0.5), inner // HD), jnp.tile(qk_gain[1], inner // HD)]
    ).reshape(1, 2 * inner)
    text = jnp.pad(context[0], ((0, 0), (0, text_pad - text_len), (0, 0)))
    whole, w_sib, w_back, mod, gates, slot, gains, text = lax.optimization_barrier(
        (whole, w_sib, w_back, mod, gates, slot, gains, text)
    )

    send = call(
        project_kernel,
        shape((2, slots, kinds * inner), BF16),
        "saaaavv",
        "v",
        [
            pltpu.VMEM((parts, width, half), BF16),
            pltpu.VMEM((2, depth, half), BF16),
            pltpu.VMEM((depth, 2 * kinds * inner), BF16),
            pltpu.VMEM((depth, half), BF16),
            pltpu.SemaphoreType.DMA((2 + 2 * kinds,)),
        ],
        flops=4 * depth * half * kinds * inner,
    )(core, whole, mod, w_own, w_sib, gains, slot)
    arrived = lax.all_to_all(
        send.reshape(2 * requests, cap, kinds * inner), ("dp", "mp"), 0, 0, axis_index_groups=planes, tiled=True
    )
    attn = call(
        functools.partial(attend_kernel, text_len),
        shape((2 * slots, inner), BF16),
        "vv",
        "v",
        flops=16 * slots * (2 * slots + text_pad) * inner,
    )(arrived.reshape(2 * slots, kinds * inner), text)
    returned = lax.all_to_all(
        attn.reshape(2 * requests, cap, inner), ("dp", "mp"), 0, 0, axis_index_groups=planes, tiled=True
    )
    partial = call(
        output_kernel, shape((parts, width, half), BF16), "svvv", "v", flops=4 * depth * half * inner
    )(core, returned.reshape(2, slots, inner), slot, w_back.reshape(parts, width, 2 * inner))
    sums = lax.all_to_all(partial, "mp", 0, 0, tiled=True)
    return call(finish_kernel, shape((width, rows), BF16), "vvvv", "v")(sums, perm, gates, pos).T


def solution(mesh):
    return jax.shard_map(
        body,
        mesh=mesh,
        in_specs=(
            P("dp", "mp"),
            P("dp", None),
            P(),
            P(),
            P(None, None, "mp"),
            P(),
            P("dp", None, None, "mp"),
            P("mp", None),
        ),
        out_specs=P("dp", "mp"),
        check_vma=False,
    )
```

```python
import functools

import jax
import jax.numpy as jnp
from jax import lax
from jax.experimental import pallas as pl
from jax.experimental.pallas import tpu as pltpu
from jax.sharding import PartitionSpec as P

HD = 64
EPS = 1e-06
DEAD = 1e30
MASKED = -1e30
VMEM_LIMIT = 24 * 1024 * 1024
CHUNKS = 2
F32, BF16, I32 = jnp.float32, jnp.bfloat16, jnp.int32


PLACES = {
    "s": pl.BlockSpec(memory_space=pltpu.SMEM),
    "v": pl.BlockSpec(memory_space=pltpu.VMEM),
    "a": pl.BlockSpec(memory_space=pl.ANY),
}


def dot_nt(a, b):
    return lax.dot_general(a, b, (((1,), (1,)), ((), ())), preferred_element_type=F32)


def dot_tn(a, b):
    return lax.dot_general(a, b, (((0,), (0,)), ((), ())), preferred_element_type=F32)


def iota(shape, axis):
    return lax.broadcasted_iota(I32, shape, axis)


def as_column(row):
    n = row.shape[1]
    return jnp.sum(jnp.where(iota((n, n), 0) == iota((n, n), 1), row, 0.0), axis=1, keepdims=True)


def one_hot(flags):
    return jnp.where(flags, 1.0, 0.0).astype(BF16)


def dealt(rows):
    half = rows // 2
    place = iota((rows, rows), 0)
    return jnp.where(place < half, 2 * place, 2 * (place - half) + 1).astype(F32)


def spread_kernel(tok_hbm, req_hbm, out_hbm, perm_ref, pos_ref, tok_ref, req_ref, halves_ref, sems):
    width, rows = tok_ref.shape
    half = rows // 2
    parts = out_hbm.shape[0]
    reads = [pltpu.make_async_copy(req_hbm, req_ref, sems.at[0]), pltpu.make_async_copy(tok_hbm, tok_ref, sems.at[1])]
    for copy in reads:
        copy.start()
    reads[0].wait()
    req = req_ref[...].astype(F32)
    req_col = as_column(req)
    earlier = (req_col < req) | ((req_col == req) & (iota((rows, rows), 0) < iota((rows, rows), 1)))
    pos = jnp.sum(jnp.where(earlier, 1.0, 0.0), axis=0, keepdims=True)
    deal = one_hot(pos == dealt(rows))
    pos_ref[...] = pos
    reads[1].wait()
    perm = dot_nt(tok_ref[...], deal).astype(BF16)
    halves_ref[0] = perm[:, :half]
    halves_ref[1] = perm[:, half:]
    writes = [pltpu.make_async_copy(halves_ref.at[m % 2], out_hbm.at[m], sems.at[2 + m]) for m in range(parts)]
    for copy in writes:
        copy.start()
    perm_ref[...] = perm
    for copy in writes:
        copy.wait()


def prepare_kernel(
    cap, core_ref, req_ref, pos_ref, steps_ref, table_ref, gate_ref, mod_hbm, gates_ref, slot_ref, mod_ref, sem
):
    rows = req_ref.shape[1]
    half = rows // 2
    requests = steps_ref.shape[1]
    levels = table_ref.shape[1]
    is_first = core_ref[0] == 0
    req = req_ref[...].astype(F32)
    first = jnp.sum(jnp.where(as_column(req) < req, 1.0, 0.0), axis=0, keepdims=True)
    deal = one_hot(pos_ref[...] == dealt(rows))
    line = iota((8, rows), 0)
    both = jnp.where(line == 0, req, jnp.where(line == 1, first, 0.0)).astype(BF16)
    both = dot_nt(both, deal)
    req_s, first_s = both[0:1], both[1:2]
    index = iota((1, rows), 1)
    odd = jnp.where(index >= half, 1, 0)
    start = jnp.floor((first_s - odd.astype(F32) + 1.0) * 0.5)
    slot = req_s * cap + (index - half * odd).astype(F32) - start
    slot_ref[...] = jnp.where(is_first, slot[:, :half], slot[:, half:])
    chosen = one_hot(iota((requests, rows), 0).astype(F32) == req_s)
    steps = jnp.broadcast_to(steps_ref[...].astype(F32), (8, requests)).astype(BF16)
    step = jnp.dot(steps, chosen, preferred_element_type=F32)[0:1]
    pick = one_hot(iota((levels, rows), 0).astype(F32) == step)
    gates_ref[...] = dot_tn(gate_ref[...], pick).astype(BF16)
    pick = jnp.where(is_first, pick[:, :half].astype(F32), pick[:, half:].astype(F32)).astype(BF16)
    mod_ref[0] = dot_tn(table_ref[0], pick).astype(BF16)
    mod_ref[1] = dot_tn(table_ref[1], pick).astype(BF16)
    copy = pltpu.make_async_copy(mod_ref, mod_hbm, sem)
    copy.start()
    copy.wait()


def flip_kernel(own_ref, sib_ref, out_ref):
    inner, depth = own_ref.shape
    for start in range(0, depth, 128):
        for side, ref in enumerate((own_ref, sib_ref)):
            block = ref[:, start : start + 128].astype(F32).T
            out_ref[start : start + 128, side * inner : (side + 1) * inner] = block.astype(BF16)


def project_kernel(
    core_ref, tok_ref, mod_hbm, own_hbm, sib0_hbm, sib1_hbm, sib2_hbm, gain_ref, slot_ref,
    send_ref, mod_ref, w_ref, hid_ref, sems,
):
    parts, width, rows = tok_ref.shape
    depth = parts * width
    kinds, _, inner = own_hbm.shape
    span = kinds * inner
    chunk = depth // CHUNKS
    modulation = pltpu.make_async_copy(mod_hbm, mod_ref, sems.at[0])
    modulation.start()
    sources = [own_hbm.at[kind] for kind in range(kinds)] + [sib0_hbm, sib1_hbm, sib2_hbm]
    weights = []
    for step in range(CHUNKS):
        lines = pl.ds(step * chunk, chunk)
        weights.append(
            [
                pltpu.make_async_copy(
                    source.at[lines], w_ref.at[lines, pl.ds(i * inner, inner)], sems.at[1 + step * len(sources) + i]
                )
                for i, source in enumerate(sources)
            ]
        )
        for copy in weights[-1]:
            copy.start()
    hits = iota((send_ref.shape[1], rows), 0).astype(F32) == slot_ref[...]
    filled = jnp.sum(jnp.where(hits, 1.0, 0.0), axis=1, keepdims=True)
    mark = jnp.where(filled > 0.5, 0.0, DEAD)
    place = one_hot(hits)
    total = sum(jnp.sum(tok_ref[m].astype(F32), axis=0, keepdims=True) for m in range(parts))
    mean = total * (1.0 / depth)
    square = sum(jnp.sum(jnp.square(tok_ref[m].astype(F32) - mean), axis=0, keepdims=True) for m in range(parts))
    inverse = lax.rsqrt(square * (1.0 / depth) + EPS)
    modulation.wait()
    for m in range(0, parts, 2):
        pair = jnp.concatenate([tok_ref[m].astype(F32), tok_ref[m + 1].astype(F32)], axis=0)
        lines = pl.ds(m * width, 2 * width)
        shift, scale = mod_ref[0, lines, :].astype(F32), mod_ref[1, lines, :].astype(F32)
        hid_ref[lines, :] = ((pair - mean) * inverse * (1.0 + scale) + shift).astype(BF16)
    proj = None
    for step in range(CHUNKS):
        for copy in weights[step]:
            copy.wait()
        lines = pl.ds(step * chunk, chunk)
        part = dot_tn(hid_ref[lines, :], w_ref[lines, :])
        proj = part if proj is None else proj + part
    normed = 2 * inner
    heads = one_hot(iota((normed, normed), 0) // HD == iota((normed, normed), 1) // HD)
    for side, target in enumerate((core_ref[0], 1 - core_ref[0])):
        mixed = proj[:, side * span : (side + 1) * span]
        turned = mixed[:, :normed]
        power = jnp.square(turned)
        high = power.astype(BF16)
        low = (power - high.astype(F32)).astype(BF16)
        power = jnp.dot(high, heads, preferred_element_type=F32) + jnp.dot(low, heads, preferred_element_type=F32)
        turned = turned * lax.rsqrt(power * (1.0 / HD) + EPS) * gain_ref[...]
        packed = jnp.concatenate([turned, mixed[:, normed:]], axis=1).astype(BF16)
        send = jnp.dot(place, packed, preferred_element_type=F32)
        send = jnp.concatenate([send[:, :inner], send[:, inner:normed] + mark, send[:, normed:]], axis=1)
        send_ref[target] = send.astype(BF16)


def attend_kernel(text_len, slots_ref, ctx_ref, out_ref):
    slots, inner = out_ref.shape
    block = 256
    text_pad = ctx_ref.shape[1]
    queries = slots_ref[:, 0:inner]
    keys = slots_ref[:, inner : 2 * inner].astype(F32)
    dead = keys > 0.5 * DEAD
    marks = jnp.where(dead, 1.0, 0.0).astype(BF16)
    keys = jnp.concatenate([jnp.where(dead, 0.0, keys).astype(BF16), ctx_ref[0]], axis=0)
    own_bias = dot_nt(jnp.full((8, inner), MASKED, BF16), marks)[0:1]
    text_bias = jnp.where(iota((1, text_pad), 1) < text_len, 0.0, MASKED)
    bias = jnp.concatenate([own_bias, text_bias], axis=1)
    values = jnp.concatenate([slots_ref[:, 2 * inner :], ctx_ref[1]], axis=0)
    values = jnp.concatenate([values, jnp.ones(values.shape, BF16)], axis=1)
    first = iota((1, inner), 1) < HD
    zero = jnp.zeros((), BF16)
    for row in range(0, slots, block):
        query = queries[row : row + block]
        query = jnp.concatenate([jnp.where(first, query, zero), jnp.where(first, zero, query)], axis=0)
        scores = dot_nt(query, keys) + bias
        weights = jnp.exp(scores - jnp.max(scores, axis=1, keepdims=True)).astype(BF16)
        mixed = jnp.dot(weights, values, preferred_element_type=F32)
        mixed = mixed[:, :inner] / mixed[:, inner:]
        out_ref[row : row + block, :] = jnp.where(first, mixed[:block], mixed[block:]).astype(BF16)


def output_kernel(core_ref, back_ref, slot_ref, w_ref, part_ref):
    core = core_ref[0]
    slots, rows = back_ref.shape[1], slot_ref.shape[1]
    place_t = one_hot(iota((rows, slots), 1).astype(F32) == as_column(slot_ref[...]))
    own = jnp.dot(place_t, back_ref[core], preferred_element_type=F32).astype(BF16)
    sib = jnp.dot(place_t, back_ref[1 - core], preferred_element_type=F32).astype(BF16)
    attn = jnp.concatenate([own, sib], axis=1)
    for m in range(part_ref.shape[0]):
        part_ref[m] = dot_nt(w_ref[m], attn).astype(BF16)


def finish_kernel(sums_ref, perm_ref, gates_ref, pos_ref, out_ref):
    parts = sums_ref.shape[0]
    halves = [sum(sums_ref[m].astype(F32) for m in range(c, parts, 2)) for c in range(2)]
    total = jnp.concatenate(halves, axis=1)
    mixed = (perm_ref[...].astype(F32) + gates_ref[...].astype(F32) * total).astype(BF16)
    rows = perm_ref.shape[1]
    deal = one_hot(pos_ref[...] == dealt(rows))
    out_ref[...] = jnp.dot(mixed, deal, preferred_element_type=F32).astype(BF16)


def call(kernel, out_shape, specs, out_specs, scratch=(), flops=0):
    return pl.pallas_call(
        kernel,
        out_shape=out_shape,
        in_specs=[PLACES[letter] for letter in specs],
        out_specs=tuple(PLACES[letter] for letter in out_specs) if len(out_specs) > 1 else PLACES[out_specs],
        scratch_shapes=list(scratch),
        compiler_params=pltpu.CompilerParams(vmem_limit_bytes=VMEM_LIMIT),
        cost_estimate=pl.CostEstimate(flops=flops, bytes_accessed=1 << 20, transcendentals=0),
    )


def body(tokens, route, tsteps, mod_table, w_qkv, qk_gain, context, w_out):
    rows, width = tokens.shape
    half = rows // 2
    requests = lax.axis_size("dp")
    parts = lax.axis_size("mp")
    chips = parts // 2
    cap = max(2, 2 * rows // requests) // 2
    slots = requests * cap
    depth, kinds, inner = w_qkv.shape
    text_len = context.shape[2]
    text_pad = -(-text_len // 128) * 128
    sibling = [(i, i ^ 1) for i in range(parts)]
    planes = [[dp * parts + 2 * z + c for c in range(2) for dp in range(requests)] for z in range(chips)]
    core = lax.rem(lax.axis_index("mp"), 2).astype(I32).reshape(1)
    shape = jax.ShapeDtypeStruct

    req = route.reshape(1, rows)
    def in_hbm(x):
        return pltpu.with_memory_space_constraint(x, pltpu.HBM)

    spread, perm, pos = call(
        spread_kernel,
        (pltpu.HBM((parts, width, half), BF16), shape((width, rows), BF16), shape((1, rows), F32)),
        "aa",
        "avv",
        [
            pltpu.VMEM((width, rows), BF16),
            pltpu.VMEM((1, rows), I32),
            pltpu.VMEM((2, width, half), BF16),
            pltpu.SemaphoreType.DMA((2 + parts,)),
        ],
    )(in_hbm(tokens.T), in_hbm(req))
    spread, w_qkv, w_out = lax.optimization_barrier((spread, w_qkv, w_out))
    whole = lax.all_to_all(spread, "mp", 0, 0, tiled=True)

    w_own = w_qkv.transpose(1, 0, 2)
    w_sib = [lax.ppermute(w_own[kind], "mp", sibling) for kind in range(kinds)]
    out_sib = lax.ppermute(w_out, "mp", sibling)
    gate_table = lax.dynamic_slice_in_dim(mod_table[:, 2, :], lax.axis_index("mp") * width, width, 1)
    mod, gates, slot = call(
        functools.partial(prepare_kernel, cap),
        (pltpu.HBM((2, depth, half), BF16), shape((width, rows), BF16), shape((1, half), F32)),
        "svvvvv",
        "avv",
        [pltpu.VMEM((2, depth, half), BF16), pltpu.SemaphoreType.DMA],
    )(core, req, pos, tsteps.reshape(1, requests), mod_table.transpose(1, 0, 2), gate_table)
    w_back = call(flip_kernel, shape((depth, 2 * inner), BF16), "vv", "v")(w_out, out_sib)
    gains = jnp.concatenate(
        [jnp.tile(qk_gain[0] * HD ** (-0.5), inner // HD), jnp.tile(qk_gain[1], inner // HD)]
    ).reshape(1, 2 * inner)
    text = jnp.pad(context[0], ((0, 0), (0, text_pad - text_len), (0, 0)))
    whole, w_sib, w_back, mod, gates, slot, gains, text = lax.optimization_barrier(
        (whole, w_sib, w_back, mod, gates, slot, gains, text)
    )

    send = call(
        project_kernel,
        shape((2, slots, kinds * inner), BF16),
        "svaaaaavv",
        "v",
        [
            pltpu.VMEM((2, depth, half), BF16),
            pltpu.VMEM((depth, 2 * kinds * inner), BF16),
            pltpu.VMEM((depth, half), BF16),
            pltpu.SemaphoreType.DMA((1 + 2 * kinds * CHUNKS,)),
        ],
        flops=4 * depth * half * kinds * inner,
    )(core, whole, in_hbm(mod), in_hbm(w_own), *[in_hbm(w) for w in w_sib], gains, slot)
    arrived = lax.all_to_all(
        send.reshape(2 * requests, cap, kinds * inner), ("dp", "mp"), 0, 0, axis_index_groups=planes, tiled=True
    )
    attn = call(
        functools.partial(attend_kernel, text_len),
        shape((2 * slots, inner), BF16),
        "vv",
        "v",
        flops=16 * slots * (2 * slots + text_pad) * inner,
    )(arrived.reshape(2 * slots, kinds * inner), text)
    returned = lax.all_to_all(
        attn.reshape(2 * requests, cap, inner), ("dp", "mp"), 0, 0, axis_index_groups=planes, tiled=True
    )
    partial = call(
        output_kernel, shape((parts, width, half), BF16), "svvv", "v", flops=4 * depth * half * inner
    )(core, returned.reshape(2, slots, inner), slot, w_back.reshape(parts, width, 2 * inner))
    sums = lax.all_to_all(partial, "mp", 0, 0, tiled=True)
    return call(finish_kernel, shape((width, rows), BF16), "vvvv", "v")(sums, perm, gates, pos).T


def solution(mesh):
    return jax.shard_map(
        body,
        mesh=mesh,
        in_specs=(
            P("dp", "mp"),
            P("dp", None),
            P(),
            P(),
            P(None, None, "mp"),
            P(),
            P("dp", None, None, "mp"),
            P("mp", None),
        ),
        out_specs=P("dp", "mp"),
        check_vma=False,
    )
```

```python
import functools

import jax
import jax.numpy as jnp
from jax import lax
from jax.experimental import pallas as pl
from jax.experimental.pallas import tpu as pltpu
from jax.sharding import PartitionSpec as P

HD = 64
EPS = 1e-06
DEAD = 1e30
MASKED = -1e30
VMEM_LIMIT = 24 * 1024 * 1024
F32, BF16, I32 = jnp.float32, jnp.bfloat16, jnp.int32


PLACES = {
    "s": pl.BlockSpec(memory_space=pltpu.SMEM),
    "v": pl.BlockSpec(memory_space=pltpu.VMEM),
    "a": pl.BlockSpec(memory_space=pl.ANY),
}


def dot_nt(a, b):
    return lax.dot_general(a, b, (((1,), (1,)), ((), ())), preferred_element_type=F32)


def dot_tn(a, b):
    return lax.dot_general(a, b, (((0,), (0,)), ((), ())), preferred_element_type=F32)


def iota(shape, axis):
    return lax.broadcasted_iota(I32, shape, axis)


def as_column(row):
    n = row.shape[1]
    return jnp.sum(jnp.where(iota((n, n), 0) == iota((n, n), 1), row, 0.0), axis=1, keepdims=True)


def one_hot(flags):
    return jnp.where(flags, 1.0, 0.0).astype(BF16)


def dealt(rows):
    half = rows // 2
    place = iota((rows, rows), 0)
    return jnp.where(place < half, 2 * place, 2 * (place - half) + 1).astype(F32)


def spread_kernel(tok_hbm, req_hbm, out_hbm, perm_ref, pos_ref, tok_ref, req_ref, halves_ref, sems):
    width, rows = tok_ref.shape
    half = rows // 2
    parts = out_hbm.shape[0]
    reads = [pltpu.make_async_copy(req_hbm, req_ref, sems.at[0]), pltpu.make_async_copy(tok_hbm, tok_ref, sems.at[1])]
    for copy in reads:
        copy.start()
    reads[0].wait()
    req = req_ref[...].astype(F32)
    req_col = as_column(req)
    earlier = (req_col < req) | ((req_col == req) & (iota((rows, rows), 0) < iota((rows, rows), 1)))
    pos = jnp.sum(jnp.where(earlier, 1.0, 0.0), axis=0, keepdims=True)
    deal = one_hot(pos == dealt(rows))
    pos_ref[...] = pos
    reads[1].wait()
    perm = dot_nt(tok_ref[...], deal).astype(BF16)
    halves_ref[0] = perm[:, :half]
    halves_ref[1] = perm[:, half:]
    writes = [pltpu.make_async_copy(halves_ref.at[m % 2], out_hbm.at[m], sems.at[2 + m]) for m in range(parts)]
    for copy in writes:
        copy.start()
    perm_ref[...] = perm
    for copy in writes:
        copy.wait()


def prepare_kernel(
    cap, core_ref, req_ref, pos_ref, steps_ref, table_ref, gate_ref, mod_ref, gates_ref, slot_ref
):
    rows = req_ref.shape[1]
    half = rows // 2
    requests = steps_ref.shape[1]
    levels = table_ref.shape[1]
    is_first = core_ref[0] == 0
    req = req_ref[...].astype(F32)
    first = jnp.sum(jnp.where(as_column(req) < req, 1.0, 0.0), axis=0, keepdims=True)
    deal = one_hot(pos_ref[...] == dealt(rows))
    line = iota((8, rows), 0)
    both = jnp.where(line == 0, req, jnp.where(line == 1, first, 0.0)).astype(BF16)
    both = dot_nt(both, deal)
    req_s, first_s = both[0:1], both[1:2]
    index = iota((1, rows), 1)
    odd = jnp.where(index >= half, 1, 0)
    start = jnp.floor((first_s - odd.astype(F32) + 1.0) * 0.5)
    slot = req_s * cap + (index - half * odd).astype(F32) - start
    slot_ref[...] = jnp.where(is_first, slot[:, :half], slot[:, half:])
    chosen = one_hot(iota((requests, rows), 0).astype(F32) == req_s)
    steps = jnp.broadcast_to(steps_ref[...].astype(F32), (8, requests)).astype(BF16)
    step = jnp.dot(steps, chosen, preferred_element_type=F32)[0:1]
    pick = one_hot(iota((levels, rows), 0).astype(F32) == step)
    gates_ref[...] = dot_tn(gate_ref[...], pick).astype(BF16)
    pick = jnp.where(is_first, pick[:, :half].astype(F32), pick[:, half:].astype(F32)).astype(BF16)
    mod_ref[0] = dot_tn(table_ref[0], pick).astype(BF16)
    mod_ref[1] = dot_tn(table_ref[1], pick).astype(BF16)


def flip_kernel(own_ref, sib_ref, out_hbm, out_ref, sem):
    inner, depth = own_ref.shape
    for start in range(0, depth, 128):
        for side, ref in enumerate((own_ref, sib_ref)):
            block = ref[:, start : start + 128].astype(F32).T
            out_ref[start : start + 128, side * inner : (side + 1) * inner] = block.astype(BF16)
    copy = pltpu.make_async_copy(out_ref, out_hbm, sem)
    copy.start()
    copy.wait()


def project_kernel(
    core_ref, tok_ref, mod_ref, own0_ref, own1_ref, own2_hbm, sib0_hbm, sib1_hbm, sib2_hbm, gain_ref, slot_ref,
    send_ref, w_ref, hid_ref, sems,
):
    parts, width, rows = tok_ref.shape
    depth = parts * width
    inner = own0_ref.shape[1]
    kinds = 3
    span = kinds * inner
    weights = [
        pltpu.make_async_copy(source, w_ref.at[:, pl.ds(i * inner, inner)], sems.at[i])
        for i, source in enumerate((own2_hbm, sib0_hbm, sib1_hbm, sib2_hbm))
    ]
    for copy in weights:
        copy.start()
    hits = iota((send_ref.shape[1], rows), 0).astype(F32) == slot_ref[...]
    filled = jnp.sum(jnp.where(hits, 1.0, 0.0), axis=1, keepdims=True)
    mark = jnp.where(filled > 0.5, 0.0, DEAD)
    place = one_hot(hits)
    total = sum(jnp.sum(tok_ref[m].astype(F32), axis=0, keepdims=True) for m in range(parts))
    mean = total * (1.0 / depth)
    square = sum(jnp.sum(jnp.square(tok_ref[m].astype(F32) - mean), axis=0, keepdims=True) for m in range(parts))
    inverse = lax.rsqrt(square * (1.0 / depth) + EPS)
    for m in range(0, parts, 2):
        pair = jnp.concatenate([tok_ref[m].astype(F32), tok_ref[m + 1].astype(F32)], axis=0)
        lines = pl.ds(m * width, 2 * width)
        shift, scale = mod_ref[0, lines, :].astype(F32), mod_ref[1, lines, :].astype(F32)
        hid_ref[lines, :] = ((pair - mean) * inverse * (1.0 + scale) + shift).astype(BF16)
    hidden = hid_ref[...]
    start = dot_tn(hidden, jnp.concatenate([own0_ref[...], own1_ref[...]], axis=1))
    for copy in weights:
        copy.wait()
    proj = jnp.concatenate([start, dot_tn(hidden, w_ref[...])], axis=1)
    normed = 2 * inner
    heads = one_hot(iota((normed, normed), 0) // HD == iota((normed, normed), 1) // HD)
    for side, target in enumerate((core_ref[0], 1 - core_ref[0])):
        mixed = proj[:, side * span : (side + 1) * span]
        turned = mixed[:, :normed]
        power = jnp.square(turned)
        high = power.astype(BF16)
        low = (power - high.astype(F32)).astype(BF16)
        power = jnp.dot(high, heads, preferred_element_type=F32) + jnp.dot(low, heads, preferred_element_type=F32)
        turned = turned * lax.rsqrt(power * (1.0 / HD) + EPS) * gain_ref[...]
        packed = jnp.concatenate([turned, mixed[:, normed:]], axis=1).astype(BF16)
        send = jnp.dot(place, packed, preferred_element_type=F32)
        send = jnp.concatenate([send[:, :inner], send[:, inner:normed] + mark, send[:, normed:]], axis=1)
        send_ref[target] = send.astype(BF16)


def attend_kernel(text_len, slots_ref, ctx_ref, out_ref):
    slots, inner = out_ref.shape
    block = 256
    text_pad = ctx_ref.shape[1]
    queries = slots_ref[:, 0:inner]
    keys = slots_ref[:, inner : 2 * inner].astype(F32)
    dead = keys > 0.5 * DEAD
    marks = jnp.where(dead, 1.0, 0.0).astype(BF16)
    keys = jnp.concatenate([jnp.where(dead, 0.0, keys).astype(BF16), ctx_ref[0]], axis=0)
    own_bias = dot_nt(jnp.full((8, inner), MASKED, BF16), marks)[0:1]
    text_bias = jnp.where(iota((1, text_pad), 1) < text_len, 0.0, MASKED)
    bias = jnp.concatenate([own_bias, text_bias], axis=1)
    values = jnp.concatenate([slots_ref[:, 2 * inner :], ctx_ref[1]], axis=0)
    values = jnp.concatenate([values, jnp.ones(values.shape, BF16)], axis=1)
    first = iota((1, inner), 1) < HD
    zero = jnp.zeros((), BF16)
    for row in range(0, slots, block):
        query = queries[row : row + block]
        query = jnp.concatenate([jnp.where(first, query, zero), jnp.where(first, zero, query)], axis=0)
        scores = dot_nt(query, keys) + bias
        weights = jnp.exp(scores - jnp.max(scores, axis=1, keepdims=True)).astype(BF16)
        mixed = jnp.dot(weights, values, preferred_element_type=F32)
        mixed = mixed[:, :inner] / mixed[:, inner:]
        out_ref[row : row + block, :] = jnp.where(first, mixed[:block], mixed[block:]).astype(BF16)


def output_kernel(core_ref, back_ref, slot_ref, w_ref, part_ref):
    core = core_ref[0]
    slots, rows = back_ref.shape[1], slot_ref.shape[1]
    place_t = one_hot(iota((rows, slots), 1).astype(F32) == as_column(slot_ref[...]))
    own = jnp.dot(place_t, back_ref[core], preferred_element_type=F32).astype(BF16)
    sib = jnp.dot(place_t, back_ref[1 - core], preferred_element_type=F32).astype(BF16)
    attn = jnp.concatenate([own, sib], axis=1)
    for m in range(part_ref.shape[0]):
        part_ref[m] = dot_nt(w_ref[m], attn).astype(BF16)


def finish_kernel(sums_ref, perm_ref, gates_ref, pos_ref, out_ref):
    parts = sums_ref.shape[0]
    halves = [sum(sums_ref[m].astype(F32) for m in range(c, parts, 2)) for c in range(2)]
    total = jnp.concatenate(halves, axis=1)
    mixed = (perm_ref[...].astype(F32) + gates_ref[...].astype(F32) * total).astype(BF16)
    rows = perm_ref.shape[1]
    deal = one_hot(pos_ref[...] == dealt(rows))
    out_ref[...] = jnp.dot(mixed, deal, preferred_element_type=F32).astype(BF16)


def call(kernel, out_shape, specs, out_specs, scratch=(), flops=0):
    return pl.pallas_call(
        kernel,
        out_shape=out_shape,
        in_specs=[PLACES[letter] for letter in specs],
        out_specs=tuple(PLACES[letter] for letter in out_specs) if len(out_specs) > 1 else PLACES[out_specs],
        scratch_shapes=list(scratch),
        compiler_params=pltpu.CompilerParams(vmem_limit_bytes=VMEM_LIMIT),
        cost_estimate=pl.CostEstimate(flops=flops, bytes_accessed=1 << 20, transcendentals=0),
    )


def body(tokens, route, tsteps, mod_table, w_qkv, qk_gain, context, w_out):
    rows, width = tokens.shape
    half = rows // 2
    requests = lax.axis_size("dp")
    parts = lax.axis_size("mp")
    chips = parts // 2
    cap = max(2, 2 * rows // requests) // 2
    slots = requests * cap
    depth, kinds, inner = w_qkv.shape
    text_len = context.shape[2]
    text_pad = -(-text_len // 128) * 128
    sibling = [(i, i ^ 1) for i in range(parts)]
    planes = [[dp * parts + 2 * z + c for c in range(2) for dp in range(requests)] for z in range(chips)]
    core = lax.rem(lax.axis_index("mp"), 2).astype(I32).reshape(1)
    shape = jax.ShapeDtypeStruct

    req = route.reshape(1, rows)
    def in_hbm(x):
        return pltpu.with_memory_space_constraint(x, pltpu.HBM)

    def in_vmem(x):
        return pltpu.with_memory_space_constraint(x, pltpu.VMEM)

    spread, perm, pos = call(
        spread_kernel,
        (pltpu.HBM((parts, width, half), BF16), shape((width, rows), BF16), shape((1, rows), F32)),
        "aa",
        "avv",
        [
            pltpu.VMEM((width, rows), BF16),
            pltpu.VMEM((1, rows), I32),
            pltpu.VMEM((2, width, half), BF16),
            pltpu.SemaphoreType.DMA((2 + parts,)),
        ],
    )(in_hbm(tokens.T), in_hbm(req))
    spread, w_qkv, w_out = lax.optimization_barrier((spread, w_qkv, w_out))
    whole = lax.all_to_all(spread, "mp", 0, 0, tiled=True)

    w_own = [w_qkv[:, kind] for kind in range(kinds)]
    w_sib = [lax.ppermute(block, "mp", sibling) for block in w_own]
    out_sib = lax.ppermute(w_out, "mp", sibling)
    gate_table = lax.dynamic_slice_in_dim(mod_table[:, 2, :], lax.axis_index("mp") * width, width, 1)
    mod, gates, slot = call(
        functools.partial(prepare_kernel, cap),
        (pltpu.VMEM((2, depth, half), BF16), shape((width, rows), BF16), shape((1, half), F32)),
        "svvvvv",
        "vvv",
    )(core, req, pos, tsteps.reshape(1, requests), mod_table.transpose(1, 0, 2), gate_table)
    w_back = call(
        flip_kernel,
        pltpu.HBM((depth, 2 * inner), BF16),
        "vv",
        "a",
        [pltpu.VMEM((depth, 2 * inner), BF16), pltpu.SemaphoreType.DMA],
    )(w_out, out_sib)
    gains = jnp.concatenate(
        [jnp.tile(qk_gain[0] * HD ** (-0.5), inner // HD), jnp.tile(qk_gain[1], inner // HD)]
    ).reshape(1, 2 * inner)
    text = jnp.pad(context[0], ((0, 0), (0, text_pad - text_len), (0, 0)))
    whole, w_own, w_sib, w_back, mod, gates, slot, gains, text = lax.optimization_barrier(
        (whole, w_own, w_sib, w_back, mod, gates, slot, gains, text)
    )

    send = call(
        project_kernel,
        shape((2, slots, kinds * inner), BF16),
        "svvvvaaaavv",
        "v",
        [
            pltpu.VMEM((depth, 4 * inner), BF16),
            pltpu.VMEM((depth, half), BF16),
            pltpu.SemaphoreType.DMA((4,)),
        ],
        flops=4 * depth * half * kinds * inner,
    )(core, whole, in_vmem(mod), *[in_vmem(w) for w in w_own[:2]], *[in_hbm(w) for w in w_own[2:] + w_sib], gains, slot)
    arrived = lax.all_to_all(
        send.reshape(2 * requests, cap, kinds * inner), ("dp", "mp"), 0, 0, axis_index_groups=planes, tiled=True
    )
    attn = call(
        functools.partial(attend_kernel, text_len),
        shape((2 * slots, inner), BF16),
        "vv",
        "v",
        flops=16 * slots * (2 * slots + text_pad) * inner,
    )(arrived.reshape(2 * slots, kinds * inner), text)
    returned = lax.all_to_all(
        attn.reshape(2 * requests, cap, inner), ("dp", "mp"), 0, 0, axis_index_groups=planes, tiled=True
    )
    partial = call(
        output_kernel, shape((parts, width, half), BF16), "svvv", "v", flops=4 * depth * half * inner
    )(core, returned.reshape(2, slots, inner), slot, w_back.reshape(parts, width, 2 * inner))
    sums = lax.all_to_all(partial, "mp", 0, 0, tiled=True)
    return call(finish_kernel, shape((width, rows), BF16), "vvvv", "v")(sums, perm, gates, pos).T


def solution(mesh):
    return jax.shard_map(
        body,
        mesh=mesh,
        in_specs=(
            P("dp", "mp"),
            P("dp", None),
            P(),
            P(),
            P(None, None, "mp"),
            P(),
            P("dp", None, None, "mp"),
            P("mp", None),
        ),
        out_specs=P("dp", "mp"),
        check_vma=False,
    )
```

```python
import functools

import jax
import jax.numpy as jnp
from jax import lax
from jax.experimental import pallas as pl
from jax.experimental.pallas import tpu as pltpu
from jax.sharding import PartitionSpec as P

HD = 64
EPS = 1e-06
DEAD = 1e30
MASKED = -1e30
VMEM_LIMIT = 24 * 1024 * 1024
F32, BF16, I32 = jnp.float32, jnp.bfloat16, jnp.int32


PLACES = {
    "s": pl.BlockSpec(memory_space=pltpu.SMEM),
    "v": pl.BlockSpec(memory_space=pltpu.VMEM),
    "a": pl.BlockSpec(memory_space=pl.ANY),
}


def dot_nt(a, b):
    return lax.dot_general(a, b, (((1,), (1,)), ((), ())), preferred_element_type=F32)


def dot_tn(a, b):
    return lax.dot_general(a, b, (((0,), (0,)), ((), ())), preferred_element_type=F32)


def iota(shape, axis):
    return lax.broadcasted_iota(I32, shape, axis)


def as_column(row):
    n = row.shape[1]
    return jnp.sum(jnp.where(iota((n, n), 0) == iota((n, n), 1), row, 0.0), axis=1, keepdims=True)


def one_hot(flags):
    return jnp.where(flags, 1.0, 0.0).astype(BF16)


def dealt(rows):
    half = rows // 2
    place = iota((rows, rows), 0)
    return jnp.where(place < half, 2 * place, 2 * (place - half) + 1).astype(F32)


def spread_kernel(tok_hbm, req_hbm, out_hbm, perm_ref, pos_ref, tok_ref, req_ref, halves_ref, sems):
    width, rows = tok_ref.shape
    half = rows // 2
    parts = out_hbm.shape[0]
    reads = [pltpu.make_async_copy(req_hbm, req_ref, sems.at[0]), pltpu.make_async_copy(tok_hbm, tok_ref, sems.at[1])]
    for copy in reads:
        copy.start()
    reads[0].wait()
    req = req_ref[...].astype(F32)
    req_col = as_column(req)
    earlier = (req_col < req) | ((req_col == req) & (iota((rows, rows), 0) < iota((rows, rows), 1)))
    pos = jnp.sum(jnp.where(earlier, 1.0, 0.0), axis=0, keepdims=True)
    deal = one_hot(pos == dealt(rows))
    pos_ref[...] = pos
    reads[1].wait()
    perm = dot_nt(tok_ref[...], deal).astype(BF16)
    halves_ref[0] = perm[:, :half]
    halves_ref[1] = perm[:, half:]
    writes = [pltpu.make_async_copy(halves_ref.at[m % 2], out_hbm.at[m], sems.at[2 + m]) for m in range(parts)]
    for copy in writes:
        copy.start()
    perm_ref[...] = perm
    for copy in writes:
        copy.wait()


def prepare_kernel(
    cap, core_ref, req_ref, pos_ref, steps_ref, table_ref, gate_ref, mod_hbm, gates_ref, slot_ref, mod_ref, sem
):
    rows = req_ref.shape[1]
    half = rows // 2
    requests = steps_ref.shape[1]
    levels = table_ref.shape[1]
    is_first = core_ref[0] == 0
    req = req_ref[...].astype(F32)
    first = jnp.sum(jnp.where(as_column(req) < req, 1.0, 0.0), axis=0, keepdims=True)
    deal = one_hot(pos_ref[...] == dealt(rows))
    line = iota((8, rows), 0)
    both = jnp.where(line == 0, req, jnp.where(line == 1, first, 0.0)).astype(BF16)
    both = dot_nt(both, deal)
    req_s, first_s = both[0:1], both[1:2]
    index = iota((1, rows), 1)
    odd = jnp.where(index >= half, 1, 0)
    start = jnp.floor((first_s - odd.astype(F32) + 1.0) * 0.5)
    slot = req_s * cap + (index - half * odd).astype(F32) - start
    slot_ref[...] = jnp.where(is_first, slot[:, :half], slot[:, half:])
    chosen = one_hot(iota((requests, rows), 0).astype(F32) == req_s)
    steps = jnp.broadcast_to(steps_ref[...].astype(F32), (8, requests)).astype(BF16)
    step = jnp.dot(steps, chosen, preferred_element_type=F32)[0:1]
    pick = one_hot(iota((levels, rows), 0).astype(F32) == step)
    gates_ref[...] = dot_tn(gate_ref[...], pick).astype(BF16)
    pick = jnp.where(is_first, pick[:, :half].astype(F32), pick[:, half:].astype(F32)).astype(BF16)
    mod_ref[0] = dot_tn(table_ref[0], pick).astype(BF16)
    mod_ref[1] = dot_tn(table_ref[1], pick).astype(BF16)
    copy = pltpu.make_async_copy(mod_ref, mod_hbm, sem)
    copy.start()
    copy.wait()


def flip_kernel(own_ref, sib_ref, out_ref):
    inner, depth = own_ref.shape
    for start in range(0, depth, 128):
        for side, ref in enumerate((own_ref, sib_ref)):
            block = ref[:, start : start + 128].astype(F32).T
            out_ref[start : start + 128, side * inner : (side + 1) * inner] = block.astype(BF16)


def project_kernel(
    core_ref, tok_ref, mod_hbm, own_hbm, sib0_hbm, sib1_hbm, sib2_hbm, gain_ref, slot_ref,
    send_ref, mod_ref, w_ref, hid_ref, sems,
):
    parts, width, rows = tok_ref.shape
    depth = parts * width
    kinds, _, inner = own_hbm.shape
    modulation = pltpu.make_async_copy(mod_hbm, mod_ref, sems.at[0])
    modulation.start()
    sources = [own_hbm.at[kind] for kind in range(kinds)] + [sib0_hbm, sib1_hbm, sib2_hbm]
    weights = [
        pltpu.make_async_copy(source, w_ref.at[i // kinds, :, pl.ds(i % kinds * inner, inner)], sems.at[1 + i])
        for i, source in enumerate(sources)
    ]
    for copy in weights:
        copy.start()
    hits = iota((send_ref.shape[1], rows), 0).astype(F32) == slot_ref[...]
    filled = jnp.sum(jnp.where(hits, 1.0, 0.0), axis=1, keepdims=True)
    mark = jnp.where(filled > 0.5, 0.0, DEAD)
    place = one_hot(hits)
    total = sum(jnp.sum(tok_ref[m].astype(F32), axis=0, keepdims=True) for m in range(parts))
    mean = total * (1.0 / depth)
    square = sum(jnp.sum(jnp.square(tok_ref[m].astype(F32) - mean), axis=0, keepdims=True) for m in range(parts))
    inverse = lax.rsqrt(square * (1.0 / depth) + EPS)
    modulation.wait()
    for m in range(0, parts, 2):
        pair = jnp.concatenate([tok_ref[m].astype(F32), tok_ref[m + 1].astype(F32)], axis=0)
        lines = pl.ds(m * width, 2 * width)
        shift, scale = mod_ref[0, lines, :].astype(F32), mod_ref[1, lines, :].astype(F32)
        hid_ref[lines, :] = ((pair - mean) * inverse * (1.0 + scale) + shift).astype(BF16)
    hidden = hid_ref[...].astype(F32).T.astype(BF16)
    normed = 2 * inner
    heads = one_hot(iota((normed, normed), 0) // HD == iota((normed, normed), 1) // HD)
    projected = []
    for side in range(2):
        for copy in weights[side * kinds : (side + 1) * kinds]:
            copy.wait()
        projected.append(jnp.dot(hidden, w_ref[side], preferred_element_type=F32))
    for mixed, target in zip(projected, (core_ref[0], 1 - core_ref[0])):
        turned = mixed[:, :normed]
        power = jnp.square(turned)
        high = power.astype(BF16)
        low = (power - high.astype(F32)).astype(BF16)
        power = jnp.dot(high, heads, preferred_element_type=F32) + jnp.dot(low, heads, preferred_element_type=F32)
        turned = turned * lax.rsqrt(power * (1.0 / HD) + EPS) * gain_ref[...]
        packed = jnp.concatenate([turned, mixed[:, normed:]], axis=1).astype(BF16)
        send = jnp.dot(place, packed, preferred_element_type=F32)
        send = jnp.concatenate([send[:, :inner], send[:, inner:normed] + mark, send[:, normed:]], axis=1)
        send_ref[target] = send.astype(BF16)


def attend_kernel(text_len, slots_ref, ctx_ref, out_ref):
    slots, inner = out_ref.shape
    block = 256
    text_pad = ctx_ref.shape[1]
    queries = slots_ref[:, 0:inner]
    keys = slots_ref[:, inner : 2 * inner].astype(F32)
    dead = keys > 0.5 * DEAD
    marks = jnp.where(dead, 1.0, 0.0).astype(BF16)
    keys = jnp.concatenate([jnp.where(dead, 0.0, keys).astype(BF16), ctx_ref[0]], axis=0)
    own_bias = dot_nt(jnp.full((8, inner), MASKED, BF16), marks)[0:1]
    text_bias = jnp.where(iota((1, text_pad), 1) < text_len, 0.0, MASKED)
    bias = jnp.concatenate([own_bias, text_bias], axis=1)
    values = jnp.concatenate([slots_ref[:, 2 * inner :], ctx_ref[1]], axis=0)
    values = jnp.concatenate([values, jnp.ones(values.shape, BF16)], axis=1)
    first = iota((1, inner), 1) < HD
    zero = jnp.zeros((), BF16)
    for row in range(0, slots, block):
        query = queries[row : row + block]
        query = jnp.concatenate([jnp.where(first, query, zero), jnp.where(first, zero, query)], axis=0)
        scores = dot_nt(query, keys) + bias
        weights = jnp.exp(scores - jnp.max(scores, axis=1, keepdims=True)).astype(BF16)
        mixed = jnp.dot(weights, values, preferred_element_type=F32)
        mixed = mixed[:, :inner] / mixed[:, inner:]
        out_ref[row : row + block, :] = jnp.where(first, mixed[:block], mixed[block:]).astype(BF16)


def output_kernel(core_ref, back_ref, slot_ref, w_ref, part_ref):
    core = core_ref[0]
    slots, rows = back_ref.shape[1], slot_ref.shape[1]
    place_t = one_hot(iota((rows, slots), 1).astype(F32) == as_column(slot_ref[...]))
    own = jnp.dot(place_t, back_ref[core], preferred_element_type=F32).astype(BF16)
    sib = jnp.dot(place_t, back_ref[1 - core], preferred_element_type=F32).astype(BF16)
    attn = jnp.concatenate([own, sib], axis=1)
    for m in range(part_ref.shape[0]):
        part_ref[m] = dot_nt(w_ref[m], attn).astype(BF16)


def finish_kernel(sums_ref, perm_ref, gates_ref, pos_ref, out_ref):
    parts = sums_ref.shape[0]
    halves = [sum(sums_ref[m].astype(F32) for m in range(c, parts, 2)) for c in range(2)]
    total = jnp.concatenate(halves, axis=1)
    mixed = (perm_ref[...].astype(F32) + gates_ref[...].astype(F32) * total).astype(BF16)
    rows = perm_ref.shape[1]
    deal = one_hot(pos_ref[...] == dealt(rows))
    out_ref[...] = jnp.dot(mixed, deal, preferred_element_type=F32).astype(BF16)


def call(kernel, out_shape, specs, out_specs, scratch=(), flops=0):
    return pl.pallas_call(
        kernel,
        out_shape=out_shape,
        in_specs=[PLACES[letter] for letter in specs],
        out_specs=tuple(PLACES[letter] for letter in out_specs) if len(out_specs) > 1 else PLACES[out_specs],
        scratch_shapes=list(scratch),
        compiler_params=pltpu.CompilerParams(vmem_limit_bytes=VMEM_LIMIT),
        cost_estimate=pl.CostEstimate(flops=flops, bytes_accessed=1 << 20, transcendentals=0),
    )


def body(tokens, route, tsteps, mod_table, w_qkv, qk_gain, context, w_out):
    rows, width = tokens.shape
    half = rows // 2
    requests = lax.axis_size("dp")
    parts = lax.axis_size("mp")
    chips = parts // 2
    cap = max(2, 2 * rows // requests) // 2
    slots = requests * cap
    depth, kinds, inner = w_qkv.shape
    text_len = context.shape[2]
    text_pad = -(-text_len // 128) * 128
    sibling = [(i, i ^ 1) for i in range(parts)]
    planes = [[dp * parts + 2 * z + c for c in range(2) for dp in range(requests)] for z in range(chips)]
    core = lax.rem(lax.axis_index("mp"), 2).astype(I32).reshape(1)
    shape = jax.ShapeDtypeStruct

    req = route.reshape(1, rows)
    def in_hbm(x):
        return pltpu.with_memory_space_constraint(x, pltpu.HBM)

    spread, perm, pos = call(
        spread_kernel,
        (pltpu.HBM((parts, width, half), BF16), shape((width, rows), BF16), shape((1, rows), F32)),
        "aa",
        "avv",
        [
            pltpu.VMEM((width, rows), BF16),
            pltpu.VMEM((1, rows), I32),
            pltpu.VMEM((2, width, half), BF16),
            pltpu.SemaphoreType.DMA((2 + parts,)),
        ],
    )(in_hbm(tokens.T), in_hbm(req))
    spread, w_qkv, w_out = lax.optimization_barrier((spread, w_qkv, w_out))
    whole = lax.all_to_all(spread, "mp", 0, 0, tiled=True)

    w_own = w_qkv.transpose(1, 0, 2)
    w_sib = [lax.ppermute(w_own[kind], "mp", sibling) for kind in range(kinds)]
    out_sib = lax.ppermute(w_out, "mp", sibling)
    gate_table = lax.dynamic_slice_in_dim(mod_table[:, 2, :], lax.axis_index("mp") * width, width, 1)
    mod, gates, slot = call(
        functools.partial(prepare_kernel, cap),
        (pltpu.HBM((2, depth, half), BF16), shape((width, rows), BF16), shape((1, half), F32)),
        "svvvvv",
        "avv",
        [pltpu.VMEM((2, depth, half), BF16), pltpu.SemaphoreType.DMA],
    )(core, req, pos, tsteps.reshape(1, requests), mod_table.transpose(1, 0, 2), gate_table)
    w_back = call(flip_kernel, shape((depth, 2 * inner), BF16), "vv", "v")(w_out, out_sib)
    gains = jnp.concatenate(
        [jnp.tile(qk_gain[0] * HD ** (-0.5), inner // HD), jnp.tile(qk_gain[1], inner // HD)]
    ).reshape(1, 2 * inner)
    text = jnp.pad(context[0], ((0, 0), (0, text_pad - text_len), (0, 0)))
    whole, w_sib, w_back, mod, gates, slot, gains, text = lax.optimization_barrier(
        (whole, w_sib, w_back, mod, gates, slot, gains, text)
    )

    send = call(
        project_kernel,
        shape((2, slots, kinds * inner), BF16),
        "svaaaaavv",
        "v",
        [
            pltpu.VMEM((2, depth, half), BF16),
            pltpu.VMEM((2, depth, kinds * inner), BF16),
            pltpu.VMEM((depth, half), BF16),
            pltpu.SemaphoreType.DMA((1 + 2 * kinds,)),
        ],
        flops=4 * depth * half * kinds * inner,
    )(core, whole, in_hbm(mod), in_hbm(w_own), *[in_hbm(w) for w in w_sib], gains, slot)
    arrived = lax.all_to_all(
        send.reshape(2 * requests, cap, kinds * inner), ("dp", "mp"), 0, 0, axis_index_groups=planes, tiled=True
    )
    attn = call(
        functools.partial(attend_kernel, text_len),
        shape((2 * slots, inner), BF16),
        "vv",
        "v",
        flops=16 * slots * (2 * slots + text_pad) * inner,
    )(arrived.reshape(2 * slots, kinds * inner), text)
    returned = lax.all_to_all(
        attn.reshape(2 * requests, cap, inner), ("dp", "mp"), 0, 0, axis_index_groups=planes, tiled=True
    )
    partial = call(
        output_kernel, shape((parts, width, half), BF16), "svvv", "v", flops=4 * depth * half * inner
    )(core, returned.reshape(2, slots, inner), slot, w_back.reshape(parts, width, 2 * inner))
    sums = lax.all_to_all(partial, "mp", 0, 0, tiled=True)
    return call(finish_kernel, shape((width, rows), BF16), "vvvv", "v")(sums, perm, gates, pos).T


def solution(mesh):
    return jax.shard_map(
        body,
        mesh=mesh,
        in_specs=(
            P("dp", "mp"),
            P("dp", None),
            P(),
            P(),
            P(None, None, "mp"),
            P(),
            P("dp", None, None, "mp"),
            P("mp", None),
        ),
        out_specs=P("dp", "mp"),
        check_vma=False,
    )
```

```python
import functools

import jax
import jax.numpy as jnp
from jax import lax
from jax.experimental import pallas as pl
from jax.experimental.pallas import tpu as pltpu
from jax.sharding import PartitionSpec as P

HD = 64
EPS = 1e-06
DEAD = 1e30
MASKED = -1e30
VMEM_LIMIT = 24 * 1024 * 1024
F32, BF16, I32 = jnp.float32, jnp.bfloat16, jnp.int32


PLACES = {
    "s": pl.BlockSpec(memory_space=pltpu.SMEM),
    "v": pl.BlockSpec(memory_space=pltpu.VMEM),
    "a": pl.BlockSpec(memory_space=pl.ANY),
}


def dot_nt(a, b):
    return lax.dot_general(a, b, (((1,), (1,)), ((), ())), preferred_element_type=F32)


def dot_tn(a, b):
    return lax.dot_general(a, b, (((0,), (0,)), ((), ())), preferred_element_type=F32)


def iota(shape, axis):
    return lax.broadcasted_iota(I32, shape, axis)


def as_column(row):
    n = row.shape[1]
    return jnp.sum(jnp.where(iota((n, n), 0) == iota((n, n), 1), row, 0.0), axis=1, keepdims=True)


def one_hot(flags):
    return jnp.where(flags, 1.0, 0.0).astype(BF16)


def dealt(rows):
    half, quarter = rows // 2, rows // 4
    place = iota((rows, rows), 0)
    core = jnp.where(place >= half, 1, 0)
    place = place - half * core
    parity = jnp.where(place >= quarter, 1, 0)
    return (4 * (place - quarter * parity) + 2 * parity + core).astype(F32)


def spread_kernel(tok_hbm, req_hbm, out_hbm, perm_ref, pos_ref, tok_ref, req_ref, halves_ref, sems):
    width, rows = tok_ref.shape
    half = rows // 2
    parts = out_hbm.shape[0]
    reads = [pltpu.make_async_copy(req_hbm, req_ref, sems.at[0]), pltpu.make_async_copy(tok_hbm, tok_ref, sems.at[1])]
    for copy in reads:
        copy.start()
    reads[0].wait()
    req = req_ref[...].astype(F32)
    req_col = as_column(req)
    earlier = (req_col < req) | ((req_col == req) & (iota((rows, rows), 0) < iota((rows, rows), 1)))
    pos = jnp.sum(jnp.where(earlier, 1.0, 0.0), axis=0, keepdims=True)
    deal = one_hot(pos == dealt(rows))
    pos_ref[...] = pos
    reads[1].wait()
    perm = dot_nt(tok_ref[...], deal).astype(BF16)
    halves_ref[0] = perm[:, :half]
    halves_ref[1] = perm[:, half:]
    writes = [pltpu.make_async_copy(halves_ref.at[m % 2], out_hbm.at[m], sems.at[2 + m]) for m in range(parts)]
    for copy in writes:
        copy.start()
    perm_ref[...] = perm
    for copy in writes:
        copy.wait()


def prepare_kernel(
    cap, core_ref, req_ref, pos_ref, steps_ref, table_ref, gate_ref, mod_hbm, gates_ref, slot_ref, mod_ref, sem
):
    rows = req_ref.shape[1]
    half = rows // 2
    requests = steps_ref.shape[1]
    levels = table_ref.shape[1]
    is_first = core_ref[0] == 0
    req = req_ref[...].astype(F32)
    first = jnp.sum(jnp.where(as_column(req) < req, 1.0, 0.0), axis=0, keepdims=True)
    deal = one_hot(pos_ref[...] == dealt(rows))
    line = iota((8, rows), 0)
    both = jnp.where(line == 0, req, jnp.where(line == 1, first, 0.0)).astype(BF16)
    both = dot_nt(both, deal)
    req_s, first_s = both[0:1], both[1:2]
    index = iota((1, rows), 1)
    side = jnp.where(index >= half, 1, 0)
    index = index - half * side
    parity = jnp.where(index >= half // 2, 1, 0)
    index = (index - half // 2 * parity).astype(F32)
    start = jnp.floor((first_s - (2 * parity + side).astype(F32) + 3.0) * 0.25)
    slot = req_s * cap + (parity * (cap // 2)).astype(F32) + index - start
    slot_ref[...] = jnp.where(is_first, slot[:, :half], slot[:, half:])
    chosen = one_hot(iota((requests, rows), 0).astype(F32) == req_s)
    steps = jnp.broadcast_to(steps_ref[...].astype(F32), (8, requests)).astype(BF16)
    step = jnp.dot(steps, chosen, preferred_element_type=F32)[0:1]
    pick = one_hot(iota((levels, rows), 0).astype(F32) == step)
    gates_ref[...] = dot_tn(gate_ref[...], pick).astype(BF16)
    pick = jnp.where(is_first, pick[:, :half].astype(F32), pick[:, half:].astype(F32)).astype(BF16)
    mod_ref[0] = dot_tn(table_ref[0], pick).astype(BF16)
    mod_ref[1] = dot_tn(table_ref[1], pick).astype(BF16)
    copy = pltpu.make_async_copy(mod_ref, mod_hbm, sem)
    copy.start()
    copy.wait()


def flip_kernel(*refs):
    sources, (out_ref, *held, sems) = refs[:4], refs[4:]
    inner, depth = held[0].shape
    parts, padded, _ = out_ref.shape
    width = depth // parts
    reads = [pltpu.make_async_copy(source, ref, sems.at[i]) for i, (source, ref) in enumerate(zip(sources, held))]
    for copy in reads:
        copy.start()
    for m in range(parts):
        out_ref[m, width:, :] = jnp.zeros((padded - width, out_ref.shape[2]), BF16)
    for i, ref in enumerate(held):
        reads[i].wait()
        turned = ref[...].astype(F32).T
        for m in range(parts):
            out_ref[m, :width, i * inner : (i + 1) * inner] = turned[m * width : (m + 1) * width].astype(BF16)


def project_kernel(
    core_ref, tok_ref, mod_hbm, own_hbm, sib0_hbm, sib1_hbm, sib2_hbm, gain_ref, slot_ref,
    send_ref, mod_ref, w_ref, hid_ref, sems,
):
    parts, width, rows = tok_ref.shape
    depth = parts * width
    kinds, _, inner = own_hbm.shape
    modulation = pltpu.make_async_copy(mod_hbm, mod_ref, sems.at[0])
    modulation.start()
    sources = [own_hbm.at[kind] for kind in range(kinds)] + [sib0_hbm, sib1_hbm, sib2_hbm]
    weights = [
        pltpu.make_async_copy(source, w_ref.at[i // kinds, :, pl.ds(i % kinds * inner, inner)], sems.at[1 + i])
        for i, source in enumerate(sources)
    ]
    for copy in weights:
        copy.start()
    hits = iota((send_ref.shape[1], rows), 0).astype(F32) == slot_ref[...]
    filled = jnp.sum(jnp.where(hits, 1.0, 0.0), axis=1, keepdims=True)
    mark = jnp.where(filled > 0.5, 0.0, DEAD)
    place = one_hot(hits)
    total = sum(jnp.sum(tok_ref[m].astype(F32), axis=0, keepdims=True) for m in range(parts))
    mean = total * (1.0 / depth)
    square = sum(jnp.sum(jnp.square(tok_ref[m].astype(F32) - mean), axis=0, keepdims=True) for m in range(parts))
    inverse = lax.rsqrt(square * (1.0 / depth) + EPS)
    modulation.wait()
    for m in range(0, parts, 2):
        pair = jnp.concatenate([tok_ref[m].astype(F32), tok_ref[m + 1].astype(F32)], axis=0)
        lines = pl.ds(m * width, 2 * width)
        shift, scale = mod_ref[0, lines, :].astype(F32), mod_ref[1, lines, :].astype(F32)
        hid_ref[lines, :] = ((pair - mean) * inverse * (1.0 + scale) + shift).astype(BF16)
    hidden = hid_ref[...].astype(F32).T.astype(BF16)
    normed = 2 * inner
    heads = one_hot(iota((normed, normed), 0) // HD == iota((normed, normed), 1) // HD)
    projected = []
    for side in range(2):
        for copy in weights[side * kinds : (side + 1) * kinds]:
            copy.wait()
        projected.append(jnp.dot(hidden, w_ref[side], preferred_element_type=F32))
    for mixed, target in zip(projected, (core_ref[0], 1 - core_ref[0])):
        turned = mixed[:, :normed]
        power = jnp.square(turned)
        high = power.astype(BF16)
        low = (power - high.astype(F32)).astype(BF16)
        power = jnp.dot(high, heads, preferred_element_type=F32) + jnp.dot(low, heads, preferred_element_type=F32)
        turned = turned * lax.rsqrt(power * (1.0 / HD) + EPS) * gain_ref[...]
        packed = jnp.concatenate([turned, mixed[:, normed:]], axis=1).astype(BF16)
        send = jnp.dot(place, packed, preferred_element_type=F32)
        send = jnp.concatenate([send[:, :inner], send[:, inner:normed] + mark, send[:, normed:]], axis=1)
        send_ref[target] = send.astype(BF16)


def attend_kernel(text_len, slots_ref, ctx_ref, out_ref):
    slots, inner = out_ref.shape
    block = 256
    text_pad = ctx_ref.shape[1]
    queries = slots_ref[:, 0:inner]
    keys = slots_ref[:, inner : 2 * inner].astype(F32)
    dead = keys > 0.5 * DEAD
    marks = jnp.where(dead, 1.0, 0.0).astype(BF16)
    keys = jnp.concatenate([jnp.where(dead, 0.0, keys).astype(BF16), ctx_ref[0]], axis=0)
    own_bias = dot_nt(jnp.full((8, inner), MASKED, BF16), marks)[0:1]
    text_bias = jnp.where(iota((1, text_pad), 1) < text_len, 0.0, MASKED)
    bias = jnp.concatenate([own_bias, text_bias], axis=1)
    values = jnp.concatenate([slots_ref[:, 2 * inner :], ctx_ref[1]], axis=0)
    values = jnp.concatenate([values, jnp.ones(values.shape, BF16)], axis=1)
    first = iota((1, inner), 1) < HD
    zero = jnp.zeros((), BF16)
    for row in range(0, slots, block):
        query = queries[row : row + block]
        query = jnp.concatenate([jnp.where(first, query, zero), jnp.where(first, zero, query)], axis=0)
        scores = dot_nt(query, keys) + bias
        weights = jnp.exp(scores - jnp.max(scores, axis=1, keepdims=True)).astype(BF16)
        mixed = jnp.dot(weights, values, preferred_element_type=F32)
        mixed = mixed[:, :inner] / mixed[:, inner:]
        out_ref[row : row + block, :] = jnp.where(first, mixed[:block], mixed[block:]).astype(BF16)


def output_kernel(sub_slots, core_ref, parity_ref, back_ref, slot_ref, w_ref, part_ref):
    core, parity = core_ref[0], parity_ref[0]
    slots, inner = back_ref.shape[1:]
    quarter = slot_ref.shape[1] // 2
    upper = part_ref.shape[1]
    slot = slot_ref[...]
    slot = as_column(jnp.where(parity == 0, slot[:, :quarter], slot[:, quarter:]))
    shift = (sub_slots * (1 - 2 * parity)).astype(F32)
    attn = []
    for moved in (slot, slot + shift):
        place_t = one_hot(iota((quarter, slots), 1).astype(F32) == moved)
        for side in (core, 1 - core):
            attn.append(jnp.dot(place_t, back_ref[side], preferred_element_type=F32).astype(BF16))
    attn = jnp.concatenate(attn, axis=1)
    empty = jnp.zeros(attn.shape, BF16)
    left, right = jnp.concatenate([attn, empty], axis=0), jnp.concatenate([empty, attn], axis=0)
    for m in range(part_ref.shape[0]):
        part_ref[m] = (dot_nt(w_ref[m, :upper], left) + dot_nt(w_ref[m, upper:], right)).astype(BF16)


def finish_kernel(sums_ref, perm_ref, gates_ref, pos_ref, out_ref):
    parts, upper, lanes = sums_ref.shape
    width, rows = perm_ref.shape
    halves = []
    first = iota((1, lanes), 1) < lanes // 2
    for core in range(2):
        even, odd = [sum(sums_ref[m].astype(F32) for m in range(2 * p + core, parts, 4)) for p in range(2)]
        above = jnp.where(first, even, pltpu.roll(odd, lanes // 2, 1))
        below = jnp.where(first, pltpu.roll(even, lanes // 2, 1), odd)
        halves.append(jnp.concatenate([above, below[: width - upper]], axis=0))
    total = jnp.concatenate(halves, axis=1)
    mixed = (perm_ref[...].astype(F32) + gates_ref[...].astype(F32) * total).astype(BF16)
    deal = one_hot(pos_ref[...] == dealt(rows))
    out_ref[...] = jnp.dot(mixed, deal, preferred_element_type=F32).astype(BF16)


def call(kernel, out_shape, specs, out_specs, scratch=(), flops=0):
    return pl.pallas_call(
        kernel,
        out_shape=out_shape,
        in_specs=[PLACES[letter] for letter in specs],
        out_specs=tuple(PLACES[letter] for letter in out_specs) if len(out_specs) > 1 else PLACES[out_specs],
        scratch_shapes=list(scratch),
        compiler_params=pltpu.CompilerParams(vmem_limit_bytes=VMEM_LIMIT),
        cost_estimate=pl.CostEstimate(flops=flops, bytes_accessed=1 << 20, transcendentals=0),
    )


def body(tokens, route, tsteps, mod_table, w_qkv, qk_gain, context, w_out):
    rows, width = tokens.shape
    half = rows // 2
    requests = lax.axis_size("dp")
    parts = lax.axis_size("mp")
    chips = parts // 2
    cap = max(2, 2 * rows // requests) // 2
    slots = requests * cap
    depth, kinds, inner = w_qkv.shape
    text_len = context.shape[2]
    text_pad = -(-text_len // 128) * 128
    sibling = [(i, i ^ 1) for i in range(parts)]
    planes = [[dp * parts + 2 * z + c for c in range(2) for dp in range(requests)] for z in range(chips)]
    pairs = [
        [dp * parts + 2 * z + c for c in range(2) for dp in range(requests) for z in (even, even + 1)]
        for even in range(0, chips, 2)
    ]
    upper = -(-width // 32) * 16
    place = lax.axis_index("mp").astype(I32)
    core = lax.rem(place, 2).reshape(1)
    parity = lax.rem(lax.div(place, 2), 2).reshape(1)
    shape = jax.ShapeDtypeStruct

    req = route.reshape(1, rows)
    def in_hbm(x):
        return pltpu.with_memory_space_constraint(x, pltpu.HBM)

    spread, perm, pos = call(
        spread_kernel,
        (pltpu.HBM((parts, width, half), BF16), shape((width, rows), BF16), shape((1, rows), F32)),
        "aa",
        "avv",
        [
            pltpu.VMEM((width, rows), BF16),
            pltpu.VMEM((1, rows), I32),
            pltpu.VMEM((2, width, half), BF16),
            pltpu.SemaphoreType.DMA((2 + parts,)),
        ],
    )(in_hbm(tokens.T), in_hbm(req))
    spread, w_qkv = lax.optimization_barrier((spread, w_qkv))
    whole = lax.all_to_all(spread, "mp", 0, 0, tiled=True)

    w_own = w_qkv.transpose(1, 0, 2)
    w_sib = [lax.ppermute(w_own[kind], "mp", sibling) for kind in range(kinds)]
    gate_table = lax.dynamic_slice_in_dim(mod_table[:, 2, :], lax.axis_index("mp") * width, width, 1)
    mod, gates, slot = call(
        functools.partial(prepare_kernel, cap),
        (pltpu.HBM((2, depth, half), BF16), shape((width, rows), BF16), shape((1, half), F32)),
        "svvvvv",
        "avv",
        [pltpu.VMEM((2, depth, half), BF16), pltpu.SemaphoreType.DMA],
    )(core, req, pos, tsteps.reshape(1, requests), mod_table.transpose(1, 0, 2), gate_table)
    gains = jnp.concatenate(
        [jnp.tile(qk_gain[0] * HD ** (-0.5), inner // HD), jnp.tile(qk_gain[1], inner // HD)]
    ).reshape(1, 2 * inner)
    text = jnp.pad(context[0], ((0, 0), (0, text_pad - text_len), (0, 0)))
    whole, w_sib, mod, gates, slot, gains, text = lax.optimization_barrier(
        (whole, w_sib, mod, gates, slot, gains, text)
    )

    send = call(
        project_kernel,
        shape((2, slots, kinds * inner), BF16),
        "svaaaaavv",
        "v",
        [
            pltpu.VMEM((2, depth, half), BF16),
            pltpu.VMEM((2, depth, kinds * inner), BF16),
            pltpu.VMEM((depth, half), BF16),
            pltpu.SemaphoreType.DMA((1 + 2 * kinds,)),
        ],
        flops=4 * depth * half * kinds * inner,
    )(core, whole, in_hbm(mod), in_hbm(w_own), *[in_hbm(w) for w in w_sib], gains, slot)
    send, w_out = lax.optimization_barrier((send, w_out))
    arrived = lax.all_to_all(
        send.reshape(2 * requests, cap, kinds * inner), ("dp", "mp"), 0, 0, axis_index_groups=planes, tiled=True
    )
    w_outs = [lax.ppermute(w_out, "mp", [(i, i ^ step) for i in range(parts)]) for step in (1, 2, 3)]
    attn = call(
        functools.partial(attend_kernel, text_len),
        shape((2 * slots, inner), BF16),
        "vv",
        "v",
        flops=16 * slots * (2 * slots + text_pad) * inner,
    )(arrived.reshape(2 * slots, kinds * inner), text)
    returned = lax.all_to_all(
        attn.reshape(4 * requests, cap // 2, inner), ("dp", "mp"), 0, 0, axis_index_groups=pairs, tiled=True
    )
    _, w_out, w_outs = lax.optimization_barrier((attn, w_out, w_outs))
    w_back = call(
        flip_kernel,
        shape((parts, 2 * upper, 4 * inner), BF16),
        "aaaa",
        "v",
        [pltpu.VMEM((inner, depth), BF16)] * 4 + [pltpu.SemaphoreType.DMA((4,))],
    )(*[in_hbm(w) for w in (w_out, *w_outs)])
    partial = call(
        functools.partial(output_kernel, cap // 2),
        shape((parts, upper, half), BF16),
        "ssvvv",
        "v",
        flops=8 * depth * half * inner,
    )(core, parity, returned.reshape(2, slots, inner), slot, w_back)
    sums = lax.all_to_all(partial, "mp", 0, 0, tiled=True)
    return call(finish_kernel, shape((width, rows), BF16), "vvvv", "v")(sums, perm, gates, pos).T


def solution(mesh):
    return jax.shard_map(
        body,
        mesh=mesh,
        in_specs=(
            P("dp", "mp"),
            P("dp", None),
            P(),
            P(),
            P(None, None, "mp"),
            P(),
            P("dp", None, None, "mp"),
            P("mp", None),
        ),
        out_specs=P("dp", "mp"),
        check_vma=False,
    )
```

```python
import functools

import jax
import jax.numpy as jnp
from jax import lax
from jax.experimental import pallas as pl
from jax.experimental.pallas import tpu as pltpu
from jax.sharding import PartitionSpec as P

HD = 64
EPS = 1e-06
DEAD = 1e30
MASKED = -1e30
VMEM_LIMIT = 24 * 1024 * 1024
F32, BF16, I32 = jnp.float32, jnp.bfloat16, jnp.int32


PLACES = {
    "s": pl.BlockSpec(memory_space=pltpu.SMEM),
    "v": pl.BlockSpec(memory_space=pltpu.VMEM),
    "a": pl.BlockSpec(memory_space=pl.ANY),
}


def dot_nt(a, b):
    return lax.dot_general(a, b, (((1,), (1,)), ((), ())), preferred_element_type=F32)


def dot_tn(a, b):
    return lax.dot_general(a, b, (((0,), (0,)), ((), ())), preferred_element_type=F32)


def iota(shape, axis):
    return lax.broadcasted_iota(I32, shape, axis)


def as_column(row):
    n = row.shape[1]
    return jnp.sum(jnp.where(iota((n, n), 0) == iota((n, n), 1), row, 0.0), axis=1, keepdims=True)


def one_hot(flags):
    return jnp.where(flags, 1.0, 0.0).astype(BF16)


def dealt(rows):
    half, quarter = rows // 2, rows // 4
    place = iota((rows, rows), 0)
    core = jnp.where(place >= half, 1, 0)
    place = place - half * core
    parity = jnp.where(place >= quarter, 1, 0)
    return (4 * (place - quarter * parity) + 2 * parity + core).astype(F32)


def spread_kernel(tok_hbm, req_hbm, out_hbm, perm_ref, pos_ref, tok_ref, req_ref, halves_ref, sems):
    width, rows = tok_ref.shape
    half = rows // 2
    parts = out_hbm.shape[0]
    reads = [pltpu.make_async_copy(req_hbm, req_ref, sems.at[0]), pltpu.make_async_copy(tok_hbm, tok_ref, sems.at[1])]
    for copy in reads:
        copy.start()
    reads[0].wait()
    req = req_ref[...].astype(F32)
    req_col = as_column(req)
    earlier = (req_col < req) | ((req_col == req) & (iota((rows, rows), 0) < iota((rows, rows), 1)))
    pos = jnp.sum(jnp.where(earlier, 1.0, 0.0), axis=0, keepdims=True)
    deal = one_hot(pos == dealt(rows))
    pos_ref[...] = pos
    reads[1].wait()
    perm = dot_nt(tok_ref[...], deal).astype(BF16)
    halves_ref[0] = perm[:, :half]
    halves_ref[1] = perm[:, half:]
    writes = [pltpu.make_async_copy(halves_ref.at[m % 2], out_hbm.at[m], sems.at[2 + m]) for m in range(parts)]
    for copy in writes:
        copy.start()
    perm_ref[...] = perm
    for copy in writes:
        copy.wait()


def prepare_kernel(
    cap, core_ref, req_ref, pos_ref, steps_ref, table_ref, gate_ref, mod_hbm, gates_ref, slot_ref, mod_ref, sem
):
    rows = req_ref.shape[1]
    half = rows // 2
    requests = steps_ref.shape[1]
    levels = table_ref.shape[1]
    is_first = core_ref[0] == 0
    req = req_ref[...].astype(F32)
    first = jnp.sum(jnp.where(as_column(req) < req, 1.0, 0.0), axis=0, keepdims=True)
    deal = one_hot(pos_ref[...] == dealt(rows))
    line = iota((8, rows), 0)
    both = jnp.where(line == 0, req, jnp.where(line == 1, first, 0.0)).astype(BF16)
    both = dot_nt(both, deal)
    req_s, first_s = both[0:1], both[1:2]
    index = iota((1, rows), 1)
    side = jnp.where(index >= half, 1, 0)
    index = index - half * side
    parity = jnp.where(index >= half // 2, 1, 0)
    index = (index - half // 2 * parity).astype(F32)
    start = jnp.floor((first_s - (2 * parity + side).astype(F32) + 3.0) * 0.25)
    slot = req_s * cap + (parity * (cap // 2)).astype(F32) + index - start
    slot_ref[...] = jnp.where(is_first, slot[:, :half], slot[:, half:])
    chosen = one_hot(iota((requests, rows), 0).astype(F32) == req_s)
    steps = jnp.broadcast_to(steps_ref[...].astype(F32), (8, requests)).astype(BF16)
    step = jnp.dot(steps, chosen, preferred_element_type=F32)[0:1]
    pick = one_hot(iota((levels, rows), 0).astype(F32) == step)
    gates_ref[...] = dot_tn(gate_ref[...], pick).astype(BF16)
    pick = jnp.where(is_first, pick[:, :half].astype(F32), pick[:, half:].astype(F32)).astype(BF16)
    mod_ref[0] = dot_tn(table_ref[0], pick).astype(BF16)
    mod_ref[1] = dot_tn(table_ref[1], pick).astype(BF16)
    copy = pltpu.make_async_copy(mod_ref, mod_hbm, sem)
    copy.start()
    copy.wait()


def project_kernel(
    core_ref, tok_ref, mod_hbm, own_hbm, sib0_hbm, sib1_hbm, sib2_hbm, gain_ref, slot_ref,
    send_hbm, mod_ref, w_ref, hid_ref, send_ref, sems,
):
    parts, width, rows = tok_ref.shape
    depth = parts * width
    kinds, _, inner = own_hbm.shape
    modulation = pltpu.make_async_copy(mod_hbm, mod_ref, sems.at[0])
    modulation.start()
    sources = [own_hbm.at[kind] for kind in range(kinds)] + [sib0_hbm, sib1_hbm, sib2_hbm]
    weights = [
        pltpu.make_async_copy(source, w_ref.at[i // kinds, :, pl.ds(i % kinds * inner, inner)], sems.at[1 + i])
        for i, source in enumerate(sources)
    ]
    for copy in weights:
        copy.start()
    hits = iota((send_hbm.shape[1], rows), 0).astype(F32) == slot_ref[...]
    filled = jnp.sum(jnp.where(hits, 1.0, 0.0), axis=1, keepdims=True)
    mark = jnp.where(filled > 0.5, 0.0, DEAD)
    place = one_hot(hits)
    total = sum(jnp.sum(tok_ref[m].astype(F32), axis=0, keepdims=True) for m in range(parts))
    mean = total * (1.0 / depth)
    square = sum(jnp.sum(jnp.square(tok_ref[m].astype(F32) - mean), axis=0, keepdims=True) for m in range(parts))
    inverse = lax.rsqrt(square * (1.0 / depth) + EPS)
    modulation.wait()
    for m in range(0, parts, 2):
        pair = jnp.concatenate([tok_ref[m].astype(F32), tok_ref[m + 1].astype(F32)], axis=0)
        lines = pl.ds(m * width, 2 * width)
        shift, scale = mod_ref[0, lines, :].astype(F32), mod_ref[1, lines, :].astype(F32)
        hid_ref[lines, :] = ((pair - mean) * inverse * (1.0 + scale) + shift).astype(BF16)
    hidden = hid_ref[...].astype(F32).T.astype(BF16)
    normed = 2 * inner
    heads = one_hot(iota((normed, normed), 0) // HD == iota((normed, normed), 1) // HD)
    writes = []
    for side, target in enumerate((core_ref[0], 1 - core_ref[0])):
        for copy in weights[side * kinds : (side + 1) * kinds]:
            copy.wait()
        mixed = jnp.dot(hidden, w_ref[side], preferred_element_type=F32)
        turned = mixed[:, :normed]
        power = jnp.square(turned)
        high = power.astype(BF16)
        low = (power - high.astype(F32)).astype(BF16)
        power = jnp.dot(high, heads, preferred_element_type=F32) + jnp.dot(low, heads, preferred_element_type=F32)
        turned = turned * lax.rsqrt(power * (1.0 / HD) + EPS) * gain_ref[...]
        packed = jnp.concatenate([turned, mixed[:, normed:]], axis=1).astype(BF16)
        send = jnp.dot(place, packed, preferred_element_type=F32)
        send = jnp.concatenate([send[:, :inner], send[:, inner:normed] + mark, send[:, normed:]], axis=1)
        send_ref[side] = send.astype(BF16)
        writes.append(pltpu.make_async_copy(send_ref.at[side], send_hbm.at[target], sems.at[1 + 2 * kinds + side]))
        writes[-1].start()
    for copy in writes:
        copy.wait()


def attend_kernel(text_len, slots_ref, ctx_ref, out_ref):
    slots, inner = out_ref.shape
    block = 256
    text_pad = ctx_ref.shape[1]
    queries = slots_ref[:, 0:inner]
    keys = slots_ref[:, inner : 2 * inner].astype(F32)
    dead = keys > 0.5 * DEAD
    marks = jnp.where(dead, 1.0, 0.0).astype(BF16)
    keys = jnp.concatenate([jnp.where(dead, 0.0, keys).astype(BF16), ctx_ref[0]], axis=0)
    own_bias = dot_nt(jnp.full((8, inner), MASKED, BF16), marks)[0:1]
    text_bias = jnp.where(iota((1, text_pad), 1) < text_len, 0.0, MASKED)
    bias = jnp.concatenate([own_bias, text_bias], axis=1)
    values = jnp.concatenate([slots_ref[:, 2 * inner :], ctx_ref[1]], axis=0)
    values = jnp.concatenate([values, jnp.ones(values.shape, BF16)], axis=1)
    first = iota((1, inner), 1) < HD
    zero = jnp.zeros((), BF16)
    for row in range(0, slots, block):
        query = queries[row : row + block]
        query = jnp.concatenate([jnp.where(first, query, zero), jnp.where(first, zero, query)], axis=0)
        scores = dot_nt(query, keys) + bias
        weights = jnp.exp(scores - jnp.max(scores, axis=1, keepdims=True)).astype(BF16)
        mixed = jnp.dot(weights, values, preferred_element_type=F32)
        mixed = mixed[:, :inner] / mixed[:, inner:]
        out_ref[row : row + block, :] = jnp.where(first, mixed[:block], mixed[block:]).astype(BF16)


def output_kernel(sub_slots, core_ref, parity_ref, back_ref, slot_ref, own_ref, sib_ref, zn_ref, zs_ref, part_ref):
    core, parity = core_ref[0], parity_ref[0]
    slots, inner = back_ref.shape[1:]
    parts, upper, lanes = part_ref.shape
    depth = own_ref.shape[1]
    width = depth // parts
    quarter = slot_ref.shape[1] // 2
    slot = slot_ref[...]
    slot = as_column(jnp.where(parity == 0, slot[:, :quarter], slot[:, quarter:]))
    shift = (sub_slots * (1 - 2 * parity)).astype(F32)
    attn = []
    for moved in (slot, slot + shift):
        place_t = one_hot(iota((quarter, slots), 1).astype(F32) == moved)
        for side in (core, 1 - core):
            attn.append(jnp.dot(place_t, back_ref[side], preferred_element_type=F32).astype(BF16))
    attn = jnp.concatenate(attn, axis=1)
    weights = jnp.concatenate([ref[...] for ref in (own_ref, sib_ref, zn_ref, zs_ref)], axis=0)
    total = jnp.dot(attn, weights, preferred_element_type=F32)
    total = jnp.concatenate([total, jnp.zeros((lanes - quarter, depth), F32)], axis=0).T
    total = jnp.concatenate([total, jnp.zeros((2 * upper - width, lanes), F32)], axis=0)
    for m in range(parts):
        above = total[m * width : m * width + upper]
        below = total[m * width + upper : m * width + 2 * upper]
        part_ref[m] = (above + pltpu.roll(below, quarter, 1)).astype(BF16)


def finish_kernel(sums_ref, perm_ref, gates_ref, pos_ref, out_ref):
    parts, upper, lanes = sums_ref.shape
    width, rows = perm_ref.shape
    halves = []
    first = iota((1, lanes), 1) < lanes // 2
    for core in range(2):
        even, odd = [sum(sums_ref[m].astype(F32) for m in range(2 * p + core, parts, 4)) for p in range(2)]
        above = jnp.where(first, even, pltpu.roll(odd, lanes // 2, 1))
        below = jnp.where(first, pltpu.roll(even, lanes // 2, 1), odd)
        halves.append(jnp.concatenate([above, below[: width - upper]], axis=0))
    total = jnp.concatenate(halves, axis=1)
    mixed = (perm_ref[...].astype(F32) + gates_ref[...].astype(F32) * total).astype(BF16)
    deal = one_hot(pos_ref[...] == dealt(rows))
    out_ref[...] = jnp.dot(mixed, deal, preferred_element_type=F32).astype(BF16)


def call(kernel, out_shape, specs, out_specs, scratch=(), flops=0):
    return pl.pallas_call(
        kernel,
        out_shape=out_shape,
        in_specs=[PLACES[letter] for letter in specs],
        out_specs=tuple(PLACES[letter] for letter in out_specs) if len(out_specs) > 1 else PLACES[out_specs],
        scratch_shapes=list(scratch),
        compiler_params=pltpu.CompilerParams(vmem_limit_bytes=VMEM_LIMIT),
        cost_estimate=pl.CostEstimate(flops=flops, bytes_accessed=1 << 20, transcendentals=0),
    )


def body(tokens, route, tsteps, mod_table, w_qkv, qk_gain, context, w_out):
    rows, width = tokens.shape
    half = rows // 2
    requests = lax.axis_size("dp")
    parts = lax.axis_size("mp")
    chips = parts // 2
    cap = max(2, 2 * rows // requests) // 2
    slots = requests * cap
    depth, kinds, inner = w_qkv.shape
    text_len = context.shape[2]
    text_pad = -(-text_len // 128) * 128
    sibling = [(i, i ^ 1) for i in range(parts)]
    planes = [[dp * parts + 2 * z + c for c in range(2) for dp in range(requests)] for z in range(chips)]
    pairs = [
        [dp * parts + 2 * z + c for c in range(2) for dp in range(requests) for z in (even, even + 1)]
        for even in range(0, chips, 2)
    ]
    upper = -(-width // 32) * 16
    place = lax.axis_index("mp").astype(I32)
    core = lax.rem(place, 2).reshape(1)
    parity = lax.rem(lax.div(place, 2), 2).reshape(1)
    shape = jax.ShapeDtypeStruct

    req = route.reshape(1, rows)
    def in_hbm(x):
        return pltpu.with_memory_space_constraint(x, pltpu.HBM)

    spread, perm, pos = call(
        spread_kernel,
        (pltpu.HBM((parts, width, half), BF16), shape((width, rows), BF16), shape((1, rows), F32)),
        "aa",
        "avv",
        [
            pltpu.VMEM((width, rows), BF16),
            pltpu.VMEM((1, rows), I32),
            pltpu.VMEM((2, width, half), BF16),
            pltpu.SemaphoreType.DMA((2 + parts,)),
        ],
    )(in_hbm(tokens.T), in_hbm(req))
    spread, w_qkv = lax.optimization_barrier((spread, w_qkv))
    whole = lax.all_to_all(spread, "mp", 0, 0, tiled=True)

    w_own = w_qkv.transpose(1, 0, 2)
    w_sib = [lax.ppermute(w_own[kind], "mp", sibling) for kind in range(kinds)]
    gate_table = lax.dynamic_slice_in_dim(mod_table[:, 2, :], lax.axis_index("mp") * width, width, 1)
    mod, gates, slot = call(
        functools.partial(prepare_kernel, cap),
        (pltpu.HBM((2, depth, half), BF16), shape((width, rows), BF16), shape((1, half), F32)),
        "svvvvv",
        "avv",
        [pltpu.VMEM((2, depth, half), BF16), pltpu.SemaphoreType.DMA],
    )(core, req, pos, tsteps.reshape(1, requests), mod_table.transpose(1, 0, 2), gate_table)
    gains = jnp.concatenate(
        [jnp.tile(qk_gain[0] * HD ** (-0.5), inner // HD), jnp.tile(qk_gain[1], inner // HD)]
    ).reshape(1, 2 * inner)
    text = jnp.pad(context[0], ((0, 0), (0, text_pad - text_len), (0, 0)))
    whole, w_sib, mod, gates, slot, gains, text = lax.optimization_barrier(
        (whole, w_sib, mod, gates, slot, gains, text)
    )

    send = call(
        project_kernel,
        pltpu.HBM((2, slots, kinds * inner), BF16),
        "svaaaaavv",
        "a",
        [
            pltpu.VMEM((2, depth, half), BF16),
            pltpu.VMEM((2, depth, kinds * inner), BF16),
            pltpu.VMEM((depth, half), BF16),
            pltpu.VMEM((2, slots, kinds * inner), BF16),
            pltpu.SemaphoreType.DMA((3 + 2 * kinds,)),
        ],
        flops=4 * depth * half * kinds * inner,
    )(core, whole, in_hbm(mod), in_hbm(w_own), *[in_hbm(w) for w in w_sib], gains, slot)
    send, w_out = lax.optimization_barrier((send, w_out))
    arrived = lax.all_to_all(
        send.reshape(2 * requests, cap, kinds * inner), ("dp", "mp"), 0, 0, axis_index_groups=planes, tiled=True
    )
    w_outs = [lax.ppermute(w_out, "mp", [(i, i ^ step) for i in range(parts)]) for step in (1, 2, 3)]
    attn = call(
        functools.partial(attend_kernel, text_len),
        shape((2 * slots, inner), BF16),
        "vv",
        "v",
        flops=16 * slots * (2 * slots + text_pad) * inner,
    )(arrived.reshape(2 * slots, kinds * inner), text)
    returned = lax.all_to_all(
        attn.reshape(4 * requests, cap // 2, inner), ("dp", "mp"), 0, 0, axis_index_groups=pairs, tiled=True
    )
    partial = call(
        functools.partial(output_kernel, cap // 2),
        shape((parts, upper, half), BF16),
        "ssvvvvvv",
        "v",
        flops=8 * depth * half * inner,
    )(core, parity, returned.reshape(2, slots, inner), slot, w_out, *w_outs)
    sums = lax.all_to_all(partial, "mp", 0, 0, tiled=True)
    return call(finish_kernel, shape((width, rows), BF16), "vvvv", "v")(sums, perm, gates, pos).T


def solution(mesh):
    return jax.shard_map(
        body,
        mesh=mesh,
        in_specs=(
            P("dp", "mp"),
            P("dp", None),
            P(),
            P(),
            P(None, None, "mp"),
            P(),
            P("dp", None, None, "mp"),
            P("mp", None),
        ),
        out_specs=P("dp", "mp"),
        check_vma=False,
    )
```

```python
import functools

import jax
import jax.numpy as jnp
from jax import lax
from jax.experimental import pallas as pl
from jax.experimental.pallas import tpu as pltpu
from jax.sharding import PartitionSpec as P

HD = 64
EPS = 1e-06
DEAD = 1e30
MASKED = -1e30
VMEM_LIMIT = 24 * 1024 * 1024
F32, BF16, I32 = jnp.float32, jnp.bfloat16, jnp.int32


PLACES = {
    "s": pl.BlockSpec(memory_space=pltpu.SMEM),
    "v": pl.BlockSpec(memory_space=pltpu.VMEM),
    "a": pl.BlockSpec(memory_space=pl.ANY),
}


def dot_nt(a, b):
    return lax.dot_general(a, b, (((1,), (1,)), ((), ())), preferred_element_type=F32)


def dot_tn(a, b):
    return lax.dot_general(a, b, (((0,), (0,)), ((), ())), preferred_element_type=F32)


def iota(shape, axis):
    return lax.broadcasted_iota(I32, shape, axis)


def as_column(row):
    n = row.shape[1]
    return jnp.sum(jnp.where(iota((n, n), 0) == iota((n, n), 1), row, 0.0), axis=1, keepdims=True)


def one_hot(flags):
    return jnp.where(flags, 1.0, 0.0).astype(BF16)


def dealt(rows):
    half, quarter = rows // 2, rows // 4
    place = iota((rows, rows), 0)
    core = jnp.where(place >= half, 1, 0)
    place = place - half * core
    parity = jnp.where(place >= quarter, 1, 0)
    return (4 * (place - quarter * parity) + 2 * parity + core).astype(F32)


def spread_kernel(tok_hbm, req_hbm, out_hbm, perm_ref, pos_ref, tok_ref, req_ref, halves_ref, sems):
    width, rows = tok_ref.shape
    half = rows // 2
    parts = out_hbm.shape[0]
    reads = [pltpu.make_async_copy(req_hbm, req_ref, sems.at[0]), pltpu.make_async_copy(tok_hbm, tok_ref, sems.at[1])]
    for copy in reads:
        copy.start()
    reads[0].wait()
    req = req_ref[...].astype(F32)
    req_col = as_column(req)
    earlier = (req_col < req) | ((req_col == req) & (iota((rows, rows), 0) < iota((rows, rows), 1)))
    pos = jnp.sum(jnp.where(earlier, 1.0, 0.0), axis=0, keepdims=True)
    deal = one_hot(pos == dealt(rows))
    pos_ref[...] = pos
    reads[1].wait()
    perm = dot_nt(tok_ref[...], deal).astype(BF16)
    halves_ref[0] = perm[:, :half]
    halves_ref[1] = perm[:, half:]
    writes = [pltpu.make_async_copy(halves_ref.at[m % 2], out_hbm.at[m], sems.at[2 + m]) for m in range(parts)]
    for copy in writes:
        copy.start()
    perm_ref[...] = perm
    for copy in writes:
        copy.wait()


def prepare_kernel(
    cap, core_ref, req_ref, pos_ref, steps_ref, table_ref, gate_ref, mod_hbm, gates_ref, slot_ref, mod_ref, sem
):
    rows = req_ref.shape[1]
    half = rows // 2
    requests = steps_ref.shape[1]
    levels = table_ref.shape[1]
    is_first = core_ref[0] == 0
    req = req_ref[...].astype(F32)
    first = jnp.sum(jnp.where(as_column(req) < req, 1.0, 0.0), axis=0, keepdims=True)
    deal = one_hot(pos_ref[...] == dealt(rows))
    line = iota((8, rows), 0)
    both = jnp.where(line == 0, req, jnp.where(line == 1, first, 0.0)).astype(BF16)
    both = dot_nt(both, deal)
    req_s, first_s = both[0:1], both[1:2]
    index = iota((1, rows), 1)
    side = jnp.where(index >= half, 1, 0)
    index = index - half * side
    parity = jnp.where(index >= half // 2, 1, 0)
    index = (index - half // 2 * parity).astype(F32)
    start = jnp.floor((first_s - (2 * parity + side).astype(F32) + 3.0) * 0.25)
    slot = req_s * cap + (parity * (cap // 2)).astype(F32) + index - start
    slot_ref[...] = jnp.where(is_first, slot[:, :half], slot[:, half:])
    chosen = one_hot(iota((requests, rows), 0).astype(F32) == req_s)
    steps = jnp.broadcast_to(steps_ref[...].astype(F32), (8, requests)).astype(BF16)
    step = jnp.dot(steps, chosen, preferred_element_type=F32)[0:1]
    pick = one_hot(iota((levels, rows), 0).astype(F32) == step)
    gates_ref[...] = dot_tn(gate_ref[...], pick).astype(BF16)
    pick = jnp.where(is_first, pick[:, :half].astype(F32), pick[:, half:].astype(F32)).astype(BF16)
    mod_ref[0] = dot_tn(table_ref[0], pick).astype(BF16)
    mod_ref[1] = dot_tn(table_ref[1], pick).astype(BF16)
    copy = pltpu.make_async_copy(mod_ref, mod_hbm, sem)
    copy.start()
    copy.wait()


def project_kernel(
    core_ref, tok_ref, mod_hbm, own_hbm, sib0_hbm, sib1_hbm, sib2_hbm, gain_ref, slot_ref,
    send_ref, mod_ref, w_ref, hid_ref, sems,
):
    parts, width, rows = tok_ref.shape
    depth = parts * width
    kinds, _, inner = own_hbm.shape
    modulation = pltpu.make_async_copy(mod_hbm, mod_ref, sems.at[0])
    modulation.start()
    sources = [own_hbm.at[kind] for kind in range(kinds)] + [sib0_hbm, sib1_hbm, sib2_hbm]
    weights = [
        pltpu.make_async_copy(source, w_ref.at[i // kinds, :, pl.ds(i % kinds * inner, inner)], sems.at[1 + i])
        for i, source in enumerate(sources)
    ]
    for copy in weights:
        copy.start()
    hits = iota((send_ref.shape[1], rows), 0).astype(F32) == slot_ref[...]
    filled = jnp.sum(jnp.where(hits, 1.0, 0.0), axis=1, keepdims=True)
    mark = jnp.where(filled > 0.5, 0.0, DEAD)
    place = one_hot(hits)
    total = sum(jnp.sum(tok_ref[m].astype(F32), axis=0, keepdims=True) for m in range(parts))
    mean = total * (1.0 / depth)
    square = sum(jnp.sum(jnp.square(tok_ref[m].astype(F32) - mean), axis=0, keepdims=True) for m in range(parts))
    inverse = lax.rsqrt(square * (1.0 / depth) + EPS)
    modulation.wait()
    for m in range(0, parts, 2):
        pair = jnp.concatenate([tok_ref[m].astype(F32), tok_ref[m + 1].astype(F32)], axis=0)
        lines = pl.ds(m * width, 2 * width)
        shift, scale = mod_ref[0, lines, :].astype(F32), mod_ref[1, lines, :].astype(F32)
        hid_ref[lines, :] = ((pair - mean) * inverse * (1.0 + scale) + shift).astype(BF16)
    hidden = hid_ref[...].astype(F32).T.astype(BF16)
    normed = 2 * inner
    heads = one_hot(iota((normed, normed), 0) // HD == iota((normed, normed), 1) // HD)
    projected = []
    for side in range(2):
        for copy in weights[side * kinds : (side + 1) * kinds]:
            copy.wait()
        projected.append(jnp.dot(hidden, w_ref[side], preferred_element_type=F32))
    for mixed, target in zip(projected, (core_ref[0], 1 - core_ref[0])):
        turned = mixed[:, :normed]
        power = jnp.square(turned)
        high = power.astype(BF16)
        low = (power - high.astype(F32)).astype(BF16)
        power = jnp.dot(high, heads, preferred_element_type=F32) + jnp.dot(low, heads, preferred_element_type=F32)
        turned = turned * lax.rsqrt(power * (1.0 / HD) + EPS) * gain_ref[...]
        packed = jnp.concatenate([turned, mixed[:, normed:]], axis=1).astype(BF16)
        send = jnp.dot(place, packed, preferred_element_type=F32)
        send = jnp.concatenate([send[:, :inner], send[:, inner:normed] + mark, send[:, normed:]], axis=1)
        send_ref[target] = send.astype(BF16)


def attend_kernel(text_len, slots_ref, ctx_ref, out_ref):
    slots, inner = out_ref.shape
    block = 256
    text_pad = ctx_ref.shape[1]
    queries = slots_ref[:, 0:inner]
    keys = slots_ref[:, inner : 2 * inner].astype(F32)
    dead = keys > 0.5 * DEAD
    marks = jnp.where(dead, 1.0, 0.0).astype(BF16)
    keys = jnp.concatenate([jnp.where(dead, 0.0, keys).astype(BF16), ctx_ref[0]], axis=0)
    own_bias = dot_nt(jnp.full((8, inner), MASKED, BF16), marks)[0:1]
    text_bias = jnp.where(iota((1, text_pad), 1) < text_len, 0.0, MASKED)
    bias = jnp.concatenate([own_bias, text_bias], axis=1)
    values = jnp.concatenate([slots_ref[:, 2 * inner :], ctx_ref[1]], axis=0)
    values = jnp.concatenate([values, jnp.ones(values.shape, BF16)], axis=1)
    first = iota((1, inner), 1) < HD
    zero = jnp.zeros((), BF16)
    for row in range(0, slots, block):
        query = queries[row : row + block]
        query = jnp.concatenate([jnp.where(first, query, zero), jnp.where(first, zero, query)], axis=0)
        scores = dot_nt(query, keys) + bias
        weights = jnp.exp(scores - jnp.max(scores, axis=1, keepdims=True)).astype(BF16)
        mixed = jnp.dot(weights, values, preferred_element_type=F32)
        mixed = mixed[:, :inner] / mixed[:, inner:]
        out_ref[row : row + block, :] = jnp.where(first, mixed[:block], mixed[block:]).astype(BF16)


def output_kernel(sub_slots, core_ref, parity_ref, back_ref, slot_ref, *refs):
    core, parity = core_ref[0], parity_ref[0]
    slots, inner = back_ref.shape[1:]
    *w_refs, part_ref = refs
    parts, upper, lanes = part_ref.shape
    depth = w_refs[0].shape[1]
    width = depth // parts
    quarter = slot_ref.shape[1] // 2
    slot = slot_ref[...]
    slot = as_column(jnp.where(parity == 0, slot[:, :quarter], slot[:, quarter:]))
    shift = (sub_slots * (1 - 2 * parity)).astype(F32)
    attn = []
    for moved in (slot, slot + shift):
        place_t = one_hot(iota((quarter, slots), 1).astype(F32) == moved)
        for side in (core, 1 - core):
            attn.append(jnp.dot(place_t, back_ref[side], preferred_element_type=F32).astype(BF16))
    attn = jnp.concatenate(attn, axis=1)
    weights = jnp.concatenate([ref[...] for ref in w_refs], axis=0)
    total = jnp.dot(attn, weights, preferred_element_type=F32)
    total = jnp.concatenate([total, jnp.zeros((lanes - quarter, depth), F32)], axis=0).T
    total = jnp.concatenate([total, jnp.zeros((2 * upper - width, lanes), F32)], axis=0)
    for m in range(parts):
        above = total[m * width : m * width + upper]
        below = total[m * width + upper : m * width + 2 * upper]
        part_ref[m] = (above + pltpu.roll(below, quarter, 1)).astype(BF16)


def finish_kernel(sums_ref, perm_ref, gates_ref, pos_ref, out_ref):
    parts, upper, lanes = sums_ref.shape
    width, rows = perm_ref.shape
    halves = []
    first = iota((1, lanes), 1) < lanes // 2
    for core in range(2):
        even, odd = [sum(sums_ref[m].astype(F32) for m in range(2 * p + core, parts, 4)) for p in range(2)]
        above = jnp.where(first, even, pltpu.roll(odd, lanes // 2, 1))
        below = jnp.where(first, pltpu.roll(even, lanes // 2, 1), odd)
        halves.append(jnp.concatenate([above, below[: width - upper]], axis=0))
    total = jnp.concatenate(halves, axis=1)
    mixed = (perm_ref[...].astype(F32) + gates_ref[...].astype(F32) * total).astype(BF16)
    deal = one_hot(pos_ref[...] == dealt(rows))
    out_ref[...] = jnp.dot(mixed, deal, preferred_element_type=F32).astype(BF16)


def call(kernel, out_shape, specs, out_specs, scratch=(), flops=0):
    return pl.pallas_call(
        kernel,
        out_shape=out_shape,
        in_specs=[PLACES[letter] for letter in specs],
        out_specs=tuple(PLACES[letter] for letter in out_specs) if len(out_specs) > 1 else PLACES[out_specs],
        scratch_shapes=list(scratch),
        compiler_params=pltpu.CompilerParams(vmem_limit_bytes=VMEM_LIMIT),
        cost_estimate=pl.CostEstimate(flops=flops, bytes_accessed=1 << 20, transcendentals=0),
    )


def body(tokens, route, tsteps, mod_table, w_qkv, qk_gain, context, w_out):
    rows, width = tokens.shape
    half = rows // 2
    requests = lax.axis_size("dp")
    parts = lax.axis_size("mp")
    chips = parts // 2
    cap = max(2, 2 * rows // requests) // 2
    slots = requests * cap
    depth, kinds, inner = w_qkv.shape
    text_len = context.shape[2]
    text_pad = -(-text_len // 128) * 128
    sibling = [(i, i ^ 1) for i in range(parts)]
    planes = [[dp * parts + 2 * z + c for c in range(2) for dp in range(requests)] for z in range(chips)]
    pairs = [
        [dp * parts + 2 * z + c for c in range(2) for dp in range(requests) for z in (even, even + 1)]
        for even in range(0, chips, 2)
    ]
    upper = -(-width // 32) * 16
    place = lax.axis_index("mp").astype(I32)
    core = lax.rem(place, 2).reshape(1)
    parity = lax.rem(lax.div(place, 2), 2).reshape(1)
    shape = jax.ShapeDtypeStruct

    req = route.reshape(1, rows)
    def in_hbm(x):
        return pltpu.with_memory_space_constraint(x, pltpu.HBM)

    spread, perm, pos = call(
        spread_kernel,
        (pltpu.HBM((parts, width, half), BF16), shape((width, rows), BF16), shape((1, rows), F32)),
        "aa",
        "avv",
        [
            pltpu.VMEM((width, rows), BF16),
            pltpu.VMEM((1, rows), I32),
            pltpu.VMEM((2, width, half), BF16),
            pltpu.SemaphoreType.DMA((2 + parts,)),
        ],
    )(in_hbm(tokens.T), in_hbm(req))
    spread, w_qkv, w_out = lax.optimization_barrier((spread, w_qkv, w_out))
    whole = lax.all_to_all(spread, "mp", 0, 0, tiled=True)

    w_own = w_qkv.transpose(1, 0, 2)
    w_sib = [lax.ppermute(w_own[kind], "mp", sibling) for kind in range(kinds)]
    out_sib = lax.ppermute(w_out, "mp", sibling)
    first_rows = inner * 3 // 8
    gate_table = lax.dynamic_slice_in_dim(mod_table[:, 2, :], lax.axis_index("mp") * width, width, 1)
    mod, gates, slot = call(
        functools.partial(prepare_kernel, cap),
        (pltpu.HBM((2, depth, half), BF16), shape((width, rows), BF16), shape((1, half), F32)),
        "svvvvv",
        "avv",
        [pltpu.VMEM((2, depth, half), BF16), pltpu.SemaphoreType.DMA],
    )(core, req, pos, tsteps.reshape(1, requests), mod_table.transpose(1, 0, 2), gate_table)
    gains = jnp.concatenate(
        [jnp.tile(qk_gain[0] * HD ** (-0.5), inner // HD), jnp.tile(qk_gain[1], inner // HD)]
    ).reshape(1, 2 * inner)
    text = jnp.pad(context[0], ((0, 0), (0, text_pad - text_len), (0, 0)))
    whole, w_sib, out_sib, mod, gates, slot, gains, text = lax.optimization_barrier(
        (whole, w_sib, out_sib, mod, gates, slot, gains, text)
    )

    send = call(
        project_kernel,
        shape((2, slots, kinds * inner), BF16),
        "svaaaaavv",
        "v",
        [
            pltpu.VMEM((2, depth, half), BF16),
            pltpu.VMEM((2, depth, kinds * inner), BF16),
            pltpu.VMEM((depth, half), BF16),
            pltpu.SemaphoreType.DMA((1 + 2 * kinds,)),
        ],
        flops=4 * depth * half * kinds * inner,
    )(core, whole, in_hbm(mod), in_hbm(w_own), *[in_hbm(w) for w in w_sib], gains, slot)
    send, early, late = lax.optimization_barrier((send, w_out[:first_rows], w_out[first_rows:]))
    arrived = lax.all_to_all(
        send.reshape(2 * requests, cap, kinds * inner), ("dp", "mp"), 0, 0, axis_index_groups=planes, tiled=True
    )
    next_level = [(i, i ^ 2) for i in range(parts)]
    next_early = lax.ppermute(early, "mp", next_level)
    next_late = lax.ppermute(late, "mp", next_level)
    far_late = lax.ppermute(late, "mp", [(i, i ^ 3) for i in range(parts)])
    far_early = lax.ppermute(next_early, "mp", sibling)
    blocks = (w_out, out_sib, next_early, next_late, far_early, far_late)
    attn = call(
        functools.partial(attend_kernel, text_len),
        shape((2 * slots, inner), BF16),
        "vv",
        "v",
        flops=16 * slots * (2 * slots + text_pad) * inner,
    )(arrived.reshape(2 * slots, kinds * inner), text)
    returned = lax.all_to_all(
        attn.reshape(4 * requests, cap // 2, inner), ("dp", "mp"), 0, 0, axis_index_groups=pairs, tiled=True
    )
    partial = call(
        functools.partial(output_kernel, cap // 2),
        shape((parts, upper, half), BF16),
        "ssvvvvvvvv",
        "v",
        flops=8 * depth * half * inner,
    )(core, parity, returned.reshape(2, slots, inner), slot, *blocks)
    sums = lax.all_to_all(partial, "mp", 0, 0, tiled=True)
    return call(finish_kernel, shape((width, rows), BF16), "vvvv", "v")(sums, perm, gates, pos).T


def solution(mesh):
    return jax.shard_map(
        body,
        mesh=mesh,
        in_specs=(
            P("dp", "mp"),
            P("dp", None),
            P(),
            P(),
            P(None, None, "mp"),
            P(),
            P("dp", None, None, "mp"),
            P("mp", None),
        ),
        out_specs=P("dp", "mp"),
        check_vma=False,
    )
```

```python
import functools

import jax
import jax.numpy as jnp
from jax import lax
from jax.experimental import pallas as pl
from jax.experimental.pallas import tpu as pltpu
from jax.sharding import PartitionSpec as P

HD = 64
EPS = 1e-06
DEAD = 1e30
MASKED = -1e30
VMEM_LIMIT = 24 * 1024 * 1024
F32, BF16, I32 = jnp.float32, jnp.bfloat16, jnp.int32


PLACES = {
    "s": pl.BlockSpec(memory_space=pltpu.SMEM),
    "v": pl.BlockSpec(memory_space=pltpu.VMEM),
    "a": pl.BlockSpec(memory_space=pl.ANY),
}


def dot_nt(a, b):
    return lax.dot_general(a, b, (((1,), (1,)), ((), ())), preferred_element_type=F32)


def dot_tn(a, b):
    return lax.dot_general(a, b, (((0,), (0,)), ((), ())), preferred_element_type=F32)


def iota(shape, axis):
    return lax.broadcasted_iota(I32, shape, axis)


def as_column(row):
    n = row.shape[1]
    return jnp.sum(jnp.where(iota((n, n), 0) == iota((n, n), 1), row, 0.0), axis=1, keepdims=True)


def one_hot(flags):
    return jnp.where(flags, 1.0, 0.0).astype(BF16)


def dealt(rows):
    half, quarter = rows // 2, rows // 4
    place = iota((rows, rows), 0)
    core = jnp.where(place >= half, 1, 0)
    place = place - half * core
    parity = jnp.where(place >= quarter, 1, 0)
    return (4 * (place - quarter * parity) + 2 * parity + core).astype(F32)


def spread_kernel(tok_hbm, req_hbm, out_hbm, perm_ref, pos_ref, tok_ref, req_ref, halves_ref, sems):
    width, rows = tok_ref.shape
    half = rows // 2
    parts = out_hbm.shape[0]
    reads = [pltpu.make_async_copy(req_hbm, req_ref, sems.at[0]), pltpu.make_async_copy(tok_hbm, tok_ref, sems.at[1])]
    for copy in reads:
        copy.start()
    reads[0].wait()
    req = req_ref[...].astype(F32)
    req_col = as_column(req)
    earlier = (req_col < req) | ((req_col == req) & (iota((rows, rows), 0) < iota((rows, rows), 1)))
    pos = jnp.sum(jnp.where(earlier, 1.0, 0.0), axis=0, keepdims=True)
    deal = one_hot(pos == dealt(rows))
    pos_ref[...] = pos
    reads[1].wait()
    perm = dot_nt(tok_ref[...], deal).astype(BF16)
    halves_ref[0] = perm[:, :half]
    halves_ref[1] = perm[:, half:]
    writes = [pltpu.make_async_copy(halves_ref.at[m % 2], out_hbm.at[m], sems.at[2 + m]) for m in range(parts)]
    for copy in writes:
        copy.start()
    perm_ref[...] = perm
    for copy in writes:
        copy.wait()


def prepare_kernel(
    cap, core_ref, req_ref, pos_ref, steps_ref, table_hbm, gate_ref,
    mod_hbm, gates_ref, slot_ref, mod_ref, table_ref, sems,
):
    read = pltpu.make_async_copy(table_hbm.at[pl.ds(0, 2)], table_ref, sems.at[2])
    read.start()
    rows = req_ref.shape[1]
    half = rows // 2
    requests = steps_ref.shape[1]
    levels = gate_ref.shape[0]
    is_first = core_ref[0] == 0
    req = req_ref[...].astype(F32)
    first = jnp.sum(jnp.where(as_column(req) < req, 1.0, 0.0), axis=0, keepdims=True)
    deal = one_hot(pos_ref[...] == dealt(rows))
    line = iota((8, rows), 0)
    both = jnp.where(line == 0, req, jnp.where(line == 1, first, 0.0)).astype(BF16)
    both = dot_nt(both, deal)
    req_s, first_s = both[0:1], both[1:2]
    index = iota((1, rows), 1)
    side = jnp.where(index >= half, 1, 0)
    index = index - half * side
    parity = jnp.where(index >= half // 2, 1, 0)
    index = (index - half // 2 * parity).astype(F32)
    start = jnp.floor((first_s - (2 * parity + side).astype(F32) + 3.0) * 0.25)
    slot = req_s * cap + (parity * (cap // 2)).astype(F32) + index - start
    slot_ref[...] = jnp.where(is_first, slot[:, :half], slot[:, half:])
    chosen = one_hot(iota((requests, rows), 0).astype(F32) == req_s)
    steps = jnp.broadcast_to(steps_ref[...].astype(F32), (8, requests)).astype(BF16)
    step = jnp.dot(steps, chosen, preferred_element_type=F32)[0:1]
    pick = one_hot(iota((levels, rows), 0).astype(F32) == step)
    gates_ref[...] = dot_tn(gate_ref[...], pick).astype(BF16)
    pick = jnp.where(is_first, pick[:, :half].astype(F32), pick[:, half:].astype(F32)).astype(BF16)
    read.wait()
    writes = []
    for part in range(2):
        mod_ref[part] = dot_tn(table_ref[part], pick).astype(BF16)
        writes.append(pltpu.make_async_copy(mod_ref.at[part], mod_hbm.at[part], sems.at[part]))
        writes[-1].start()
    for copy in writes:
        copy.wait()


def project_kernel(
    core_ref, tok_ref, mod_hbm, own0_ref, own1_ref, own2_ref, sib0_hbm, sib1_hbm, sib2_hbm, gain_ref, slot_ref,
    send_ref, mod_ref, w_ref, hid_ref, sems,
):
    parts, width, rows = tok_ref.shape
    depth = parts * width
    inner = own0_ref.shape[1]
    modulation = pltpu.make_async_copy(mod_hbm, mod_ref, sems.at[0])
    modulation.start()
    weights = [
        pltpu.make_async_copy(source, w_ref.at[:, pl.ds(i * inner, inner)], sems.at[1 + i])
        for i, source in enumerate((sib0_hbm, sib1_hbm, sib2_hbm))
    ]
    for copy in weights:
        copy.start()
    hits = iota((send_ref.shape[1], rows), 0).astype(F32) == slot_ref[...]
    filled = jnp.sum(jnp.where(hits, 1.0, 0.0), axis=1, keepdims=True)
    mark = jnp.where(filled > 0.5, 0.0, DEAD)
    place = one_hot(hits)
    total = sum(jnp.sum(tok_ref[m].astype(F32), axis=0, keepdims=True) for m in range(parts))
    mean = total * (1.0 / depth)
    square = sum(jnp.sum(jnp.square(tok_ref[m].astype(F32) - mean), axis=0, keepdims=True) for m in range(parts))
    inverse = lax.rsqrt(square * (1.0 / depth) + EPS)
    modulation.wait()
    for m in range(0, parts, 2):
        pair = jnp.concatenate([tok_ref[m].astype(F32), tok_ref[m + 1].astype(F32)], axis=0)
        lines = pl.ds(m * width, 2 * width)
        shift, scale = mod_ref[0, lines, :].astype(F32), mod_ref[1, lines, :].astype(F32)
        hid_ref[lines, :] = ((pair - mean) * inverse * (1.0 + scale) + shift).astype(BF16)
    hidden = hid_ref[...].astype(F32).T.astype(BF16)
    normed = 2 * inner
    heads = one_hot(iota((normed, normed), 0) // HD == iota((normed, normed), 1) // HD)
    gain = [gain_ref[0:1, :] * HD ** (-0.5)] * (inner // HD) + [gain_ref[1:2, :]] * (inner // HD)
    gain = jnp.concatenate(gain, axis=1)
    own = jnp.concatenate([own0_ref[...], own1_ref[...], own2_ref[...]], axis=1)
    projected = [jnp.dot(hidden, own, preferred_element_type=F32)]
    for copy in weights:
        copy.wait()
    projected.append(jnp.dot(hidden, w_ref[...], preferred_element_type=F32))
    for mixed, target in zip(projected, (core_ref[0], 1 - core_ref[0])):
        turned = mixed[:, :normed]
        power = jnp.square(turned)
        high = power.astype(BF16)
        low = (power - high.astype(F32)).astype(BF16)
        power = jnp.dot(high, heads, preferred_element_type=F32) + jnp.dot(low, heads, preferred_element_type=F32)
        turned = turned * lax.rsqrt(power * (1.0 / HD) + EPS) * gain
        packed = jnp.concatenate([turned, mixed[:, normed:]], axis=1).astype(BF16)
        send = jnp.dot(place, packed, preferred_element_type=F32)
        send = jnp.concatenate([send[:, :inner], send[:, inner:normed] + mark, send[:, normed:]], axis=1)
        send_ref[target] = send.astype(BF16)


def attend_kernel(text_len, slots_ref, ctx_ref, out_ref):
    slots, inner = out_ref.shape
    block = 256
    text_pad = ctx_ref.shape[1]
    queries = slots_ref[:, 0:inner]
    keys = slots_ref[:, inner : 2 * inner].astype(F32)
    dead = keys > 0.5 * DEAD
    marks = jnp.where(dead, 1.0, 0.0).astype(BF16)
    keys = jnp.concatenate([jnp.where(dead, 0.0, keys).astype(BF16), ctx_ref[0]], axis=0)
    own_bias = dot_nt(jnp.full((8, inner), MASKED, BF16), marks)[0:1]
    text_bias = jnp.where(iota((1, text_pad), 1) < text_len, 0.0, MASKED)
    bias = jnp.concatenate([own_bias, text_bias], axis=1)
    values = jnp.concatenate([slots_ref[:, 2 * inner :], ctx_ref[1]], axis=0)
    values = jnp.concatenate([values, jnp.ones(values.shape, BF16)], axis=1)
    first = iota((1, inner), 1) < HD
    zero = jnp.zeros((), BF16)
    for row in range(0, slots, block):
        query = queries[row : row + block]
        query = jnp.concatenate([jnp.where(first, query, zero), jnp.where(first, zero, query)], axis=0)
        scores = dot_nt(query, keys) + bias
        weights = jnp.exp(scores - jnp.max(scores, axis=1, keepdims=True)).astype(BF16)
        mixed = jnp.dot(weights, values, preferred_element_type=F32)
        mixed = mixed[:, :inner] / mixed[:, inner:]
        out_ref[row : row + block, :] = jnp.where(first, mixed[:block], mixed[block:]).astype(BF16)


def output_kernel(sub_slots, core_ref, parity_ref, back_ref, slot_ref, *refs):
    core, parity = core_ref[0], parity_ref[0]
    slots, inner = back_ref.shape[1:]
    *w_refs, part_ref = refs
    parts, upper, lanes = part_ref.shape
    depth = w_refs[0].shape[1]
    width = depth // parts
    quarter = slot_ref.shape[1] // 2
    slot = slot_ref[...]
    slot = as_column(jnp.where(parity == 0, slot[:, :quarter], slot[:, quarter:]))
    shift = (sub_slots * (1 - 2 * parity)).astype(F32)
    attn = []
    for moved in (slot, slot + shift):
        place_t = one_hot(iota((quarter, slots), 1).astype(F32) == moved)
        for side in (core, 1 - core):
            attn.append(jnp.dot(place_t, back_ref[side], preferred_element_type=F32).astype(BF16))
    attn = jnp.concatenate(attn, axis=1)
    weights = jnp.concatenate([ref[...] for ref in w_refs], axis=0)
    total = jnp.dot(attn, weights, preferred_element_type=F32)
    total = jnp.concatenate([total, jnp.zeros((lanes - quarter, depth), F32)], axis=0).T
    total = jnp.concatenate([total, jnp.zeros((2 * upper - width, lanes), F32)], axis=0)
    for m in range(parts):
        above = total[m * width : m * width + upper]
        below = total[m * width + upper : m * width + 2 * upper]
        part_ref[m] = (above + pltpu.roll(below, quarter, 1)).astype(BF16)


def finish_kernel(sums_ref, perm_ref, gates_ref, pos_ref, out_ref):
    parts, upper, lanes = sums_ref.shape
    width, rows = perm_ref.shape
    halves = []
    first = iota((1, lanes), 1) < lanes // 2
    for core in range(2):
        even, odd = [sum(sums_ref[m].astype(F32) for m in range(2 * p + core, parts, 4)) for p in range(2)]
        above = jnp.where(first, even, pltpu.roll(odd, lanes // 2, 1))
        below = jnp.where(first, pltpu.roll(even, lanes // 2, 1), odd)
        halves.append(jnp.concatenate([above, below[: width - upper]], axis=0))
    total = jnp.concatenate(halves, axis=1)
    mixed = (perm_ref[...].astype(F32) + gates_ref[...].astype(F32) * total).astype(BF16)
    deal = one_hot(pos_ref[...] == dealt(rows))
    out_ref[...] = jnp.dot(mixed, deal, preferred_element_type=F32).astype(BF16)


def call(kernel, out_shape, specs, out_specs, scratch=(), flops=0):
    return pl.pallas_call(
        kernel,
        out_shape=out_shape,
        in_specs=[PLACES[letter] for letter in specs],
        out_specs=tuple(PLACES[letter] for letter in out_specs) if len(out_specs) > 1 else PLACES[out_specs],
        scratch_shapes=list(scratch),
        compiler_params=pltpu.CompilerParams(vmem_limit_bytes=VMEM_LIMIT),
        cost_estimate=pl.CostEstimate(flops=flops, bytes_accessed=1 << 20, transcendentals=0),
    )


def body(tokens, route, tsteps, mod_table, w_qkv, qk_gain, context, w_out):
    rows, width = tokens.shape
    half = rows // 2
    requests = lax.axis_size("dp")
    parts = lax.axis_size("mp")
    chips = parts // 2
    cap = max(2, 2 * rows // requests) // 2
    slots = requests * cap
    depth, kinds, inner = w_qkv.shape
    text_len = context.shape[2]
    text_pad = -(-text_len // 128) * 128
    sibling = [(i, i ^ 1) for i in range(parts)]
    planes = [[dp * parts + 2 * z + c for c in range(2) for dp in range(requests)] for z in range(chips)]
    pairs = [
        [dp * parts + 2 * z + c for c in range(2) for dp in range(requests) for z in (even, even + 1)]
        for even in range(0, chips, 2)
    ]
    upper = -(-width // 32) * 16
    place = lax.axis_index("mp").astype(I32)
    core = lax.rem(place, 2).reshape(1)
    parity = lax.rem(lax.div(place, 2), 2).reshape(1)
    shape = jax.ShapeDtypeStruct

    req = route.reshape(1, rows)
    def in_hbm(x):
        return pltpu.with_memory_space_constraint(x, pltpu.HBM)

    def in_vmem(x):
        return pltpu.with_memory_space_constraint(x, pltpu.VMEM)

    spread, perm, pos = call(
        spread_kernel,
        (pltpu.HBM((parts, width, half), BF16), shape((width, rows), BF16), shape((1, rows), F32)),
        "aa",
        "avv",
        [
            pltpu.VMEM((width, rows), BF16),
            pltpu.VMEM((1, rows), I32),
            pltpu.VMEM((2, width, half), BF16),
            pltpu.SemaphoreType.DMA((2 + parts,)),
        ],
    )(in_hbm(tokens.T), in_hbm(req))
    spread, w_qkv, w_out = lax.optimization_barrier((spread, w_qkv, w_out))
    whole = lax.all_to_all(spread, "mp", 0, 0, tiled=True)

    w_own = [w_qkv[:, kind] for kind in range(kinds)]
    w_sib = [lax.ppermute(block, "mp", sibling) for block in w_own]
    out_sib = lax.ppermute(w_out, "mp", sibling)
    first_rows = inner * 3 // 8
    gate_table = lax.dynamic_slice_in_dim(mod_table[:, 2, :], lax.axis_index("mp") * width, width, 1)
    mod, gates, slot = call(
        functools.partial(prepare_kernel, cap),
        (pltpu.HBM((2, depth, half), BF16), shape((width, rows), BF16), shape((1, half), F32)),
        "svvvav",
        "avv",
        [
            pltpu.VMEM((2, depth, half), BF16),
            pltpu.VMEM((2, gate_table.shape[0], depth), BF16),
            pltpu.SemaphoreType.DMA((3,)),
        ],
    )(core, req, pos, tsteps.reshape(1, requests), in_hbm(mod_table.transpose(1, 0, 2)), gate_table)
    whole, w_own, w_sib, out_sib, mod, gates, slot = lax.optimization_barrier(
        (whole, w_own, w_sib, out_sib, mod, gates, slot)
    )

    send = call(
        project_kernel,
        shape((2, slots, kinds * inner), BF16),
        "svavvvaaavv",
        "v",
        [
            pltpu.VMEM((2, depth, half), BF16),
            pltpu.VMEM((depth, kinds * inner), BF16),
            pltpu.VMEM((depth, half), BF16),
            pltpu.SemaphoreType.DMA((1 + kinds,)),
        ],
        flops=4 * depth * half * kinds * inner,
    )(core, whole, in_hbm(mod), *[in_vmem(w) for w in w_own], *[in_hbm(w) for w in w_sib], qk_gain, slot)
    send, early, late, context = lax.optimization_barrier(
        (send, w_out[:first_rows], w_out[first_rows:], context)
    )
    text = jnp.pad(context[0], ((0, 0), (0, text_pad - text_len), (0, 0)))
    arrived = lax.all_to_all(
        send.reshape(2 * requests, cap, kinds * inner), ("dp", "mp"), 0, 0, axis_index_groups=planes, tiled=True
    )
    next_level = [(i, i ^ 2) for i in range(parts)]
    next_early = lax.ppermute(early, "mp", next_level)
    next_late = lax.ppermute(late, "mp", next_level)
    far_late = lax.ppermute(late, "mp", [(i, i ^ 3) for i in range(parts)])
    far_early = lax.ppermute(next_early, "mp", sibling)
    blocks = (w_out, out_sib, next_early, next_late, far_early, far_late)
    attn = call(
        functools.partial(attend_kernel, text_len),
        shape((2 * slots, inner), BF16),
        "vv",
        "v",
        flops=16 * slots * (2 * slots + text_pad) * inner,
    )(arrived.reshape(2 * slots, kinds * inner), text)
    returned = lax.all_to_all(
        attn.reshape(4 * requests, cap // 2, inner), ("dp", "mp"), 0, 0, axis_index_groups=pairs, tiled=True
    )
    partial = call(
        functools.partial(output_kernel, cap // 2),
        shape((parts, upper, half), BF16),
        "ssvvvvvvvv",
        "v",
        flops=8 * depth * half * inner,
    )(core, parity, returned.reshape(2, slots, inner), slot, *blocks)
    sums = lax.all_to_all(partial, "mp", 0, 0, tiled=True)
    return call(finish_kernel, shape((width, rows), BF16), "vvvv", "v")(sums, perm, gates, pos).T


def solution(mesh):
    return jax.shard_map(
        body,
        mesh=mesh,
        in_specs=(
            P("dp", "mp"),
            P("dp", None),
            P(),
            P(),
            P(None, None, "mp"),
            P(),
            P("dp", None, None, "mp"),
            P("mp", None),
        ),
        out_specs=P("dp", "mp"),
        check_vma=False,
    )
```

```python
import functools

import jax
import jax.numpy as jnp
from jax import lax
from jax.experimental import pallas as pl
from jax.experimental.pallas import tpu as pltpu
from jax.sharding import PartitionSpec as P

HD = 64
EPS = 1e-06
DEAD = 1e30
MASKED = -1e30
VMEM_LIMIT = 24 * 1024 * 1024
F32, BF16, I32 = jnp.float32, jnp.bfloat16, jnp.int32


PLACES = {
    "s": pl.BlockSpec(memory_space=pltpu.SMEM),
    "v": pl.BlockSpec(memory_space=pltpu.VMEM),
    "a": pl.BlockSpec(memory_space=pl.ANY),
}


def dot_nt(a, b):
    return lax.dot_general(a, b, (((1,), (1,)), ((), ())), preferred_element_type=F32)


def dot_tn(a, b):
    return lax.dot_general(a, b, (((0,), (0,)), ((), ())), preferred_element_type=F32)


def iota(shape, axis):
    return lax.broadcasted_iota(I32, shape, axis)


def as_column(row):
    n = row.shape[1]
    return jnp.sum(jnp.where(iota((n, n), 0) == iota((n, n), 1), row, 0.0), axis=1, keepdims=True)


def one_hot(flags):
    return jnp.where(flags, 1.0, 0.0).astype(BF16)


def dealt(rows):
    half, quarter = rows // 2, rows // 4
    place = iota((rows, rows), 0)
    core = jnp.where(place >= half, 1, 0)
    place = place - half * core
    parity = jnp.where(place >= quarter, 1, 0)
    return (4 * (place - quarter * parity) + 2 * parity + core).astype(F32)


def spread_kernel(tok_hbm, req_hbm, out_hbm, perm_ref, pos_ref, tok_ref, req_ref, halves_ref, sems):
    width, rows = tok_ref.shape
    half = rows // 2
    parts = out_hbm.shape[0]
    reads = [pltpu.make_async_copy(req_hbm, req_ref, sems.at[0]), pltpu.make_async_copy(tok_hbm, tok_ref, sems.at[1])]
    for copy in reads:
        copy.start()
    reads[0].wait()
    req = req_ref[...].astype(F32)
    req_col = as_column(req)
    earlier = (req_col < req) | ((req_col == req) & (iota((rows, rows), 0) < iota((rows, rows), 1)))
    pos = jnp.sum(jnp.where(earlier, 1.0, 0.0), axis=0, keepdims=True)
    deal = one_hot(pos == dealt(rows))
    pos_ref[...] = pos
    reads[1].wait()
    perm = dot_nt(tok_ref[...], deal).astype(BF16)
    halves_ref[0] = perm[:, :half]
    halves_ref[1] = perm[:, half:]
    writes = [pltpu.make_async_copy(halves_ref.at[m % 2], out_hbm.at[m], sems.at[2 + m]) for m in range(parts)]
    for copy in writes:
        copy.start()
    perm_ref[...] = perm
    for copy in writes:
        copy.wait()


def prepare_kernel(
    cap, core_ref, req_ref, pos_ref, steps_ref, table_hbm, gate_ref,
    mod_hbm, gates_ref, slot_ref, mod_ref, table_ref, sems,
):
    read = pltpu.make_async_copy(table_hbm.at[pl.ds(0, 2)], table_ref, sems.at[2])
    read.start()
    rows = req_ref.shape[1]
    half = rows // 2
    requests = steps_ref.shape[1]
    levels = gate_ref.shape[0]
    is_first = core_ref[0] == 0
    req = req_ref[...].astype(F32)
    first = jnp.sum(jnp.where(as_column(req) < req, 1.0, 0.0), axis=0, keepdims=True)
    deal = one_hot(pos_ref[...] == dealt(rows))
    line = iota((8, rows), 0)
    both = jnp.where(line == 0, req, jnp.where(line == 1, first, 0.0)).astype(BF16)
    both = dot_nt(both, deal)
    req_s, first_s = both[0:1], both[1:2]
    index = iota((1, rows), 1)
    side = jnp.where(index >= half, 1, 0)
    index = index - half * side
    parity = jnp.where(index >= half // 2, 1, 0)
    index = (index - half // 2 * parity).astype(F32)
    start = jnp.floor((first_s - (2 * parity + side).astype(F32) + 3.0) * 0.25)
    slot = req_s * cap + (parity * (cap // 2)).astype(F32) + index - start
    slot_ref[...] = jnp.where(is_first, slot[:, :half], slot[:, half:])
    chosen = one_hot(iota((requests, rows), 0).astype(F32) == req_s)
    steps = jnp.broadcast_to(steps_ref[...].astype(F32), (8, requests)).astype(BF16)
    step = jnp.dot(steps, chosen, preferred_element_type=F32)[0:1]
    pick = one_hot(iota((levels, rows), 0).astype(F32) == step)
    gates_ref[...] = dot_tn(gate_ref[...], pick).astype(BF16)
    pick = jnp.where(is_first, pick[:, :half].astype(F32), pick[:, half:].astype(F32)).astype(BF16)
    read.wait()
    writes = []
    for part in range(2):
        mod_ref[part] = dot_tn(table_ref[part], pick).astype(BF16)
        writes.append(pltpu.make_async_copy(mod_ref.at[part], mod_hbm.at[part], sems.at[part]))
        writes[-1].start()
    for copy in writes:
        copy.wait()


def project_kernel(
    core_ref, tok_ref, mod_hbm, own0_ref, own1_ref, own2_ref, sib0_hbm, sib1_hbm, sib2_hbm, gain_ref, slot_ref,
    send_ref, mod_ref, w_ref, hid_ref, sems,
):
    parts, width, rows = tok_ref.shape
    depth = parts * width
    inner = own0_ref.shape[1]
    modulation = pltpu.make_async_copy(mod_hbm, mod_ref, sems.at[0])
    modulation.start()
    weights = [
        pltpu.make_async_copy(source, w_ref.at[:, pl.ds(i * inner, inner)], sems.at[1 + i])
        for i, source in enumerate((sib0_hbm, sib1_hbm, sib2_hbm))
    ]
    for copy in weights:
        copy.start()
    hits = iota((send_ref.shape[1], rows), 0).astype(F32) == slot_ref[...]
    filled = jnp.sum(jnp.where(hits, 1.0, 0.0), axis=1, keepdims=True)
    mark = jnp.where(filled > 0.5, 0.0, DEAD)
    place = one_hot(hits)
    total = sum(jnp.sum(tok_ref[m].astype(F32), axis=0, keepdims=True) for m in range(parts))
    mean = total * (1.0 / depth)
    square = sum(jnp.sum(jnp.square(tok_ref[m].astype(F32) - mean), axis=0, keepdims=True) for m in range(parts))
    inverse = lax.rsqrt(square * (1.0 / depth) + EPS)
    modulation.wait()
    for m in range(0, parts, 2):
        pair = jnp.concatenate([tok_ref[m].astype(F32), tok_ref[m + 1].astype(F32)], axis=0)
        lines = pl.ds(m * width, 2 * width)
        shift, scale = mod_ref[0, lines, :].astype(F32), mod_ref[1, lines, :].astype(F32)
        hid_ref[lines, :] = ((pair - mean) * inverse * (1.0 + scale) + shift).astype(BF16)
    hidden = hid_ref[...].astype(F32).T.astype(BF16)
    normed = 2 * inner
    heads = one_hot(iota((normed, normed), 0) // HD == iota((normed, normed), 1) // HD)
    gain = [gain_ref[0:1, :] * HD ** (-0.5)] * (inner // HD) + [gain_ref[1:2, :]] * (inner // HD)
    gain = jnp.concatenate(gain, axis=1)
    own = jnp.concatenate([own0_ref[...], own1_ref[...], own2_ref[...]], axis=1)
    projected = [jnp.dot(hidden, own, preferred_element_type=F32)]
    for copy in weights:
        copy.wait()
    projected.append(jnp.dot(hidden, w_ref[...], preferred_element_type=F32))
    for mixed, target in zip(projected, (core_ref[0], 1 - core_ref[0])):
        turned = mixed[:, :normed]
        power = jnp.square(turned)
        high = power.astype(BF16)
        low = (power - high.astype(F32)).astype(BF16)
        power = jnp.dot(high, heads, preferred_element_type=F32) + jnp.dot(low, heads, preferred_element_type=F32)
        turned = turned * lax.rsqrt(power * (1.0 / HD) + EPS) * gain
        packed = jnp.concatenate([turned, mixed[:, normed:]], axis=1).astype(BF16)
        send = jnp.dot(place, packed, preferred_element_type=F32)
        send = jnp.concatenate([send[:, :inner], send[:, inner:normed] + mark, send[:, normed:]], axis=1)
        send_ref[target] = send.astype(BF16)


def attend_kernel(text_len, slots_ref, ctx_ref, out_ref):
    slots, inner = out_ref.shape
    block = 256
    text_pad = ctx_ref.shape[1]
    queries = slots_ref[:, 0:inner]
    keys = slots_ref[:, inner : 2 * inner].astype(F32)
    dead = keys > 0.5 * DEAD
    marks = jnp.where(dead, 1.0, 0.0).astype(BF16)
    keys = jnp.concatenate([jnp.where(dead, 0.0, keys).astype(BF16), ctx_ref[0]], axis=0)
    own_bias = dot_nt(jnp.full((8, inner), MASKED, BF16), marks)[0:1]
    text_bias = jnp.where(iota((1, text_pad), 1) < text_len, 0.0, MASKED)
    bias = jnp.concatenate([own_bias, text_bias], axis=1)
    values = jnp.concatenate([slots_ref[:, 2 * inner :], ctx_ref[1]], axis=0)
    values = jnp.concatenate([values, jnp.ones(values.shape, BF16)], axis=1)
    first = iota((1, inner), 1) < HD
    zero = jnp.zeros((), BF16)
    for row in range(0, slots, block):
        query = queries[row : row + block]
        query = jnp.concatenate([jnp.where(first, query, zero), jnp.where(first, zero, query)], axis=0)
        scores = dot_nt(query, keys) + bias
        weights = jnp.exp(scores - jnp.max(scores, axis=1, keepdims=True)).astype(BF16)
        mixed = jnp.dot(weights, values, preferred_element_type=F32)
        mixed = mixed[:, :inner] / mixed[:, inner:]
        out_ref[row : row + block, :] = jnp.where(first, mixed[:block], mixed[block:]).astype(BF16)


def output_kernel(sub_slots, core_ref, parity_ref, back_ref, slot_ref, *refs):
    core, parity = core_ref[0], parity_ref[0]
    slots, inner = back_ref.shape[1:]
    *w_refs, part_ref = refs
    parts, upper, lanes = part_ref.shape
    depth = w_refs[0].shape[1]
    width = depth // parts
    quarter = slot_ref.shape[1] // 2
    slot = slot_ref[...]
    slot = as_column(jnp.where(parity == 0, slot[:, :quarter], slot[:, quarter:]))
    shift = (sub_slots * (1 - 2 * parity)).astype(F32)
    attn = []
    for moved in (slot, slot + shift):
        place_t = one_hot(iota((quarter, slots), 1).astype(F32) == moved)
        for side in (core, 1 - core):
            attn.append(jnp.dot(place_t, back_ref[side], preferred_element_type=F32).astype(BF16))
    attn = jnp.concatenate(attn, axis=1)
    weights = jnp.concatenate([ref[...] for ref in w_refs], axis=0)
    total = jnp.dot(attn, weights, preferred_element_type=F32)
    total = jnp.concatenate([total, jnp.zeros((lanes - quarter, depth), F32)], axis=0).T
    total = jnp.concatenate([total, jnp.zeros((2 * upper - width, lanes), F32)], axis=0)
    for m in range(parts):
        above = total[m * width : m * width + upper]
        below = total[m * width + upper : m * width + 2 * upper]
        part_ref[m] = (above + pltpu.roll(below, quarter, 1)).astype(BF16)


def stage_kernel(hbm, out_ref, sem):
    copy = pltpu.make_async_copy(hbm, out_ref, sem)
    copy.start()
    copy.wait()


def finish_kernel(sums_ref, perm_ref, gates_ref, pos_ref, out_ref):
    parts, upper, lanes = sums_ref.shape
    width, rows = perm_ref.shape
    halves = []
    first = iota((1, lanes), 1) < lanes // 2
    for core in range(2):
        even, odd = [sum(sums_ref[m].astype(F32) for m in range(2 * p + core, parts, 4)) for p in range(2)]
        above = jnp.where(first, even, pltpu.roll(odd, lanes // 2, 1))
        below = jnp.where(first, pltpu.roll(even, lanes // 2, 1), odd)
        halves.append(jnp.concatenate([above, below[: width - upper]], axis=0))
    total = jnp.concatenate(halves, axis=1)
    mixed = (perm_ref[...].astype(F32) + gates_ref[...].astype(F32) * total).astype(BF16)
    deal = one_hot(pos_ref[...] == dealt(rows))
    out_ref[...] = jnp.dot(mixed, deal, preferred_element_type=F32).astype(BF16)


def call(kernel, out_shape, specs, out_specs, scratch=(), flops=0):
    return pl.pallas_call(
        kernel,
        out_shape=out_shape,
        in_specs=[PLACES[letter] for letter in specs],
        out_specs=tuple(PLACES[letter] for letter in out_specs) if len(out_specs) > 1 else PLACES[out_specs],
        scratch_shapes=list(scratch),
        compiler_params=pltpu.CompilerParams(vmem_limit_bytes=VMEM_LIMIT),
        cost_estimate=pl.CostEstimate(flops=flops, bytes_accessed=1 << 20, transcendentals=0),
    )


def body(tokens, route, tsteps, mod_table, w_qkv, qk_gain, context, w_out):
    rows, width = tokens.shape
    half = rows // 2
    requests = lax.axis_size("dp")
    parts = lax.axis_size("mp")
    chips = parts // 2
    cap = max(2, 2 * rows // requests) // 2
    slots = requests * cap
    depth, kinds, inner = w_qkv.shape
    text_len = context.shape[2]
    text_pad = -(-text_len // 128) * 128
    sibling = [(i, i ^ 1) for i in range(parts)]
    planes = [[dp * parts + 2 * z + c for c in range(2) for dp in range(requests)] for z in range(chips)]
    pairs = [
        [dp * parts + 2 * z + c for c in range(2) for dp in range(requests) for z in (even, even + 1)]
        for even in range(0, chips, 2)
    ]
    upper = -(-width // 32) * 16
    place = lax.axis_index("mp").astype(I32)
    core = lax.rem(place, 2).reshape(1)
    parity = lax.rem(lax.div(place, 2), 2).reshape(1)
    shape = jax.ShapeDtypeStruct

    req = route.reshape(1, rows)
    def in_hbm(x):
        return pltpu.with_memory_space_constraint(x, pltpu.HBM)

    def in_vmem(x):
        return pltpu.with_memory_space_constraint(x, pltpu.VMEM)

    spread, perm, pos = call(
        spread_kernel,
        (pltpu.HBM((parts, width, half), BF16), shape((width, rows), BF16), shape((1, rows), F32)),
        "aa",
        "avv",
        [
            pltpu.VMEM((width, rows), BF16),
            pltpu.VMEM((1, rows), I32),
            pltpu.VMEM((2, width, half), BF16),
            pltpu.SemaphoreType.DMA((2 + parts,)),
        ],
    )(in_hbm(tokens.T), in_hbm(req))
    spread, w_qkv, w_out = lax.optimization_barrier((spread, w_qkv, w_out))
    whole = lax.all_to_all(spread, "mp", 0, 0, tiled=True)

    w_own = [w_qkv[:, kind] for kind in range(kinds)]
    w_sib = [lax.ppermute(block, "mp", sibling) for block in w_own]
    out_sib = lax.ppermute(w_out, "mp", sibling)
    first_rows = inner * 3 // 8
    gate_table = lax.dynamic_slice_in_dim(mod_table[:, 2, :], lax.axis_index("mp") * width, width, 1)
    mod, gates, slot = call(
        functools.partial(prepare_kernel, cap),
        (pltpu.HBM((2, depth, half), BF16), shape((width, rows), BF16), shape((1, half), F32)),
        "svvvav",
        "avv",
        [
            pltpu.VMEM((2, depth, half), BF16),
            pltpu.VMEM((2, gate_table.shape[0], depth), BF16),
            pltpu.SemaphoreType.DMA((3,)),
        ],
    )(core, req, pos, tsteps.reshape(1, requests), in_hbm(mod_table.transpose(1, 0, 2)), gate_table)
    whole, w_own, w_sib, out_sib, mod, gates, slot = lax.optimization_barrier(
        (whole, w_own, w_sib, out_sib, mod, gates, slot)
    )

    send = call(
        project_kernel,
        shape((2, slots, kinds * inner), BF16),
        "svavvvaaavv",
        "v",
        [
            pltpu.VMEM((2, depth, half), BF16),
            pltpu.VMEM((depth, kinds * inner), BF16),
            pltpu.VMEM((depth, half), BF16),
            pltpu.SemaphoreType.DMA((1 + kinds,)),
        ],
        flops=4 * depth * half * kinds * inner,
    )(core, whole, in_hbm(mod), *[in_vmem(w) for w in w_own], *[in_hbm(w) for w in w_sib], qk_gain, slot)
    send, early, late, context = lax.optimization_barrier(
        (send, w_out[:first_rows], w_out[first_rows:], context)
    )
    text = jnp.pad(context[0], ((0, 0), (0, text_pad - text_len), (0, 0)))
    arrived = lax.all_to_all(
        send.reshape(2 * requests, cap, kinds * inner), ("dp", "mp"), 0, 0, axis_index_groups=planes, tiled=True
    )
    next_level = [(i, i ^ 2) for i in range(parts)]
    next_early = lax.ppermute(early, "mp", next_level)
    next_late = lax.ppermute(late, "mp", next_level)
    far_late = lax.ppermute(late, "mp", [(i, i ^ 3) for i in range(parts)])
    far_early = lax.ppermute(next_early, "mp", sibling)
    attn = call(
        functools.partial(attend_kernel, text_len),
        shape((2 * slots, inner), BF16),
        "vv",
        "v",
        flops=16 * slots * (2 * slots + text_pad) * inner,
    )(arrived.reshape(2 * slots, kinds * inner), text)
    returned = lax.all_to_all(
        attn.reshape(4 * requests, cap // 2, inner), ("dp", "mp"), 0, 0, axis_index_groups=pairs, tiled=True
    )
    _, out_sib = lax.optimization_barrier((attn, out_sib))
    out_sib = call(stage_kernel, shape((inner, depth), BF16), "a", "v", [pltpu.SemaphoreType.DMA])(in_hbm(out_sib))
    blocks = (w_out, out_sib, next_early, next_late, far_early, far_late)
    partial = call(
        functools.partial(output_kernel, cap // 2),
        shape((parts, upper, half), BF16),
        "ssvvvvvvvv",
        "v",
        flops=8 * depth * half * inner,
    )(core, parity, returned.reshape(2, slots, inner), slot, *blocks)
    sums = lax.all_to_all(partial, "mp", 0, 0, tiled=True)
    return call(finish_kernel, shape((width, rows), BF16), "vvvv", "v")(sums, perm, gates, pos).T


def solution(mesh):
    return jax.shard_map(
        body,
        mesh=mesh,
        in_specs=(
            P("dp", "mp"),
            P("dp", None),
            P(),
            P(),
            P(None, None, "mp"),
            P(),
            P("dp", None, None, "mp"),
            P("mp", None),
        ),
        out_specs=P("dp", "mp"),
        check_vma=False,
    )
```

```python
import functools

import jax
import jax.numpy as jnp
from jax import lax
from jax.experimental import pallas as pl
from jax.experimental.pallas import tpu as pltpu
from jax.sharding import PartitionSpec as P

HD = 64
EPS = 1e-06
DEAD = 1e30
MASKED = -1e30
VMEM_LIMIT = 24 * 1024 * 1024
F32, BF16, I32 = jnp.float32, jnp.bfloat16, jnp.int32


PLACES = {
    "s": pl.BlockSpec(memory_space=pltpu.SMEM),
    "v": pl.BlockSpec(memory_space=pltpu.VMEM),
    "a": pl.BlockSpec(memory_space=pl.ANY),
}


def dot_nt(a, b):
    return lax.dot_general(a, b, (((1,), (1,)), ((), ())), preferred_element_type=F32)


def dot_tn(a, b):
    return lax.dot_general(a, b, (((0,), (0,)), ((), ())), preferred_element_type=F32)


def iota(shape, axis):
    return lax.broadcasted_iota(I32, shape, axis)


def as_column(row):
    n = row.shape[1]
    return jnp.sum(jnp.where(iota((n, n), 0) == iota((n, n), 1), row, 0.0), axis=1, keepdims=True)


def one_hot(flags):
    return jnp.where(flags, 1.0, 0.0).astype(BF16)


def dealt(rows):
    half, quarter = rows // 2, rows // 4
    place = iota((rows, rows), 0)
    core = jnp.where(place >= half, 1, 0)
    place = place - half * core
    parity = jnp.where(place >= quarter, 1, 0)
    return (4 * (place - quarter * parity) + 2 * parity + core).astype(F32)


def spread_kernel(tok_hbm, req_hbm, out_hbm, perm_ref, pos_ref, tok_ref, req_ref, halves_ref, sems):
    width, rows = tok_ref.shape
    half = rows // 2
    parts = out_hbm.shape[0]
    reads = [pltpu.make_async_copy(req_hbm, req_ref, sems.at[0]), pltpu.make_async_copy(tok_hbm, tok_ref, sems.at[1])]
    for copy in reads:
        copy.start()
    reads[0].wait()
    req = req_ref[...].astype(F32)
    req_col = as_column(req)
    earlier = (req_col < req) | ((req_col == req) & (iota((rows, rows), 0) < iota((rows, rows), 1)))
    pos = jnp.sum(jnp.where(earlier, 1.0, 0.0), axis=0, keepdims=True)
    deal = one_hot(pos == dealt(rows))
    pos_ref[...] = pos
    reads[1].wait()
    perm = dot_nt(tok_ref[...], deal).astype(BF16)
    halves_ref[0] = perm[:, :half]
    halves_ref[1] = perm[:, half:]
    writes = [pltpu.make_async_copy(halves_ref.at[m % 2], out_hbm.at[m], sems.at[2 + m]) for m in range(parts)]
    for copy in writes:
        copy.start()
    perm_ref[...] = perm
    for copy in writes:
        copy.wait()


def prepare_kernel(
    cap, core_ref, req_ref, pos_ref, steps_ref, table_hbm, gate_ref,
    mod_hbm, gates_ref, slot_ref, mod_ref, table_ref, sems,
):
    read = pltpu.make_async_copy(table_hbm.at[pl.ds(0, 2)], table_ref, sems.at[2])
    read.start()
    rows = req_ref.shape[1]
    half = rows // 2
    requests = steps_ref.shape[1]
    levels = gate_ref.shape[0]
    is_first = core_ref[0] == 0
    req = req_ref[...].astype(F32)
    first = jnp.sum(jnp.where(as_column(req) < req, 1.0, 0.0), axis=0, keepdims=True)
    deal = one_hot(pos_ref[...] == dealt(rows))
    line = iota((8, rows), 0)
    both = jnp.where(line == 0, req, jnp.where(line == 1, first, 0.0)).astype(BF16)
    both = dot_nt(both, deal)
    req_s, first_s = both[0:1], both[1:2]
    index = iota((1, rows), 1)
    side = jnp.where(index >= half, 1, 0)
    index = index - half * side
    parity = jnp.where(index >= half // 2, 1, 0)
    index = (index - half // 2 * parity).astype(F32)
    start = jnp.floor((first_s - (2 * parity + side).astype(F32) + 3.0) * 0.25)
    slot = req_s * cap + (parity * (cap // 2)).astype(F32) + index - start
    slot_ref[...] = jnp.where(is_first, slot[:, :half], slot[:, half:])
    chosen = one_hot(iota((requests, rows), 0).astype(F32) == req_s)
    steps = jnp.broadcast_to(steps_ref[...].astype(F32), (8, requests)).astype(BF16)
    step = jnp.dot(steps, chosen, preferred_element_type=F32)[0:1]
    pick = one_hot(iota((levels, rows), 0).astype(F32) == step)
    gates_ref[...] = dot_tn(gate_ref[...], pick).astype(BF16)
    pick = jnp.where(is_first, pick[:, :half].astype(F32), pick[:, half:].astype(F32)).astype(BF16)
    read.wait()
    writes = []
    for part in range(2):
        mod_ref[part] = dot_tn(table_ref[part], pick).astype(BF16)
        writes.append(pltpu.make_async_copy(mod_ref.at[part], mod_hbm.at[part], sems.at[part]))
        writes[-1].start()
    for copy in writes:
        copy.wait()


def project_kernel(
    core_ref, tok_ref, mod_hbm, own0_ref, own1_ref, own2_ref, sib0_hbm, sib1_hbm, sib2_hbm, gain_ref, slot_ref,
    send_ref, mod_ref, w_ref, hid_ref, sems,
):
    parts, width, rows = tok_ref.shape
    depth = parts * width
    inner = own0_ref.shape[1]
    modulation = pltpu.make_async_copy(mod_hbm, mod_ref, sems.at[0])
    modulation.start()
    weights = [
        pltpu.make_async_copy(source, w_ref.at[:, pl.ds(i * inner, inner)], sems.at[1 + i])
        for i, source in enumerate((sib0_hbm, sib1_hbm, sib2_hbm))
    ]
    for copy in weights:
        copy.start()
    hits = iota((send_ref.shape[1], rows), 0).astype(F32) == slot_ref[...]
    filled = jnp.sum(jnp.where(hits, 1.0, 0.0), axis=1, keepdims=True)
    mark = jnp.where(filled > 0.5, 0.0, DEAD)
    place = one_hot(hits)
    total = sum(jnp.sum(tok_ref[m].astype(F32), axis=0, keepdims=True) for m in range(parts))
    mean = total * (1.0 / depth)
    square = sum(jnp.sum(jnp.square(tok_ref[m].astype(F32) - mean), axis=0, keepdims=True) for m in range(parts))
    inverse = lax.rsqrt(square * (1.0 / depth) + EPS)
    modulation.wait()
    for m in range(0, parts, 2):
        pair = jnp.concatenate([tok_ref[m].astype(F32), tok_ref[m + 1].astype(F32)], axis=0)
        lines = pl.ds(m * width, 2 * width)
        shift, scale = mod_ref[0, lines, :].astype(F32), mod_ref[1, lines, :].astype(F32)
        hid_ref[lines, :] = ((pair - mean) * inverse * (1.0 + scale) + shift).astype(BF16)
    hidden = hid_ref[...].astype(F32).T.astype(BF16)
    normed = 2 * inner
    heads = one_hot(iota((normed, normed), 0) // HD == iota((normed, normed), 1) // HD)
    gain = [gain_ref[0:1, :] * HD ** (-0.5)] * (inner // HD) + [gain_ref[1:2, :]] * (inner // HD)
    gain = jnp.concatenate(gain, axis=1)
    own = jnp.concatenate([own0_ref[...], own1_ref[...], own2_ref[...]], axis=1)
    projected = [jnp.dot(hidden, own, preferred_element_type=F32)]
    for copy in weights:
        copy.wait()
    projected.append(jnp.dot(hidden, w_ref[...], preferred_element_type=F32))
    for mixed, target in zip(projected, (core_ref[0], 1 - core_ref[0])):
        turned = mixed[:, :normed]
        power = jnp.square(turned)
        high = power.astype(BF16)
        low = (power - high.astype(F32)).astype(BF16)
        power = jnp.dot(high, heads, preferred_element_type=F32) + jnp.dot(low, heads, preferred_element_type=F32)
        turned = turned * lax.rsqrt(power * (1.0 / HD) + EPS) * gain
        packed = jnp.concatenate([turned, mixed[:, normed:]], axis=1).astype(BF16)
        send = jnp.dot(place, packed, preferred_element_type=F32)
        send = jnp.concatenate([send[:, :inner], send[:, inner:normed] + mark, send[:, normed:]], axis=1)
        send_ref[target] = send.astype(BF16)


def attend_kernel(text_len, slots_ref, ctx_ref, out_ref):
    slots, inner = out_ref.shape
    block = 256
    text_pad = ctx_ref.shape[1]
    queries = slots_ref[:, 0:inner]
    keys = slots_ref[:, inner : 2 * inner].astype(F32)
    dead = keys > 0.5 * DEAD
    marks = jnp.where(dead, 1.0, 0.0).astype(BF16)
    keys = jnp.concatenate([jnp.where(dead, 0.0, keys).astype(BF16), ctx_ref[0]], axis=0)
    own_bias = dot_nt(jnp.full((8, inner), MASKED, BF16), marks)[0:1]
    text_bias = jnp.where(iota((1, text_pad), 1) < text_len, 0.0, MASKED)
    bias = jnp.concatenate([own_bias, text_bias], axis=1)
    values = jnp.concatenate([slots_ref[:, 2 * inner :], ctx_ref[1]], axis=0)
    values = jnp.concatenate([values, jnp.ones(values.shape, BF16)], axis=1)
    first = iota((1, inner), 1) < HD
    zero = jnp.zeros((), BF16)
    for row in range(0, slots, block):
        query = queries[row : row + block]
        query = jnp.concatenate([jnp.where(first, query, zero), jnp.where(first, zero, query)], axis=0)
        scores = dot_nt(query, keys) + bias
        weights = jnp.exp(scores - jnp.max(scores, axis=1, keepdims=True)).astype(BF16)
        mixed = jnp.dot(weights, values, preferred_element_type=F32)
        mixed = mixed[:, :inner] / mixed[:, inner:]
        out_ref[row : row + block, :] = jnp.where(first, mixed[:block], mixed[block:]).astype(BF16)


def output_kernel(sub_slots, core_ref, parity_ref, back_ref, slot_ref, *refs):
    core, parity = core_ref[0], parity_ref[0]
    slots, inner = back_ref.shape[1:]
    *w_refs, part_ref = refs
    parts, upper, lanes = part_ref.shape
    depth = w_refs[0].shape[1]
    width = depth // parts
    quarter = slot_ref.shape[1] // 2
    slot = slot_ref[...]
    slot = as_column(jnp.where(parity == 0, slot[:, :quarter], slot[:, quarter:]))
    shift = (sub_slots * (1 - 2 * parity)).astype(F32)
    attn = []
    for moved in (slot, slot + shift):
        place_t = one_hot(iota((quarter, slots), 1).astype(F32) == moved)
        for side in (core, 1 - core):
            attn.append(jnp.dot(place_t, back_ref[side], preferred_element_type=F32).astype(BF16))
    attn = jnp.concatenate(attn, axis=1)
    weights = jnp.concatenate([ref[...] for ref in w_refs], axis=0)
    total = jnp.dot(attn, weights, preferred_element_type=F32)
    total = jnp.concatenate([total, jnp.zeros((lanes - quarter, depth), F32)], axis=0).T
    total = jnp.concatenate([total, jnp.zeros((2 * upper - width, lanes), F32)], axis=0)
    for m in range(parts):
        above = total[m * width : m * width + upper]
        below = total[m * width + upper : m * width + 2 * upper]
        part_ref[m] = (above + pltpu.roll(below, quarter, 1)).astype(BF16)


def stage_kernel(hbm, out_ref, sem):
    copy = pltpu.make_async_copy(hbm, out_ref, sem)
    copy.start()
    copy.wait()


def finish_kernel(sums_ref, perm_ref, gates_ref, pos_ref, out_ref):
    parts, upper, lanes = sums_ref.shape
    width, rows = perm_ref.shape
    halves = []
    first = iota((1, lanes), 1) < lanes // 2
    for core in range(2):
        even, odd = [sum(sums_ref[m].astype(F32) for m in range(2 * p + core, parts, 4)) for p in range(2)]
        above = jnp.where(first, even, pltpu.roll(odd, lanes // 2, 1))
        below = jnp.where(first, pltpu.roll(even, lanes // 2, 1), odd)
        halves.append(jnp.concatenate([above, below[: width - upper]], axis=0))
    total = jnp.concatenate(halves, axis=1)
    mixed = (perm_ref[...].astype(F32) + gates_ref[...].astype(F32) * total).astype(BF16)
    deal = one_hot(pos_ref[...] == dealt(rows))
    out_ref[...] = jnp.dot(mixed, deal, preferred_element_type=F32).astype(BF16)


def call(kernel, out_shape, specs, out_specs, scratch=(), flops=0):
    return pl.pallas_call(
        kernel,
        out_shape=out_shape,
        in_specs=[PLACES[letter] for letter in specs],
        out_specs=tuple(PLACES[letter] for letter in out_specs) if len(out_specs) > 1 else PLACES[out_specs],
        scratch_shapes=list(scratch),
        compiler_params=pltpu.CompilerParams(vmem_limit_bytes=VMEM_LIMIT),
        cost_estimate=pl.CostEstimate(flops=flops, bytes_accessed=1 << 20, transcendentals=0),
    )


def body(tokens, route, tsteps, mod_table, w_qkv, qk_gain, context, w_out):
    rows, width = tokens.shape
    half = rows // 2
    requests = lax.axis_size("dp")
    parts = lax.axis_size("mp")
    chips = parts // 2
    cap = max(2, 2 * rows // requests) // 2
    slots = requests * cap
    depth, kinds, inner = w_qkv.shape
    text_len = context.shape[2]
    text_pad = -(-text_len // 128) * 128
    sibling = [(i, i ^ 1) for i in range(parts)]
    planes = [[dp * parts + 2 * z + c for c in range(2) for dp in range(requests)] for z in range(chips)]
    pairs = [
        [dp * parts + 2 * z + c for c in range(2) for dp in range(requests) for z in (even, even + 1)]
        for even in range(0, chips, 2)
    ]
    upper = -(-width // 32) * 16
    place = lax.axis_index("mp").astype(I32)
    core = lax.rem(place, 2).reshape(1)
    parity = lax.rem(lax.div(place, 2), 2).reshape(1)
    shape = jax.ShapeDtypeStruct

    req = route.reshape(1, rows)
    def in_hbm(x):
        return pltpu.with_memory_space_constraint(x, pltpu.HBM)

    def in_vmem(x):
        return pltpu.with_memory_space_constraint(x, pltpu.VMEM)

    spread, perm, pos = call(
        spread_kernel,
        (pltpu.HBM((parts, width, half), BF16), shape((width, rows), BF16), shape((1, rows), F32)),
        "aa",
        "avv",
        [
            pltpu.VMEM((width, rows), BF16),
            pltpu.VMEM((1, rows), I32),
            pltpu.VMEM((2, width, half), BF16),
            pltpu.SemaphoreType.DMA((2 + parts,)),
        ],
    )(in_hbm(tokens.T), in_hbm(req))
    spread, w_qkv, w_out = lax.optimization_barrier((spread, w_qkv, w_out))
    whole = lax.all_to_all(spread, "mp", 0, 0, tiled=True)

    w_own = [w_qkv[:, kind] for kind in range(kinds)]
    w_sib = [lax.ppermute(block, "mp", sibling) for block in w_own]
    out_sib = lax.ppermute(w_out, "mp", sibling)
    first_rows = inner * 3 // 8
    gate_table = lax.dynamic_slice_in_dim(mod_table[:, 2, :], lax.axis_index("mp") * width, width, 1)
    mod, gates, slot = call(
        functools.partial(prepare_kernel, cap),
        (pltpu.HBM((2, depth, half), BF16), shape((width, rows), BF16), shape((1, half), F32)),
        "svvvav",
        "avv",
        [
            pltpu.VMEM((2, depth, half), BF16),
            pltpu.VMEM((2, gate_table.shape[0], depth), BF16),
            pltpu.SemaphoreType.DMA((3,)),
        ],
    )(core, req, pos, tsteps.reshape(1, requests), in_hbm(mod_table.transpose(1, 0, 2)), gate_table)
    whole, w_own, w_sib, out_sib, mod, gates, slot = lax.optimization_barrier(
        (whole, w_own, w_sib, out_sib, mod, gates, slot)
    )

    send = call(
        project_kernel,
        shape((2, slots, kinds * inner), BF16),
        "svavvvaaavv",
        "v",
        [
            pltpu.VMEM((2, depth, half), BF16),
            pltpu.VMEM((depth, kinds * inner), BF16),
            pltpu.VMEM((depth, half), BF16),
            pltpu.SemaphoreType.DMA((1 + kinds,)),
        ],
        flops=4 * depth * half * kinds * inner,
    )(core, whole, in_hbm(mod), *[in_vmem(w) for w in w_own], *[in_hbm(w) for w in w_sib], qk_gain, slot)
    send, late, w_out, context = lax.optimization_barrier((send, w_out[first_rows:], w_out, context))
    text = jnp.pad(context[0], ((0, 0), (0, text_pad - text_len), (0, 0)))
    arrived = lax.all_to_all(
        send.reshape(2 * requests, cap, kinds * inner), ("dp", "mp"), 0, 0, axis_index_groups=planes, tiled=True
    )
    next_level = [(i, i ^ 2) for i in range(parts)]
    out_next = lax.ppermute(w_out, "mp", next_level)
    far_late = lax.ppermute(late, "mp", [(i, i ^ 3) for i in range(parts)])
    far_early = lax.ppermute(out_next[:first_rows], "mp", sibling)
    attn = call(
        functools.partial(attend_kernel, text_len),
        shape((2 * slots, inner), BF16),
        "vv",
        "v",
        flops=16 * slots * (2 * slots + text_pad) * inner,
    )(arrived.reshape(2 * slots, kinds * inner), text)
    returned = lax.all_to_all(
        attn.reshape(4 * requests, cap // 2, inner), ("dp", "mp"), 0, 0, axis_index_groups=pairs, tiled=True
    )
    _, out_sib = lax.optimization_barrier((attn, out_sib))
    out_sib = call(stage_kernel, shape((inner, depth), BF16), "a", "v", [pltpu.SemaphoreType.DMA])(in_hbm(out_sib))
    blocks = (w_out, out_sib, out_next, far_early, far_late)
    partial = call(
        functools.partial(output_kernel, cap // 2),
        shape((parts, upper, half), BF16),
        "ssvvvvvvv",
        "v",
        flops=8 * depth * half * inner,
    )(core, parity, returned.reshape(2, slots, inner), slot, *blocks)
    sums = lax.all_to_all(partial, "mp", 0, 0, tiled=True)
    return call(finish_kernel, shape((width, rows), BF16), "vvvv", "v")(sums, perm, gates, pos).T


def solution(mesh):
    return jax.shard_map(
        body,
        mesh=mesh,
        in_specs=(
            P("dp", "mp"),
            P("dp", None),
            P(),
            P(),
            P(None, None, "mp"),
            P(),
            P("dp", None, None, "mp"),
            P("mp", None),
        ),
        out_specs=P("dp", "mp"),
        check_vma=False,
    )
```

```python
import functools

import jax
import jax.numpy as jnp
from jax import lax
from jax.experimental import pallas as pl
from jax.experimental.pallas import tpu as pltpu
from jax.sharding import PartitionSpec as P

HD = 64
EPS = 1e-06
DEAD = 1e30
MASKED = -1e30
VMEM_LIMIT = 24 * 1024 * 1024
F32, BF16, I32 = jnp.float32, jnp.bfloat16, jnp.int32


PLACES = {
    "s": pl.BlockSpec(memory_space=pltpu.SMEM),
    "v": pl.BlockSpec(memory_space=pltpu.VMEM),
    "a": pl.BlockSpec(memory_space=pl.ANY),
}


def dot_nt(a, b):
    return lax.dot_general(a, b, (((1,), (1,)), ((), ())), preferred_element_type=F32)


def dot_tn(a, b):
    return lax.dot_general(a, b, (((0,), (0,)), ((), ())), preferred_element_type=F32)


def iota(shape, axis):
    return lax.broadcasted_iota(I32, shape, axis)


def as_column(row):
    n = row.shape[1]
    return jnp.sum(jnp.where(iota((n, n), 0) == iota((n, n), 1), row, 0.0), axis=1, keepdims=True)


def one_hot(flags):
    return jnp.where(flags, 1.0, 0.0).astype(BF16)


def dealt(rows):
    half, quarter = rows // 2, rows // 4
    place = iota((rows, rows), 0)
    core = jnp.where(place >= half, 1, 0)
    place = place - half * core
    parity = jnp.where(place >= quarter, 1, 0)
    return (4 * (place - quarter * parity) + 2 * parity + core).astype(F32)


def spread_kernel(tok_hbm, req_hbm, out_hbm, perm_ref, pos_ref, tok_ref, req_ref, halves_ref, sems):
    width, rows = tok_ref.shape
    half = rows // 2
    parts = out_hbm.shape[0]
    reads = [pltpu.make_async_copy(req_hbm, req_ref, sems.at[0]), pltpu.make_async_copy(tok_hbm, tok_ref, sems.at[1])]
    for copy in reads:
        copy.start()
    reads[0].wait()
    req = req_ref[...].astype(F32)
    req_col = as_column(req)
    earlier = (req_col < req) | ((req_col == req) & (iota((rows, rows), 0) < iota((rows, rows), 1)))
    pos = jnp.sum(jnp.where(earlier, 1.0, 0.0), axis=0, keepdims=True)
    deal = one_hot(pos == dealt(rows))
    pos_ref[...] = pos
    reads[1].wait()
    perm = dot_nt(tok_ref[...], deal).astype(BF16)
    halves_ref[0] = perm[:, :half]
    halves_ref[1] = perm[:, half:]
    writes = [pltpu.make_async_copy(halves_ref.at[m % 2], out_hbm.at[m], sems.at[2 + m]) for m in range(parts)]
    for copy in writes:
        copy.start()
    perm_ref[...] = perm
    for copy in writes:
        copy.wait()


def prepare_kernel(
    cap, core_ref, req_ref, pos_ref, steps_ref, table_hbm, gate_ref,
    mod_hbm, gates_ref, slot_ref, mod_ref, table_ref, sems,
):
    read = pltpu.make_async_copy(table_hbm.at[pl.ds(0, 2)], table_ref, sems.at[2])
    read.start()
    rows = req_ref.shape[1]
    half = rows // 2
    requests = steps_ref.shape[1]
    levels = gate_ref.shape[0]
    is_first = core_ref[0] == 0
    req = req_ref[...].astype(F32)
    first = jnp.sum(jnp.where(as_column(req) < req, 1.0, 0.0), axis=0, keepdims=True)
    deal = one_hot(pos_ref[...] == dealt(rows))
    line = iota((8, rows), 0)
    both = jnp.where(line == 0, req, jnp.where(line == 1, first, 0.0)).astype(BF16)
    both = dot_nt(both, deal)
    req_s, first_s = both[0:1], both[1:2]
    index = iota((1, rows), 1)
    side = jnp.where(index >= half, 1, 0)
    index = index - half * side
    parity = jnp.where(index >= half // 2, 1, 0)
    index = (index - half // 2 * parity).astype(F32)
    start = jnp.floor((first_s - (2 * parity + side).astype(F32) + 3.0) * 0.25)
    slot = req_s * cap + (parity * (cap // 2)).astype(F32) + index - start
    slot_ref[...] = jnp.where(is_first, slot[:, :half], slot[:, half:])
    chosen = one_hot(iota((requests, rows), 0).astype(F32) == req_s)
    steps = jnp.broadcast_to(steps_ref[...].astype(F32), (8, requests)).astype(BF16)
    step = jnp.dot(steps, chosen, preferred_element_type=F32)[0:1]
    pick = one_hot(iota((levels, rows), 0).astype(F32) == step)
    gates_ref[...] = dot_tn(gate_ref[...], pick).astype(BF16)
    pick = jnp.where(is_first, pick[:, :half].astype(F32), pick[:, half:].astype(F32)).astype(BF16)
    read.wait()
    writes = []
    for part in range(2):
        mod_ref[part] = dot_tn(table_ref[part], pick).astype(BF16)
        writes.append(pltpu.make_async_copy(mod_ref.at[part], mod_hbm.at[part], sems.at[part]))
        writes[-1].start()
    for copy in writes:
        copy.wait()


def project_kernel(
    core_ref, tok_ref, mod_hbm, own0_ref, own1_ref, own2_ref, sib0_hbm, sib1_hbm, sib2_hbm, gain_ref, slot_ref,
    send_ref, mod_ref, w_ref, hid_ref, sems,
):
    parts, width, rows = tok_ref.shape
    depth = parts * width
    inner = own0_ref.shape[1]
    modulation = pltpu.make_async_copy(mod_hbm, mod_ref, sems.at[0])
    modulation.start()
    weights = [
        pltpu.make_async_copy(source, w_ref.at[:, pl.ds(i * inner, inner)], sems.at[1 + i])
        for i, source in enumerate((sib0_hbm, sib1_hbm, sib2_hbm))
    ]
    for copy in weights:
        copy.start()
    hits = iota((send_ref.shape[1], rows), 0).astype(F32) == slot_ref[...]
    filled = jnp.sum(jnp.where(hits, 1.0, 0.0), axis=1, keepdims=True)
    mark = jnp.where(filled > 0.5, 0.0, DEAD)
    place = one_hot(hits)
    total = sum(jnp.sum(tok_ref[m].astype(F32), axis=0, keepdims=True) for m in range(parts))
    mean = total * (1.0 / depth)
    square = sum(jnp.sum(jnp.square(tok_ref[m].astype(F32) - mean), axis=0, keepdims=True) for m in range(parts))
    inverse = lax.rsqrt(square * (1.0 / depth) + EPS)
    modulation.wait()
    for m in range(0, parts, 2):
        pair = jnp.concatenate([tok_ref[m].astype(F32), tok_ref[m + 1].astype(F32)], axis=0)
        lines = pl.ds(m * width, 2 * width)
        shift, scale = mod_ref[0, lines, :].astype(F32), mod_ref[1, lines, :].astype(F32)
        hid_ref[lines, :] = ((pair - mean) * inverse * (1.0 + scale) + shift).astype(BF16)
    hidden = hid_ref[...].astype(F32).T.astype(BF16)
    normed = 2 * inner
    heads = one_hot(iota((normed, normed), 0) // HD == iota((normed, normed), 1) // HD)
    gain = [gain_ref[0:1, :] * HD ** (-0.5)] * (inner // HD) + [gain_ref[1:2, :]] * (inner // HD)
    gain = jnp.concatenate(gain, axis=1)
    own = jnp.concatenate([own0_ref[...], own1_ref[...], own2_ref[...]], axis=1)
    projected = [jnp.dot(hidden, own, preferred_element_type=F32)]
    for copy in weights:
        copy.wait()
    projected.append(jnp.dot(hidden, w_ref[...], preferred_element_type=F32))
    for mixed, target in zip(projected, (core_ref[0], 1 - core_ref[0])):
        turned = mixed[:, :normed]
        power = jnp.square(turned)
        high = power.astype(BF16)
        low = (power - high.astype(F32)).astype(BF16)
        power = jnp.dot(high, heads, preferred_element_type=F32) + jnp.dot(low, heads, preferred_element_type=F32)
        turned = turned * lax.rsqrt(power * (1.0 / HD) + EPS) * gain
        packed = jnp.concatenate([turned, mixed[:, normed:]], axis=1).astype(BF16)
        send = jnp.dot(place, packed, preferred_element_type=F32)
        send = jnp.concatenate([send[:, :inner], send[:, inner:normed] + mark, send[:, normed:]], axis=1)
        send_ref[target] = send.astype(BF16)


def attend_kernel(text_len, slots_ref, ctx_ref, out_ref):
    slots, inner = out_ref.shape
    block = 512
    text_pad = ctx_ref.shape[1]
    queries = slots_ref[:, 0:inner]
    keys = slots_ref[:, inner : 2 * inner].astype(F32)
    dead = keys > 0.5 * DEAD
    marks = jnp.where(dead, 1.0, 0.0).astype(BF16)
    keys = jnp.concatenate([jnp.where(dead, 0.0, keys).astype(BF16), ctx_ref[0]], axis=0)
    own_bias = dot_nt(jnp.full((8, inner), MASKED, BF16), marks)[0:1]
    text_bias = jnp.where(iota((1, text_pad), 1) < text_len, 0.0, MASKED)
    bias = jnp.concatenate([own_bias, text_bias], axis=1)
    values = jnp.concatenate([slots_ref[:, 2 * inner :], ctx_ref[1]], axis=0)
    first = iota((1, inner), 1) < HD
    zero, one = jnp.zeros((), BF16), jnp.ones((), BF16)
    for row in range(0, slots, block):
        query = queries[row : row + block]
        query = jnp.concatenate([jnp.where(first, query, zero), jnp.where(first, zero, query)], axis=0)
        scores = dot_nt(query, keys) + bias
        weights = jnp.exp(scores - jnp.max(scores, axis=1, keepdims=True)).astype(BF16)
        upper = jnp.dot(weights[:block], jnp.where(first, values, one), preferred_element_type=F32)
        lower = jnp.dot(weights[block:], jnp.where(first, one, values), preferred_element_type=F32)
        sums = pltpu.roll(jnp.where(first, lower, upper), HD, 1)
        out_ref[row : row + block, :] = (jnp.where(first, upper, lower) / sums).astype(BF16)


def output_kernel(sub_slots, core_ref, parity_ref, back_ref, slot_ref, *refs):
    core, parity = core_ref[0], parity_ref[0]
    slots, inner = back_ref.shape[1:]
    *w_refs, part_ref = refs
    parts, upper, lanes = part_ref.shape
    depth = w_refs[0].shape[1]
    width = depth // parts
    quarter = slot_ref.shape[1] // 2
    slot = slot_ref[...]
    slot = as_column(jnp.where(parity == 0, slot[:, :quarter], slot[:, quarter:]))
    shift = (sub_slots * (1 - 2 * parity)).astype(F32)
    attn = []
    for moved in (slot, slot + shift):
        place_t = one_hot(iota((quarter, slots), 1).astype(F32) == moved)
        for side in (core, 1 - core):
            attn.append(jnp.dot(place_t, back_ref[side], preferred_element_type=F32).astype(BF16))
    attn = jnp.concatenate(attn, axis=1)
    weights = jnp.concatenate([ref[...] for ref in w_refs], axis=0)
    attn = jnp.concatenate([attn] * (lanes // quarter), axis=0)
    total = jnp.dot(attn, weights, preferred_element_type=F32).T
    total = jnp.concatenate([total, jnp.zeros((2 * upper - width, lanes), F32)], axis=0)
    first = iota((1, lanes), 1) < quarter
    for m in range(parts):
        above = total[m * width : m * width + upper]
        below = total[m * width + upper : m * width + 2 * upper]
        part_ref[m] = jnp.where(first, above, below).astype(BF16)


def stage_kernel(hbm, out_ref, sem):
    copy = pltpu.make_async_copy(hbm, out_ref, sem)
    copy.start()
    copy.wait()


def finish_kernel(sums_ref, perm_ref, gates_ref, pos_ref, out_ref):
    parts, upper, lanes = sums_ref.shape
    width, rows = perm_ref.shape
    halves = []
    first = iota((1, lanes), 1) < lanes // 2
    for core in range(2):
        even, odd = [sum(sums_ref[m].astype(F32) for m in range(2 * p + core, parts, 4)) for p in range(2)]
        above = jnp.where(first, even, pltpu.roll(odd, lanes // 2, 1))
        below = jnp.where(first, pltpu.roll(even, lanes // 2, 1), odd)
        halves.append(jnp.concatenate([above, below[: width - upper]], axis=0))
    total = jnp.concatenate(halves, axis=1)
    mixed = (perm_ref[...].astype(F32) + gates_ref[...].astype(F32) * total).astype(BF16)
    deal = one_hot(pos_ref[...] == dealt(rows))
    out_ref[...] = jnp.dot(mixed, deal, preferred_element_type=F32).astype(BF16)


def call(kernel, out_shape, specs, out_specs, scratch=(), flops=0):
    return pl.pallas_call(
        kernel,
        out_shape=out_shape,
        in_specs=[PLACES[letter] for letter in specs],
        out_specs=tuple(PLACES[letter] for letter in out_specs) if len(out_specs) > 1 else PLACES[out_specs],
        scratch_shapes=list(scratch),
        compiler_params=pltpu.CompilerParams(vmem_limit_bytes=VMEM_LIMIT),
        cost_estimate=pl.CostEstimate(flops=flops, bytes_accessed=1 << 20, transcendentals=0),
    )


def body(tokens, route, tsteps, mod_table, w_qkv, qk_gain, context, w_out):
    rows, width = tokens.shape
    half = rows // 2
    requests = lax.axis_size("dp")
    parts = lax.axis_size("mp")
    chips = parts // 2
    cap = max(2, 2 * rows // requests) // 2
    slots = requests * cap
    depth, kinds, inner = w_qkv.shape
    text_len = context.shape[2]
    text_pad = -(-text_len // 128) * 128
    sibling = [(i, i ^ 1) for i in range(parts)]
    planes = [[dp * parts + 2 * z + c for c in range(2) for dp in range(requests)] for z in range(chips)]
    pairs = [
        [dp * parts + 2 * z + c for c in range(2) for dp in range(requests) for z in (even, even + 1)]
        for even in range(0, chips, 2)
    ]
    upper = -(-width // 32) * 16
    place = lax.axis_index("mp").astype(I32)
    core = lax.rem(place, 2).reshape(1)
    parity = lax.rem(lax.div(place, 2), 2).reshape(1)
    shape = jax.ShapeDtypeStruct

    req = route.reshape(1, rows)
    def in_hbm(x):
        return pltpu.with_memory_space_constraint(x, pltpu.HBM)

    def in_vmem(x):
        return pltpu.with_memory_space_constraint(x, pltpu.VMEM)

    spread, perm, pos = call(
        spread_kernel,
        (pltpu.HBM((parts, width, half), BF16), shape((width, rows), BF16), shape((1, rows), F32)),
        "aa",
        "avv",
        [
            pltpu.VMEM((width, rows), BF16),
            pltpu.VMEM((1, rows), I32),
            pltpu.VMEM((2, width, half), BF16),
            pltpu.SemaphoreType.DMA((2 + parts,)),
        ],
    )(in_hbm(tokens.T), in_hbm(req))
    spread, w_qkv, w_out = lax.optimization_barrier((spread, w_qkv, w_out))
    whole = lax.all_to_all(spread, "mp", 0, 0, tiled=True)

    w_own = [w_qkv[:, kind] for kind in range(kinds)]
    w_sib = [lax.ppermute(block, "mp", sibling) for block in w_own]
    out_sib = lax.ppermute(w_out, "mp", sibling)
    first_rows = inner * 3 // 8
    gate_table = lax.dynamic_slice_in_dim(mod_table[:, 2, :], lax.axis_index("mp") * width, width, 1)
    mod, gates, slot = call(
        functools.partial(prepare_kernel, cap),
        (pltpu.HBM((2, depth, half), BF16), shape((width, rows), BF16), shape((1, half), F32)),
        "svvvav",
        "avv",
        [
            pltpu.VMEM((2, depth, half), BF16),
            pltpu.VMEM((2, gate_table.shape[0], depth), BF16),
            pltpu.SemaphoreType.DMA((3,)),
        ],
    )(core, req, pos, tsteps.reshape(1, requests), in_hbm(mod_table.transpose(1, 0, 2)), gate_table)
    whole, w_own, w_sib, out_sib, mod, gates, slot = lax.optimization_barrier(
        (whole, w_own, w_sib, out_sib, mod, gates, slot)
    )

    send = call(
        project_kernel,
        shape((2, slots, kinds * inner), BF16),
        "svavvvaaavv",
        "v",
        [
            pltpu.VMEM((2, depth, half), BF16),
            pltpu.VMEM((depth, kinds * inner), BF16),
            pltpu.VMEM((depth, half), BF16),
            pltpu.SemaphoreType.DMA((1 + kinds,)),
        ],
        flops=4 * depth * half * kinds * inner,
    )(core, whole, in_hbm(mod), *[in_vmem(w) for w in w_own], *[in_hbm(w) for w in w_sib], qk_gain, slot)
    send, late, w_out, context = lax.optimization_barrier((send, w_out[first_rows:], w_out, context))
    text = jnp.pad(context[0], ((0, 0), (0, text_pad - text_len), (0, 0)))
    arrived = lax.all_to_all(
        send.reshape(2 * requests, cap, kinds * inner), ("dp", "mp"), 0, 0, axis_index_groups=planes, tiled=True
    )
    next_level = [(i, i ^ 2) for i in range(parts)]
    out_next = lax.ppermute(w_out, "mp", next_level)
    far_late = lax.ppermute(late, "mp", [(i, i ^ 3) for i in range(parts)])
    far_early = lax.ppermute(out_next[:first_rows], "mp", sibling)
    attn = call(
        functools.partial(attend_kernel, text_len),
        shape((2 * slots, inner), BF16),
        "vv",
        "v",
        flops=16 * slots * (2 * slots + text_pad) * inner,
    )(arrived.reshape(2 * slots, kinds * inner), text)
    returned = lax.all_to_all(
        attn.reshape(4 * requests, cap // 2, inner), ("dp", "mp"), 0, 0, axis_index_groups=pairs, tiled=True
    )
    _, out_sib = lax.optimization_barrier((attn, out_sib))
    out_sib = call(stage_kernel, shape((inner, depth), BF16), "a", "v", [pltpu.SemaphoreType.DMA])(in_hbm(out_sib))
    blocks = (w_out, out_sib, out_next, far_early, far_late)
    partial = call(
        functools.partial(output_kernel, cap // 2),
        shape((parts, upper, half), BF16),
        "ssvvvvvvv",
        "v",
        flops=8 * depth * half * inner,
    )(core, parity, returned.reshape(2, slots, inner), slot, *blocks)
    sums = lax.all_to_all(partial, "mp", 0, 0, tiled=True)
    return call(finish_kernel, shape((width, rows), BF16), "vvvv", "v")(sums, perm, gates, pos).T


def solution(mesh):
    return jax.shard_map(
        body,
        mesh=mesh,
        in_specs=(
            P("dp", "mp"),
            P("dp", None),
            P(),
            P(),
            P(None, None, "mp"),
            P(),
            P("dp", None, None, "mp"),
            P("mp", None),
        ),
        out_specs=P("dp", "mp"),
        check_vma=False,
    )
```

```python
import functools

import jax
import jax.numpy as jnp
from jax import lax
from jax.experimental import pallas as pl
from jax.experimental.pallas import tpu as pltpu
from jax.sharding import PartitionSpec as P

HD = 64
EPS = 1e-06
DEAD = 1e30
MASKED = -1e30
VMEM_LIMIT = 24 * 1024 * 1024
VMEM_MOST = 60 * 1024 * 1024
F32, BF16, I32 = jnp.float32, jnp.bfloat16, jnp.int32


PLACES = {
    "s": pl.BlockSpec(memory_space=pltpu.SMEM),
    "v": pl.BlockSpec(memory_space=pltpu.VMEM),
    "a": pl.BlockSpec(memory_space=pl.ANY),
}


def dot_nt(a, b):
    return lax.dot_general(a, b, (((1,), (1,)), ((), ())), preferred_element_type=F32)


def dot_tn(a, b):
    return lax.dot_general(a, b, (((0,), (0,)), ((), ())), preferred_element_type=F32)


def iota(shape, axis):
    return lax.broadcasted_iota(I32, shape, axis)


def as_column(row):
    n = row.shape[1]
    return jnp.sum(jnp.where(iota((n, n), 0) == iota((n, n), 1), row, 0.0), axis=1, keepdims=True)


def one_hot(flags):
    return jnp.where(flags, 1.0, 0.0).astype(BF16)


def dealt(rows):
    half, quarter = rows // 2, rows // 4
    place = iota((rows, rows), 0)
    core = jnp.where(place >= half, 1, 0)
    place = place - half * core
    parity = jnp.where(place >= quarter, 1, 0)
    return (4 * (place - quarter * parity) + 2 * parity + core).astype(F32)


def spread_kernel(tok_ref, req_ref, out_ref, perm_ref, pos_ref):
    width, rows = tok_ref.shape
    half = rows // 2
    req = req_ref[...].astype(F32)
    req_col = as_column(req)
    earlier = (req_col < req) | ((req_col == req) & (iota((rows, rows), 0) < iota((rows, rows), 1)))
    pos = jnp.sum(jnp.where(earlier, 1.0, 0.0), axis=0, keepdims=True)
    pos_ref[...] = pos
    perm = dot_nt(tok_ref[...], one_hot(pos == dealt(rows))).astype(BF16)
    perm_ref[...] = perm
    for m in range(out_ref.shape[0]):
        out_ref[m] = perm[:, (m % 2) * half : (m % 2 + 1) * half]


def prepare_kernel(
    cap, core_ref, req_ref, pos_ref, steps_ref, table_ref, gate_ref, mod_hbm, gates_ref, slot_ref, mod_ref, sems
):
    rows = req_ref.shape[1]
    half = rows // 2
    requests = steps_ref.shape[1]
    levels = gate_ref.shape[0]
    is_first = core_ref[0] == 0
    req = req_ref[...].astype(F32)
    first = jnp.sum(jnp.where(as_column(req) < req, 1.0, 0.0), axis=0, keepdims=True)
    deal = one_hot(pos_ref[...] == dealt(rows))
    line = iota((8, rows), 0)
    both = jnp.where(line == 0, req, jnp.where(line == 1, first, 0.0)).astype(BF16)
    both = dot_nt(both, deal)
    req_s, first_s = both[0:1], both[1:2]
    index = iota((1, rows), 1)
    side = jnp.where(index >= half, 1, 0)
    index = index - half * side
    parity = jnp.where(index >= half // 2, 1, 0)
    index = (index - half // 2 * parity).astype(F32)
    start = jnp.floor((first_s - (2 * parity + side).astype(F32) + 3.0) * 0.25)
    slot = req_s * cap + (parity * (cap // 2)).astype(F32) + index - start
    slot_ref[...] = jnp.where(is_first, slot[:, :half], slot[:, half:])
    chosen = one_hot(iota((requests, rows), 0).astype(F32) == req_s)
    steps = jnp.broadcast_to(steps_ref[...].astype(F32), (8, requests)).astype(BF16)
    step = jnp.dot(steps, chosen, preferred_element_type=F32)[0:1]
    pick = one_hot(iota((levels, rows), 0).astype(F32) == step)
    gates_ref[...] = dot_tn(gate_ref[...], pick).astype(BF16)
    pick = jnp.where(is_first, pick[:, :half].astype(F32), pick[:, half:].astype(F32)).astype(BF16)
    writes = []
    for part in range(2):
        mod_ref[part] = dot_tn(table_ref[part], pick).astype(BF16)
        writes.append(pltpu.make_async_copy(mod_ref.at[part], mod_hbm.at[part], sems.at[part]))
        writes[-1].start()
    for copy in writes:
        copy.wait()


def project_kernel(
    core_ref, tok_ref, mod_hbm, own0_ref, own1_ref, own2_ref, sib0_hbm, sib1_hbm, sib2_hbm, gain_ref, slot_ref,
    send_ref, mod_ref, w_ref, hid_ref, sems,
):
    parts, width, rows = tok_ref.shape
    depth = parts * width
    inner = own0_ref.shape[1]
    modulation = pltpu.make_async_copy(mod_hbm, mod_ref, sems.at[0])
    modulation.start()
    weights = [
        pltpu.make_async_copy(source, w_ref.at[:, pl.ds(i * inner, inner)], sems.at[1 + i])
        for i, source in enumerate((sib0_hbm, sib1_hbm, sib2_hbm))
    ]
    for copy in weights:
        copy.start()
    hits = iota((send_ref.shape[1], rows), 0).astype(F32) == slot_ref[...]
    filled = jnp.sum(jnp.where(hits, 1.0, 0.0), axis=1, keepdims=True)
    mark = jnp.where(filled > 0.5, 0.0, DEAD)
    place = one_hot(hits)
    total = sum(jnp.sum(tok_ref[m].astype(F32), axis=0, keepdims=True) for m in range(parts))
    mean = total * (1.0 / depth)
    square = sum(jnp.sum(jnp.square(tok_ref[m].astype(F32) - mean), axis=0, keepdims=True) for m in range(parts))
    inverse = lax.rsqrt(square * (1.0 / depth) + EPS)
    modulation.wait()
    for m in range(0, parts, 2):
        pair = jnp.concatenate([tok_ref[m].astype(F32), tok_ref[m + 1].astype(F32)], axis=0)
        lines = pl.ds(m * width, 2 * width)
        shift, scale = mod_ref[0, lines, :].astype(F32), mod_ref[1, lines, :].astype(F32)
        hid_ref[lines, :] = ((pair - mean) * inverse * (1.0 + scale) + shift).astype(BF16)
    hidden = hid_ref[...].astype(F32).T.astype(BF16)
    normed = 2 * inner
    heads = one_hot(iota((normed, normed), 0) // HD == iota((normed, normed), 1) // HD)
    gain = [gain_ref[0:1, :] * HD ** (-0.5)] * (inner // HD) + [gain_ref[1:2, :]] * (inner // HD)
    gain = jnp.concatenate(gain, axis=1)
    own = jnp.concatenate([own0_ref[...], own1_ref[...], own2_ref[...]], axis=1)
    projected = [jnp.dot(hidden, own, preferred_element_type=F32)]
    for copy in weights:
        copy.wait()
    projected.append(jnp.dot(hidden, w_ref[...], preferred_element_type=F32))
    for mixed, target in zip(projected, (core_ref[0], 1 - core_ref[0])):
        turned = mixed[:, :normed]
        power = jnp.square(turned)
        high = power.astype(BF16)
        low = (power - high.astype(F32)).astype(BF16)
        power = jnp.dot(high, heads, preferred_element_type=F32) + jnp.dot(low, heads, preferred_element_type=F32)
        turned = turned * lax.rsqrt(power * (1.0 / HD) + EPS) * gain
        packed = jnp.concatenate([turned, mixed[:, normed:]], axis=1).astype(BF16)
        send = jnp.dot(place, packed, preferred_element_type=F32)
        send = jnp.concatenate([send[:, :inner], send[:, inner:normed] + mark, send[:, normed:]], axis=1)
        send_ref[target] = send.astype(BF16)


def attend_kernel(text_len, slots_ref, ctx_ref, out_ref):
    slots, inner = out_ref.shape
    block = 512
    text_pad = ctx_ref.shape[1]
    queries = slots_ref[:, 0:inner]
    keys = slots_ref[:, inner : 2 * inner].astype(F32)
    dead = keys > 0.5 * DEAD
    marks = jnp.where(dead, 1.0, 0.0).astype(BF16)
    keys = jnp.concatenate([jnp.where(dead, 0.0, keys).astype(BF16), ctx_ref[0]], axis=0)
    own_bias = dot_nt(jnp.full((8, inner), MASKED, BF16), marks)[0:1]
    text_bias = jnp.where(iota((1, text_pad), 1) < text_len, 0.0, MASKED)
    bias = jnp.concatenate([own_bias, text_bias], axis=1)
    values = jnp.concatenate([slots_ref[:, 2 * inner :], ctx_ref[1]], axis=0)
    first = iota((1, inner), 1) < HD
    zero, one = jnp.zeros((), BF16), jnp.ones((), BF16)
    for row in range(0, slots, block):
        query = queries[row : row + block]
        query = jnp.concatenate([jnp.where(first, query, zero), jnp.where(first, zero, query)], axis=0)
        scores = dot_nt(query, keys) + bias
        weights = jnp.exp(scores - jnp.max(scores, axis=1, keepdims=True)).astype(BF16)
        upper = jnp.dot(weights[:block], jnp.where(first, values, one), preferred_element_type=F32)
        lower = jnp.dot(weights[block:], jnp.where(first, one, values), preferred_element_type=F32)
        sums = pltpu.roll(jnp.where(first, lower, upper), HD, 1)
        out_ref[row : row + block, :] = (jnp.where(first, upper, lower) / sums).astype(BF16)


def output_kernel(sub_slots, core_ref, parity_ref, back_ref, slot_ref, *refs):
    core, parity = core_ref[0], parity_ref[0]
    slots, inner = back_ref.shape[1:]
    *w_refs, part_ref = refs
    parts, upper, lanes = part_ref.shape
    depth = w_refs[0].shape[1]
    width = depth // parts
    quarter = slot_ref.shape[1] // 2
    slot = slot_ref[...]
    slot = as_column(jnp.where(parity == 0, slot[:, :quarter], slot[:, quarter:]))
    shift = (sub_slots * (1 - 2 * parity)).astype(F32)
    attn = []
    for moved in (slot, slot + shift):
        place_t = one_hot(iota((quarter, slots), 1).astype(F32) == moved)
        for side in (core, 1 - core):
            attn.append(jnp.dot(place_t, back_ref[side], preferred_element_type=F32).astype(BF16))
    attn = jnp.concatenate(attn, axis=1)
    weights = jnp.concatenate([ref[...] for ref in w_refs], axis=0)
    attn = jnp.concatenate([attn] * (lanes // quarter), axis=0)
    total = jnp.dot(attn, weights, preferred_element_type=F32).T
    total = jnp.concatenate([total, jnp.zeros((2 * upper - width, lanes), F32)], axis=0)
    first = iota((1, lanes), 1) < quarter
    for m in range(parts):
        above = total[m * width : m * width + upper]
        below = total[m * width + upper : m * width + 2 * upper]
        part_ref[m] = jnp.where(first, above, below).astype(BF16)


def stage_kernel(hbm, out_ref, sem):
    copy = pltpu.make_async_copy(hbm, out_ref, sem)
    copy.start()
    copy.wait()


def finish_kernel(sums_ref, perm_ref, gates_ref, pos_ref, out_ref):
    parts, upper, lanes = sums_ref.shape
    width, rows = perm_ref.shape
    halves = []
    first = iota((1, lanes), 1) < lanes // 2
    for core in range(2):
        even, odd = [sum(sums_ref[m].astype(F32) for m in range(2 * p + core, parts, 4)) for p in range(2)]
        above = jnp.where(first, even, pltpu.roll(odd, lanes // 2, 1))
        below = jnp.where(first, pltpu.roll(even, lanes // 2, 1), odd)
        halves.append(jnp.concatenate([above, below[: width - upper]], axis=0))
    total = jnp.concatenate(halves, axis=1)
    mixed = (perm_ref[...].astype(F32) + gates_ref[...].astype(F32) * total).astype(BF16)
    deal = one_hot(pos_ref[...] == dealt(rows))
    out_ref[...] = jnp.dot(mixed, deal, preferred_element_type=F32).astype(BF16)


def call(kernel, out_shape, specs, out_specs, scratch=(), flops=0, limit=VMEM_LIMIT):
    return pl.pallas_call(
        kernel,
        out_shape=out_shape,
        in_specs=[PLACES[letter] for letter in specs],
        out_specs=tuple(PLACES[letter] for letter in out_specs) if len(out_specs) > 1 else PLACES[out_specs],
        scratch_shapes=list(scratch),
        compiler_params=pltpu.CompilerParams(vmem_limit_bytes=limit),
        cost_estimate=pl.CostEstimate(flops=flops, bytes_accessed=1 << 20, transcendentals=0),
    )


def body(tokens, route, tsteps, mod_table, w_qkv, qk_gain, context, w_out):
    rows, width = tokens.shape
    half = rows // 2
    requests = lax.axis_size("dp")
    parts = lax.axis_size("mp")
    chips = parts // 2
    cap = max(2, 2 * rows // requests) // 2
    slots = requests * cap
    depth, kinds, inner = w_qkv.shape
    text_len = context.shape[2]
    text_pad = -(-text_len // 128) * 128
    sibling = [(i, i ^ 1) for i in range(parts)]
    planes = [[dp * parts + 2 * z + c for c in range(2) for dp in range(requests)] for z in range(chips)]
    pairs = [
        [dp * parts + 2 * z + c for c in range(2) for dp in range(requests) for z in (even, even + 1)]
        for even in range(0, chips, 2)
    ]
    upper = -(-width // 32) * 16
    place = lax.axis_index("mp").astype(I32)
    core = lax.rem(place, 2).reshape(1)
    parity = lax.rem(lax.div(place, 2), 2).reshape(1)
    shape = jax.ShapeDtypeStruct

    req = route.reshape(1, rows)
    def in_hbm(x):
        return pltpu.with_memory_space_constraint(x, pltpu.HBM)

    def in_vmem(x):
        return pltpu.with_memory_space_constraint(x, pltpu.VMEM)

    spread, perm, pos = call(
        spread_kernel,
        (shape((parts, width, half), BF16), shape((width, rows), BF16), shape((1, rows), F32)),
        "vv",
        "vvv",
        limit=VMEM_MOST,
    )(tokens.T, req)
    spread, w_qkv, w_out = lax.optimization_barrier((spread, w_qkv, w_out))
    whole = lax.all_to_all(spread, "mp", 0, 0, tiled=True)

    w_own = [w_qkv[:, kind] for kind in range(kinds)]
    w_sib = [lax.ppermute(block, "mp", sibling) for block in w_own]
    out_sib = lax.ppermute(w_out, "mp", sibling)
    first_rows = inner * 3 // 8
    gate_table = lax.dynamic_slice_in_dim(mod_table[:, 2, :], lax.axis_index("mp") * width, width, 1)
    mod, gates, slot = call(
        functools.partial(prepare_kernel, cap),
        (pltpu.HBM((2, depth, half), BF16), shape((width, rows), BF16), shape((1, half), F32)),
        "svvvvv",
        "avv",
        [pltpu.VMEM((2, depth, half), BF16), pltpu.SemaphoreType.DMA((2,))],
    )(core, req, pos, tsteps.reshape(1, requests), mod_table.transpose(1, 0, 2), gate_table)
    whole, w_own, w_sib, out_sib, mod, gates, slot = lax.optimization_barrier(
        (whole, w_own, w_sib, out_sib, mod, gates, slot)
    )

    send = call(
        project_kernel,
        shape((2, slots, kinds * inner), BF16),
        "svavvvaaavv",
        "v",
        [
            pltpu.VMEM((2, depth, half), BF16),
            pltpu.VMEM((depth, kinds * inner), BF16),
            pltpu.VMEM((depth, half), BF16),
            pltpu.SemaphoreType.DMA((1 + kinds,)),
        ],
        flops=4 * depth * half * kinds * inner,
    )(core, whole, in_hbm(mod), *[in_vmem(w) for w in w_own], *[in_hbm(w) for w in w_sib], qk_gain, slot)
    send, late, w_out, context = lax.optimization_barrier((send, w_out[first_rows:], w_out, context))
    text = jnp.pad(context[0], ((0, 0), (0, text_pad - text_len), (0, 0)))
    arrived = lax.all_to_all(
        send.reshape(2 * requests, cap, kinds * inner), ("dp", "mp"), 0, 0, axis_index_groups=planes, tiled=True
    )
    next_level = [(i, i ^ 2) for i in range(parts)]
    out_next = lax.ppermute(w_out, "mp", next_level)
    far_late = lax.ppermute(late, "mp", [(i, i ^ 3) for i in range(parts)])
    far_early = lax.ppermute(out_next[:first_rows], "mp", sibling)
    attn = call(
        functools.partial(attend_kernel, text_len),
        shape((2 * slots, inner), BF16),
        "vv",
        "v",
        flops=16 * slots * (2 * slots + text_pad) * inner,
    )(arrived.reshape(2 * slots, kinds * inner), text)
    returned = lax.all_to_all(
        attn.reshape(4 * requests, cap // 2, inner), ("dp", "mp"), 0, 0, axis_index_groups=pairs, tiled=True
    )
    _, out_sib = lax.optimization_barrier((attn, out_sib))
    out_sib = call(stage_kernel, shape((inner, depth), BF16), "a", "v", [pltpu.SemaphoreType.DMA])(in_hbm(out_sib))
    blocks = (w_out, out_sib, out_next, far_early, far_late)
    partial = call(
        functools.partial(output_kernel, cap // 2),
        shape((parts, upper, half), BF16),
        "ssvvvvvvv",
        "v",
        flops=8 * depth * half * inner,
    )(core, parity, returned.reshape(2, slots, inner), slot, *blocks)
    sums = lax.all_to_all(partial, "mp", 0, 0, tiled=True)
    return call(finish_kernel, shape((width, rows), BF16), "vvvv", "v")(sums, perm, gates, pos).T


def solution(mesh):
    return jax.shard_map(
        body,
        mesh=mesh,
        in_specs=(
            P("dp", "mp"),
            P("dp", None),
            P(),
            P(),
            P(None, None, "mp"),
            P(),
            P("dp", None, None, "mp"),
            P("mp", None),
        ),
        out_specs=P("dp", "mp"),
        check_vma=False,
    )
```

```python
import functools

import jax
import jax.numpy as jnp
from jax import lax
from jax.experimental import pallas as pl
from jax.experimental.pallas import tpu as pltpu
from jax.sharding import PartitionSpec as P

HD = 64
EPS = 1e-06
DEAD = 1e30
MASKED = -1e30
VMEM_LIMIT = 24 * 1024 * 1024
VMEM_MOST = 60 * 1024 * 1024
F32, BF16, I32 = jnp.float32, jnp.bfloat16, jnp.int32


PLACES = {
    "s": pl.BlockSpec(memory_space=pltpu.SMEM),
    "v": pl.BlockSpec(memory_space=pltpu.VMEM),
    "a": pl.BlockSpec(memory_space=pl.ANY),
}


def dot_nt(a, b):
    return lax.dot_general(a, b, (((1,), (1,)), ((), ())), preferred_element_type=F32)


def dot_tn(a, b):
    return lax.dot_general(a, b, (((0,), (0,)), ((), ())), preferred_element_type=F32)


def iota(shape, axis):
    return lax.broadcasted_iota(I32, shape, axis)


def as_column(row):
    n = row.shape[1]
    return jnp.sum(jnp.where(iota((n, n), 0) == iota((n, n), 1), row, 0.0), axis=1, keepdims=True)


def one_hot(flags):
    return jnp.where(flags, 1.0, 0.0).astype(BF16)


def dealt(rows):
    half, quarter = rows // 2, rows // 4
    place = iota((rows, rows), 0)
    core = jnp.where(place >= half, 1, 0)
    place = place - half * core
    parity = jnp.where(place >= quarter, 1, 0)
    return (4 * (place - quarter * parity) + 2 * parity + core).astype(F32)


def spread_kernel(tok_ref, req_ref, out_ref, perm_ref, pos_ref):
    width, rows = tok_ref.shape
    half = rows // 2
    req = req_ref[...].astype(F32)
    req_col = as_column(req)
    earlier = (req_col < req) | ((req_col == req) & (iota((rows, rows), 0) < iota((rows, rows), 1)))
    pos = jnp.sum(jnp.where(earlier, 1.0, 0.0), axis=0, keepdims=True)
    pos_ref[...] = pos
    perm = dot_nt(tok_ref[...], one_hot(pos == dealt(rows))).astype(BF16)
    perm_ref[...] = perm
    for m in range(out_ref.shape[0]):
        out_ref[m] = perm[:, (m % 2) * half : (m % 2 + 1) * half]


def prepare_kernel(
    cap, core_ref, req_ref, pos_ref, steps_ref, table_ref, gate_ref, mod_hbm, gates_ref, slot_ref, mod_ref, sems
):
    rows = req_ref.shape[1]
    half = rows // 2
    requests = steps_ref.shape[1]
    levels = gate_ref.shape[0]
    is_first = core_ref[0] == 0
    req = req_ref[...].astype(F32)
    first = jnp.sum(jnp.where(as_column(req) < req, 1.0, 0.0), axis=0, keepdims=True)
    deal = one_hot(pos_ref[...] == dealt(rows))
    line = iota((8, rows), 0)
    both = jnp.where(line == 0, req, jnp.where(line == 1, first, 0.0)).astype(BF16)
    both = dot_nt(both, deal)
    req_s, first_s = both[0:1], both[1:2]
    index = iota((1, rows), 1)
    side = jnp.where(index >= half, 1, 0)
    index = index - half * side
    parity = jnp.where(index >= half // 2, 1, 0)
    index = (index - half // 2 * parity).astype(F32)
    start = jnp.floor((first_s - (2 * parity + side).astype(F32) + 3.0) * 0.25)
    slot = req_s * cap + (parity * (cap // 2)).astype(F32) + index - start
    slot_ref[...] = jnp.where(is_first, slot[:, :half], slot[:, half:])
    chosen = one_hot(iota((requests, rows), 0).astype(F32) == req_s)
    steps = jnp.broadcast_to(steps_ref[...].astype(F32), (8, requests)).astype(BF16)
    step = jnp.dot(steps, chosen, preferred_element_type=F32)[0:1]
    pick = one_hot(iota((levels, rows), 0).astype(F32) == step)
    gates_ref[...] = dot_tn(gate_ref[...], pick).astype(BF16)
    pick = jnp.where(is_first, pick[:, :half].astype(F32), pick[:, half:].astype(F32)).astype(BF16)
    writes = []
    for part in range(2):
        mod_ref[part] = dot_tn(table_ref[part], pick).astype(BF16)
        writes.append(pltpu.make_async_copy(mod_ref.at[part], mod_hbm.at[part], sems.at[part]))
        writes[-1].start()
    for copy in writes:
        copy.wait()


def project_kernel(
    core_ref, tok_ref, mod_hbm, own0_ref, own1_ref, own2_ref, sib0_hbm, sib1_hbm, sib2_hbm, gain_ref, slot_ref,
    send_ref, mod_ref, w_ref, hid_ref, sems,
):
    parts, width, rows = tok_ref.shape
    depth = parts * width
    inner = own0_ref.shape[1]
    chunks = [pl.ds(i * (depth // 2), depth // 2) for i in range(2)]
    modulation = [
        pltpu.make_async_copy(mod_hbm.at[:, chunk], mod_ref.at[:, chunk], sems.at[4 * i])
        for i, chunk in enumerate(chunks)
    ]
    for copy in modulation:
        copy.start()
    weights = [
        pltpu.make_async_copy(source, w_ref.at[:, pl.ds(i * inner, inner)], sems.at[1 + i])
        for i, source in enumerate((sib0_hbm, sib1_hbm, sib2_hbm))
    ]
    for copy in weights:
        copy.start()
    hits = iota((send_ref.shape[1], rows), 0).astype(F32) == slot_ref[...]
    filled = jnp.sum(jnp.where(hits, 1.0, 0.0), axis=1, keepdims=True)
    mark = jnp.where(filled > 0.5, 0.0, DEAD)
    place = one_hot(hits)
    total = sum(jnp.sum(tok_ref[m].astype(F32), axis=0, keepdims=True) for m in range(parts))
    mean = total * (1.0 / depth)
    square = sum(jnp.sum(jnp.square(tok_ref[m].astype(F32) - mean), axis=0, keepdims=True) for m in range(parts))
    inverse = lax.rsqrt(square * (1.0 / depth) + EPS)
    for m in range(0, parts, 2):
        if m % (parts // 2) == 0:
            modulation[m // (parts // 2)].wait()
        pair = jnp.concatenate([tok_ref[m].astype(F32), tok_ref[m + 1].astype(F32)], axis=0)
        lines = pl.ds(m * width, 2 * width)
        shift, scale = mod_ref[0, lines, :].astype(F32), mod_ref[1, lines, :].astype(F32)
        hid_ref[lines, :] = ((pair - mean) * inverse * (1.0 + scale) + shift).astype(BF16)
    hidden = hid_ref[...].astype(F32).T.astype(BF16)
    normed = 2 * inner
    heads = one_hot(iota((normed, normed), 0) // HD == iota((normed, normed), 1) // HD)
    gain = [gain_ref[0:1, :] * HD ** (-0.5)] * (inner // HD) + [gain_ref[1:2, :]] * (inner // HD)
    gain = jnp.concatenate(gain, axis=1)
    own = jnp.concatenate([own0_ref[...], own1_ref[...], own2_ref[...]], axis=1)
    projected = [jnp.dot(hidden, own, preferred_element_type=F32)]
    for copy in weights:
        copy.wait()
    projected.append(jnp.dot(hidden, w_ref[...], preferred_element_type=F32))
    for mixed, target in zip(projected, (core_ref[0], 1 - core_ref[0])):
        turned = mixed[:, :normed]
        power = jnp.square(turned)
        high = power.astype(BF16)
        low = (power - high.astype(F32)).astype(BF16)
        power = jnp.dot(high, heads, preferred_element_type=F32) + jnp.dot(low, heads, preferred_element_type=F32)
        turned = turned * lax.rsqrt(power * (1.0 / HD) + EPS) * gain
        packed = jnp.concatenate([turned, mixed[:, normed:]], axis=1).astype(BF16)
        send = jnp.dot(place, packed, preferred_element_type=F32)
        send = jnp.concatenate([send[:, :inner], send[:, inner:normed] + mark, send[:, normed:]], axis=1)
        send_ref[target] = send.astype(BF16)


def attend_kernel(text_len, slots_ref, ctx_ref, out_ref):
    slots, inner = out_ref.shape
    block = 512
    text_pad = ctx_ref.shape[1]
    queries = slots_ref[:, 0:inner]
    keys = slots_ref[:, inner : 2 * inner].astype(F32)
    dead = keys > 0.5 * DEAD
    marks = jnp.where(dead, 1.0, 0.0).astype(BF16)
    keys = jnp.concatenate([jnp.where(dead, 0.0, keys).astype(BF16), ctx_ref[0]], axis=0)
    own_bias = dot_nt(jnp.full((8, inner), MASKED, BF16), marks)[0:1]
    text_bias = jnp.where(iota((1, text_pad), 1) < text_len, 0.0, MASKED)
    bias = jnp.concatenate([own_bias, text_bias], axis=1)
    values = jnp.concatenate([slots_ref[:, 2 * inner :], ctx_ref[1]], axis=0)
    first = iota((1, inner), 1) < HD
    zero, one = jnp.zeros((), BF16), jnp.ones((), BF16)
    for row in range(0, slots, block):
        query = queries[row : row + block]
        query = jnp.concatenate([jnp.where(first, query, zero), jnp.where(first, zero, query)], axis=0)
        scores = dot_nt(query, keys) + bias
        weights = jnp.exp(scores - jnp.max(scores, axis=1, keepdims=True)).astype(BF16)
        upper = jnp.dot(weights[:block], jnp.where(first, values, one), preferred_element_type=F32)
        lower = jnp.dot(weights[block:], jnp.where(first, one, values), preferred_element_type=F32)
        sums = pltpu.roll(jnp.where(first, lower, upper), HD, 1)
        out_ref[row : row + block, :] = (jnp.where(first, upper, lower) / sums).astype(BF16)


def output_kernel(sub_slots, core_ref, parity_ref, back_ref, slot_ref, *refs):
    core, parity = core_ref[0], parity_ref[0]
    slots, inner = back_ref.shape[1:]
    *w_refs, part_ref = refs
    parts, upper, lanes = part_ref.shape
    depth = w_refs[0].shape[1]
    width = depth // parts
    quarter = slot_ref.shape[1] // 2
    slot = slot_ref[...]
    slot = as_column(jnp.where(parity == 0, slot[:, :quarter], slot[:, quarter:]))
    shift = (sub_slots * (1 - 2 * parity)).astype(F32)
    attn = []
    for moved in (slot, slot + shift):
        place_t = one_hot(iota((quarter, slots), 1).astype(F32) == moved)
        for side in (core, 1 - core):
            attn.append(jnp.dot(place_t, back_ref[side], preferred_element_type=F32).astype(BF16))
    attn = jnp.concatenate(attn, axis=1)
    weights = jnp.concatenate([ref[...] for ref in w_refs], axis=0)
    attn = jnp.concatenate([attn] * (lanes // quarter), axis=0)
    total = jnp.dot(attn, weights, preferred_element_type=F32).T
    total = jnp.concatenate([total, jnp.zeros((2 * upper - width, lanes), F32)], axis=0)
    first = iota((1, lanes), 1) < quarter
    for m in range(parts):
        above = total[m * width : m * width + upper]
        below = total[m * width + upper : m * width + 2 * upper]
        part_ref[m] = jnp.where(first, above, below).astype(BF16)


def stage_kernel(hbm, out_ref, sem):
    copy = pltpu.make_async_copy(hbm, out_ref, sem)
    copy.start()
    copy.wait()


def finish_kernel(sums_ref, perm_ref, gates_ref, pos_ref, out_ref):
    parts, upper, lanes = sums_ref.shape
    width, rows = perm_ref.shape
    halves = []
    first = iota((1, lanes), 1) < lanes // 2
    for core in range(2):
        even, odd = [sum(sums_ref[m].astype(F32) for m in range(2 * p + core, parts, 4)) for p in range(2)]
        above = jnp.where(first, even, pltpu.roll(odd, lanes // 2, 1))
        below = jnp.where(first, pltpu.roll(even, lanes // 2, 1), odd)
        halves.append(jnp.concatenate([above, below[: width - upper]], axis=0))
    total = jnp.concatenate(halves, axis=1)
    mixed = (perm_ref[...].astype(F32) + gates_ref[...].astype(F32) * total).astype(BF16)
    deal = one_hot(pos_ref[...] == dealt(rows))
    out_ref[...] = jnp.dot(mixed, deal, preferred_element_type=F32).astype(BF16)


def call(kernel, out_shape, specs, out_specs, scratch=(), flops=0, limit=VMEM_LIMIT):
    return pl.pallas_call(
        kernel,
        out_shape=out_shape,
        in_specs=[PLACES[letter] for letter in specs],
        out_specs=tuple(PLACES[letter] for letter in out_specs) if len(out_specs) > 1 else PLACES[out_specs],
        scratch_shapes=list(scratch),
        compiler_params=pltpu.CompilerParams(vmem_limit_bytes=limit),
        cost_estimate=pl.CostEstimate(flops=flops, bytes_accessed=1 << 20, transcendentals=0),
    )


def body(tokens, route, tsteps, mod_table, w_qkv, qk_gain, context, w_out):
    rows, width = tokens.shape
    half = rows // 2
    requests = lax.axis_size("dp")
    parts = lax.axis_size("mp")
    chips = parts // 2
    cap = max(2, 2 * rows // requests) // 2
    slots = requests * cap
    depth, kinds, inner = w_qkv.shape
    text_len = context.shape[2]
    text_pad = -(-text_len // 128) * 128
    sibling = [(i, i ^ 1) for i in range(parts)]
    planes = [[dp * parts + 2 * z + c for c in range(2) for dp in range(requests)] for z in range(chips)]
    pairs = [
        [dp * parts + 2 * z + c for c in range(2) for dp in range(requests) for z in (even, even + 1)]
        for even in range(0, chips, 2)
    ]
    upper = -(-width // 32) * 16
    place = lax.axis_index("mp").astype(I32)
    core = lax.rem(place, 2).reshape(1)
    parity = lax.rem(lax.div(place, 2), 2).reshape(1)
    shape = jax.ShapeDtypeStruct

    req = route.reshape(1, rows)
    def in_hbm(x):
        return pltpu.with_memory_space_constraint(x, pltpu.HBM)

    def in_vmem(x):
        return pltpu.with_memory_space_constraint(x, pltpu.VMEM)

    spread, perm, pos = call(
        spread_kernel,
        (shape((parts, width, half), BF16), shape((width, rows), BF16), shape((1, rows), F32)),
        "vv",
        "vvv",
        limit=VMEM_MOST,
    )(tokens.T, req)
    spread, w_qkv, w_out = lax.optimization_barrier((spread, w_qkv, w_out))
    whole = lax.all_to_all(spread, "mp", 0, 0, tiled=True)

    w_own = [w_qkv[:, kind] for kind in range(kinds)]
    w_sib = [lax.ppermute(block, "mp", sibling) for block in w_own]
    out_sib = lax.ppermute(w_out, "mp", sibling)
    first_rows = inner * 3 // 8
    gate_table = lax.dynamic_slice_in_dim(mod_table[:, 2, :], lax.axis_index("mp") * width, width, 1)
    mod, gates, slot = call(
        functools.partial(prepare_kernel, cap),
        (pltpu.HBM((2, depth, half), BF16), shape((width, rows), BF16), shape((1, half), F32)),
        "svvvvv",
        "avv",
        [pltpu.VMEM((2, depth, half), BF16), pltpu.SemaphoreType.DMA((2,))],
    )(core, req, pos, tsteps.reshape(1, requests), mod_table.transpose(1, 0, 2), gate_table)
    whole, w_own, w_sib, out_sib, mod, gates, slot = lax.optimization_barrier(
        (whole, w_own, w_sib, out_sib, mod, gates, slot)
    )

    send = call(
        project_kernel,
        shape((2, slots, kinds * inner), BF16),
        "svavvvaaavv",
        "v",
        [
            pltpu.VMEM((2, depth, half), BF16),
            pltpu.VMEM((depth, kinds * inner), BF16),
            pltpu.VMEM((depth, half), BF16),
            pltpu.SemaphoreType.DMA((2 + kinds,)),
        ],
        flops=4 * depth * half * kinds * inner,
    )(core, whole, in_hbm(mod), *[in_vmem(w) for w in w_own], *[in_hbm(w) for w in w_sib], qk_gain, slot)
    send, late, w_out, context = lax.optimization_barrier((send, w_out[first_rows:], w_out, context))
    text = jnp.pad(context[0], ((0, 0), (0, text_pad - text_len), (0, 0)))
    arrived = lax.all_to_all(
        send.reshape(2 * requests, cap, kinds * inner), ("dp", "mp"), 0, 0, axis_index_groups=planes, tiled=True
    )
    next_level = [(i, i ^ 2) for i in range(parts)]
    out_next = lax.ppermute(w_out, "mp", next_level)
    far_late = lax.ppermute(late, "mp", [(i, i ^ 3) for i in range(parts)])
    far_early = lax.ppermute(out_next[:first_rows], "mp", sibling)
    attn = call(
        functools.partial(attend_kernel, text_len),
        shape((2 * slots, inner), BF16),
        "vv",
        "v",
        flops=16 * slots * (2 * slots + text_pad) * inner,
    )(arrived.reshape(2 * slots, kinds * inner), text)
    returned = lax.all_to_all(
        attn.reshape(4 * requests, cap // 2, inner), ("dp", "mp"), 0, 0, axis_index_groups=pairs, tiled=True
    )
    _, out_sib = lax.optimization_barrier((attn, out_sib))
    out_sib = call(stage_kernel, shape((inner, depth), BF16), "a", "v", [pltpu.SemaphoreType.DMA])(in_hbm(out_sib))
    blocks = (w_out, out_sib, out_next, far_early, far_late)
    partial = call(
        functools.partial(output_kernel, cap // 2),
        shape((parts, upper, half), BF16),
        "ssvvvvvvv",
        "v",
        flops=8 * depth * half * inner,
    )(core, parity, returned.reshape(2, slots, inner), slot, *blocks)
    sums = lax.all_to_all(partial, "mp", 0, 0, tiled=True)
    return call(finish_kernel, shape((width, rows), BF16), "vvvv", "v")(sums, perm, gates, pos).T


def solution(mesh):
    return jax.shard_map(
        body,
        mesh=mesh,
        in_specs=(
            P("dp", "mp"),
            P("dp", None),
            P(),
            P(),
            P(None, None, "mp"),
            P(),
            P("dp", None, None, "mp"),
            P("mp", None),
        ),
        out_specs=P("dp", "mp"),
        check_vma=False,
    )
```

```python
import functools

import jax
import jax.numpy as jnp
from jax import lax
from jax.experimental import pallas as pl
from jax.experimental.pallas import tpu as pltpu
from jax.sharding import PartitionSpec as P

HD = 64
EPS = 1e-06
DEAD = 1e30
MASKED = -1e30
LOG2_E = 1.4426950408889634
VMEM_LIMIT = 24 * 1024 * 1024
VMEM_MOST = 60 * 1024 * 1024
F32, BF16, I32 = jnp.float32, jnp.bfloat16, jnp.int32


PLACES = {
    "s": pl.BlockSpec(memory_space=pltpu.SMEM),
    "v": pl.BlockSpec(memory_space=pltpu.VMEM),
    "a": pl.BlockSpec(memory_space=pl.ANY),
}


def dot_nt(a, b):
    return lax.dot_general(a, b, (((1,), (1,)), ((), ())), preferred_element_type=F32)


def dot_tn(a, b):
    return lax.dot_general(a, b, (((0,), (0,)), ((), ())), preferred_element_type=F32)


def iota(shape, axis):
    return lax.broadcasted_iota(I32, shape, axis)


def as_column(row):
    n = row.shape[1]
    return jnp.sum(jnp.where(iota((n, n), 0) == iota((n, n), 1), row, 0.0), axis=1, keepdims=True)


def one_hot(flags):
    return jnp.where(flags, 1.0, 0.0).astype(BF16)


def dealt(rows):
    half, quarter = rows // 2, rows // 4
    place = iota((rows, rows), 0)
    core = jnp.where(place >= half, 1, 0)
    place = place - half * core
    parity = jnp.where(place >= quarter, 1, 0)
    return (4 * (place - quarter * parity) + 2 * parity + core).astype(F32)


def spread_kernel(tok_ref, req_ref, out_ref, perm_ref, pos_ref):
    width, rows = tok_ref.shape
    half = rows // 2
    req = req_ref[...].astype(F32)
    req_col = as_column(req)
    earlier = (req_col < req) | ((req_col == req) & (iota((rows, rows), 0) < iota((rows, rows), 1)))
    pos = jnp.sum(jnp.where(earlier, 1.0, 0.0), axis=0, keepdims=True)
    pos_ref[...] = pos
    perm = dot_nt(tok_ref[...], one_hot(pos == dealt(rows))).astype(BF16)
    perm_ref[...] = perm
    for m in range(out_ref.shape[0]):
        out_ref[m] = perm[:, (m % 2) * half : (m % 2 + 1) * half]


def prepare_kernel(
    cap, core_ref, req_ref, pos_ref, steps_ref, table_ref, gate_ref, mod_hbm, gates_ref, slot_ref, mod_ref, sems
):
    rows = req_ref.shape[1]
    half = rows // 2
    requests = steps_ref.shape[1]
    levels = gate_ref.shape[0]
    is_first = core_ref[0] == 0
    req = req_ref[...].astype(F32)
    first = jnp.sum(jnp.where(as_column(req) < req, 1.0, 0.0), axis=0, keepdims=True)
    deal = one_hot(pos_ref[...] == dealt(rows))
    line = iota((8, rows), 0)
    both = jnp.where(line == 0, req, jnp.where(line == 1, first, 0.0)).astype(BF16)
    both = dot_nt(both, deal)
    req_s, first_s = both[0:1], both[1:2]
    index = iota((1, rows), 1)
    side = jnp.where(index >= half, 1, 0)
    index = index - half * side
    parity = jnp.where(index >= half // 2, 1, 0)
    index = (index - half // 2 * parity).astype(F32)
    start = jnp.floor((first_s - (2 * parity + side).astype(F32) + 3.0) * 0.25)
    slot = req_s * cap + (parity * (cap // 2)).astype(F32) + index - start
    slot_ref[...] = jnp.where(is_first, slot[:, :half], slot[:, half:])
    chosen = one_hot(iota((requests, rows), 0).astype(F32) == req_s)
    steps = jnp.broadcast_to(steps_ref[...].astype(F32), (8, requests)).astype(BF16)
    step = jnp.dot(steps, chosen, preferred_element_type=F32)[0:1]
    pick = one_hot(iota((levels, rows), 0).astype(F32) == step)
    gates_ref[...] = dot_tn(gate_ref[...], pick).astype(BF16)
    pick = jnp.where(is_first, pick[:, :half].astype(F32), pick[:, half:].astype(F32)).astype(BF16)
    writes = []
    for part in range(2):
        mod_ref[part] = dot_tn(table_ref[part], pick).astype(BF16)
        writes.append(pltpu.make_async_copy(mod_ref.at[part], mod_hbm.at[part], sems.at[part]))
        writes[-1].start()
    for copy in writes:
        copy.wait()


def project_kernel(
    core_ref, tok_ref, mod_hbm, own0_ref, own1_ref, own2_ref, sib0_hbm, sib1_hbm, sib2_hbm, gain_ref, slot_ref,
    send_ref, mod_ref, w_ref, hid_ref, sems,
):
    parts, width, rows = tok_ref.shape
    depth = parts * width
    inner = own0_ref.shape[1]
    modulation = pltpu.make_async_copy(mod_hbm, mod_ref, sems.at[0])
    modulation.start()
    weights = [
        pltpu.make_async_copy(source, w_ref.at[:, pl.ds(i * inner, inner)], sems.at[1 + i])
        for i, source in enumerate((sib0_hbm, sib1_hbm, sib2_hbm))
    ]
    for copy in weights:
        copy.start()
    hits = iota((send_ref.shape[1], rows), 0).astype(F32) == slot_ref[...]
    filled = jnp.sum(jnp.where(hits, 1.0, 0.0), axis=1, keepdims=True)
    mark = jnp.where(filled > 0.5, 0.0, DEAD)
    place = one_hot(hits)
    total = sum(jnp.sum(tok_ref[m].astype(F32), axis=0, keepdims=True) for m in range(parts))
    mean = total * (1.0 / depth)
    square = sum(jnp.sum(jnp.square(tok_ref[m].astype(F32) - mean), axis=0, keepdims=True) for m in range(parts))
    inverse = lax.rsqrt(square * (1.0 / depth) + EPS)
    modulation.wait()
    for m in range(0, parts, 2):
        pair = jnp.concatenate([tok_ref[m].astype(F32), tok_ref[m + 1].astype(F32)], axis=0)
        lines = pl.ds(m * width, 2 * width)
        shift, scale = mod_ref[0, lines, :].astype(F32), mod_ref[1, lines, :].astype(F32)
        hid_ref[lines, :] = ((pair - mean) * inverse * (1.0 + scale) + shift).astype(BF16)
    hidden = hid_ref[...].astype(F32).T.astype(BF16)
    normed = 2 * inner
    heads = one_hot(iota((normed, normed), 0) // HD == iota((normed, normed), 1) // HD)
    gain = [gain_ref[0:1, :] * (HD ** (-0.5) * LOG2_E)] * (inner // HD) + [gain_ref[1:2, :]] * (inner // HD)
    gain = jnp.concatenate(gain, axis=1)
    own = jnp.concatenate([own0_ref[...], own1_ref[...], own2_ref[...]], axis=1)
    projected = [jnp.dot(hidden, own, preferred_element_type=F32)]
    for copy in weights:
        copy.wait()
    projected.append(jnp.dot(hidden, w_ref[...], preferred_element_type=F32))
    for mixed, target in zip(projected, (core_ref[0], 1 - core_ref[0])):
        turned = mixed[:, :normed]
        power = jnp.square(turned)
        high = power.astype(BF16)
        low = (power - high.astype(F32)).astype(BF16)
        power = jnp.dot(high, heads, preferred_element_type=F32) + jnp.dot(low, heads, preferred_element_type=F32)
        turned = turned * lax.rsqrt(power * (1.0 / HD) + EPS) * gain
        packed = jnp.concatenate([turned, mixed[:, normed:]], axis=1).astype(BF16)
        send = jnp.dot(place, packed, preferred_element_type=F32)
        send = jnp.concatenate([send[:, :inner], send[:, inner:normed] + mark, send[:, normed:]], axis=1)
        send_ref[target] = send.astype(BF16)


def attend_kernel(text_len, slots_ref, ctx_ref, out_ref):
    slots, inner = out_ref.shape
    block = 512
    text_pad = ctx_ref.shape[1]
    queries = slots_ref[:, 0:inner]
    keys = slots_ref[:, inner : 2 * inner].astype(F32)
    dead = keys > 0.5 * DEAD
    marks = jnp.where(dead, 1.0, 0.0).astype(BF16)
    keys = jnp.concatenate([jnp.where(dead, 0.0, keys).astype(BF16), ctx_ref[0]], axis=0)
    own_bias = dot_nt(jnp.full((8, inner), MASKED, BF16), marks)[0:1]
    text_bias = jnp.where(iota((1, text_pad), 1) < text_len, 0.0, MASKED)
    bias = jnp.concatenate([own_bias, text_bias], axis=1)
    values = jnp.concatenate([slots_ref[:, 2 * inner :], ctx_ref[1]], axis=0)
    first = iota((1, inner), 1) < HD
    zero, one = jnp.zeros((), BF16), jnp.ones((), BF16)
    for row in range(0, slots, block):
        query = queries[row : row + block]
        query = jnp.concatenate([jnp.where(first, query, zero), jnp.where(first, zero, query)], axis=0)
        scores = dot_nt(query, keys) + bias
        weights = jnp.exp2(scores - jnp.max(scores, axis=1, keepdims=True)).astype(BF16)
        upper = jnp.dot(weights[:block], jnp.where(first, values, one), preferred_element_type=F32)
        lower = jnp.dot(weights[block:], jnp.where(first, one, values), preferred_element_type=F32)
        sums = pltpu.roll(jnp.where(first, lower, upper), HD, 1)
        out_ref[row : row + block, :] = (jnp.where(first, upper, lower) / sums).astype(BF16)


def output_kernel(sub_slots, core_ref, parity_ref, back_ref, slot_ref, *refs):
    core, parity = core_ref[0], parity_ref[0]
    slots, inner = back_ref.shape[1:]
    *w_refs, part_ref = refs
    parts, upper, lanes = part_ref.shape
    depth = w_refs[0].shape[1]
    width = depth // parts
    quarter = slot_ref.shape[1] // 2
    slot = slot_ref[...]
    slot = as_column(jnp.where(parity == 0, slot[:, :quarter], slot[:, quarter:]))
    shift = (sub_slots * (1 - 2 * parity)).astype(F32)
    attn = []
    for moved in (slot, slot + shift):
        place_t = one_hot(iota((quarter, slots), 1).astype(F32) == moved)
        for side in (core, 1 - core):
            attn.append(jnp.dot(place_t, back_ref[side], preferred_element_type=F32).astype(BF16))
    attn = jnp.concatenate(attn, axis=1)
    weights = jnp.concatenate([ref[...] for ref in w_refs], axis=0)
    attn = jnp.concatenate([attn] * (lanes // quarter), axis=0)
    total = jnp.dot(attn, weights, preferred_element_type=F32).T
    total = jnp.concatenate([total, jnp.zeros((2 * upper - width, lanes), F32)], axis=0)
    first = iota((1, lanes), 1) < quarter
    for m in range(parts):
        above = total[m * width : m * width + upper]
        below = total[m * width + upper : m * width + 2 * upper]
        part_ref[m] = jnp.where(first, above, below).astype(BF16)


def stage_kernel(hbm, out_ref, sem):
    copy = pltpu.make_async_copy(hbm, out_ref, sem)
    copy.start()
    copy.wait()


def finish_kernel(sums_ref, perm_ref, gates_ref, pos_ref, out_ref):
    parts, upper, lanes = sums_ref.shape
    width, rows = perm_ref.shape
    halves = []
    first = iota((1, lanes), 1) < lanes // 2
    for core in range(2):
        even, odd = [sum(sums_ref[m].astype(F32) for m in range(2 * p + core, parts, 4)) for p in range(2)]
        above = jnp.where(first, even, pltpu.roll(odd, lanes // 2, 1))
        below = jnp.where(first, pltpu.roll(even, lanes // 2, 1), odd)
        halves.append(jnp.concatenate([above, below[: width - upper]], axis=0))
    total = jnp.concatenate(halves, axis=1)
    mixed = (perm_ref[...].astype(F32) + gates_ref[...].astype(F32) * total).astype(BF16)
    deal = one_hot(pos_ref[...] == dealt(rows))
    out_ref[...] = jnp.dot(mixed, deal, preferred_element_type=F32).astype(BF16)


def call(kernel, out_shape, specs, out_specs, scratch=(), flops=0, limit=VMEM_LIMIT):
    return pl.pallas_call(
        kernel,
        out_shape=out_shape,
        in_specs=[PLACES[letter] for letter in specs],
        out_specs=tuple(PLACES[letter] for letter in out_specs) if len(out_specs) > 1 else PLACES[out_specs],
        scratch_shapes=list(scratch),
        compiler_params=pltpu.CompilerParams(vmem_limit_bytes=limit),
        cost_estimate=pl.CostEstimate(flops=flops, bytes_accessed=1 << 20, transcendentals=0),
    )


def body(tokens, route, tsteps, mod_table, w_qkv, qk_gain, context, w_out):
    rows, width = tokens.shape
    half = rows // 2
    requests = lax.axis_size("dp")
    parts = lax.axis_size("mp")
    chips = parts // 2
    cap = max(2, 2 * rows // requests) // 2
    slots = requests * cap
    depth, kinds, inner = w_qkv.shape
    text_len = context.shape[2]
    text_pad = -(-text_len // 128) * 128
    sibling = [(i, i ^ 1) for i in range(parts)]
    planes = [[dp * parts + 2 * z + c for c in range(2) for dp in range(requests)] for z in range(chips)]
    pairs = [
        [dp * parts + 2 * z + c for c in range(2) for dp in range(requests) for z in (even, even + 1)]
        for even in range(0, chips, 2)
    ]
    upper = -(-width // 32) * 16
    place = lax.axis_index("mp").astype(I32)
    core = lax.rem(place, 2).reshape(1)
    parity = lax.rem(lax.div(place, 2), 2).reshape(1)
    shape = jax.ShapeDtypeStruct

    req = route.reshape(1, rows)
    def in_hbm(x):
        return pltpu.with_memory_space_constraint(x, pltpu.HBM)

    def in_vmem(x):
        return pltpu.with_memory_space_constraint(x, pltpu.VMEM)

    spread, perm, pos = call(
        spread_kernel,
        (shape((parts, width, half), BF16), shape((width, rows), BF16), shape((1, rows), F32)),
        "vv",
        "vvv",
        limit=VMEM_MOST,
    )(tokens.T, req)
    spread, w_qkv, w_out = lax.optimization_barrier((spread, w_qkv, w_out))
    whole = lax.all_to_all(spread, "mp", 0, 0, tiled=True)

    w_own = [w_qkv[:, kind] for kind in range(kinds)]
    w_sib = [lax.ppermute(block, "mp", sibling) for block in w_own]
    out_sib = lax.ppermute(w_out, "mp", sibling)
    first_rows = inner * 3 // 8
    gate_table = lax.dynamic_slice_in_dim(mod_table[:, 2, :], lax.axis_index("mp") * width, width, 1)
    mod, gates, slot = call(
        functools.partial(prepare_kernel, cap),
        (pltpu.HBM((2, depth, half), BF16), shape((width, rows), BF16), shape((1, half), F32)),
        "svvvvv",
        "avv",
        [pltpu.VMEM((2, depth, half), BF16), pltpu.SemaphoreType.DMA((2,))],
    )(core, req, pos, tsteps.reshape(1, requests), mod_table.transpose(1, 0, 2), gate_table)
    whole, w_own, w_sib, out_sib, mod, gates, slot = lax.optimization_barrier(
        (whole, w_own, w_sib, out_sib, mod, gates, slot)
    )

    send = call(
        project_kernel,
        shape((2, slots, kinds * inner), BF16),
        "svavvvaaavv",
        "v",
        [
            pltpu.VMEM((2, depth, half), BF16),
            pltpu.VMEM((depth, kinds * inner), BF16),
            pltpu.VMEM((depth, half), BF16),
            pltpu.SemaphoreType.DMA((1 + kinds,)),
        ],
        flops=4 * depth * half * kinds * inner,
    )(core, whole, in_hbm(mod), *[in_vmem(w) for w in w_own], *[in_hbm(w) for w in w_sib], qk_gain, slot)
    send, late, w_out, context = lax.optimization_barrier((send, w_out[first_rows:], w_out, context))
    text = jnp.pad(context[0], ((0, 0), (0, text_pad - text_len), (0, 0)))
    arrived = lax.all_to_all(
        send.reshape(2 * requests, cap, kinds * inner), ("dp", "mp"), 0, 0, axis_index_groups=planes, tiled=True
    )
    next_level = [(i, i ^ 2) for i in range(parts)]
    out_next = lax.ppermute(w_out, "mp", next_level)
    far_late = lax.ppermute(late, "mp", [(i, i ^ 3) for i in range(parts)])
    far_early = lax.ppermute(out_next[:first_rows], "mp", sibling)
    attn = call(
        functools.partial(attend_kernel, text_len),
        shape((2 * slots, inner), BF16),
        "vv",
        "v",
        flops=16 * slots * (2 * slots + text_pad) * inner,
    )(arrived.reshape(2 * slots, kinds * inner), text)
    returned = lax.all_to_all(
        attn.reshape(4 * requests, cap // 2, inner), ("dp", "mp"), 0, 0, axis_index_groups=pairs, tiled=True
    )
    _, out_sib = lax.optimization_barrier((attn, out_sib))
    out_sib = call(stage_kernel, shape((inner, depth), BF16), "a", "v", [pltpu.SemaphoreType.DMA])(in_hbm(out_sib))
    blocks = (w_out, out_sib, out_next, far_early, far_late)
    partial = call(
        functools.partial(output_kernel, cap // 2),
        shape((parts, upper, half), BF16),
        "ssvvvvvvv",
        "v",
        flops=8 * depth * half * inner,
    )(core, parity, returned.reshape(2, slots, inner), slot, *blocks)
    sums = lax.all_to_all(partial, "mp", 0, 0, tiled=True)
    return call(finish_kernel, shape((width, rows), BF16), "vvvv", "v")(sums, perm, gates, pos).T


def solution(mesh):
    return jax.shard_map(
        body,
        mesh=mesh,
        in_specs=(
            P("dp", "mp"),
            P("dp", None),
            P(),
            P(),
            P(None, None, "mp"),
            P(),
            P("dp", None, None, "mp"),
            P("mp", None),
        ),
        out_specs=P("dp", "mp"),
        check_vma=False,
    )
```
